128 devices in a mesh: ctx: 16 (over z, y_hi, core), row: 2 (over y_lo), col: 4 (over x).
Axes of the slice: x: 4, y: 4 (y_hi: 2, y_lo: 2; y = y_hi * 2 + y_lo), z: 4, core: 2. Of those that a mesh axis runs over, the one named last changes fastest.
Arguments:
- tokens: bfloat16 [4096, 4096], P('ctx', ('row', 'col')), may hold values from -6 to 6
- w_feat: bfloat16 [4096, 3, 4096], P(None, None, ('row', 'col')), may hold values from -0.09375 to 0.09375
- short_filter: float32 [7, 3, 4096], P(None, None, ('row', 'col')), may hold values from -2 to 2
- mr_filter: float32 [128, 4096], P(None, ('row', 'col')), may hold values from -0.5 to 0.5
- queries: bfloat16 [4096, 4096], P('ctx', ('row', 'col')), may hold values from -6 to 6
- key_rows: bfloat16 [4096, 4096], P('ctx', ('row', 'col')), may hold values from -6 to 6
- cotangent: bfloat16 [4096, 4096], P('ctx', ('row', 'col')), may hold values from -6 to 6
Outputs:
- block_out: bfloat16 [4096, 4096], P('ctx', ('row', 'col'))
- grad_input: bfloat16 [4096, 4096], P('ctx', ('row', 'col'))
- grad_feat: float32 [4096, 3, 4096], P('ctx', None, ('row', 'col'))
- grad_short: float32 [7, 3, 4096], P(None, None, ('row', 'col'))
- grad_mr: float32 [128, 4096], P(None, ('row', 'col'))
- grad_queries: bfloat16 [4096, 4096], P('ctx', ('row', 'col'))
- grad_keys: bfloat16 [4096, 4096], P('ctx', ('row', 'col'))
The draws below stay inside these ranges and needn't reach their ends.
All inputs are finite; a program needn't handle non-finite values.
Results may differ from the reference program's by a relative error of at most 0.025.
Values may be sent and summed in bfloat16 or wider, within the bound.
A program may use at most 192 MiB of HBM per device.

```python
import jax
import jax.numpy as jnp
from jax import lax

DH = 128
SHORT = 7
MRLEN = 128
C = 4096
S = 4096
N_CTX = 16
N_ROW = 2
N_COL = 4


def draw_queries(key, part):
    key = jax.random.fold_in(key, 5)
    return jnp.clip(jax.random.normal(key, (S, C), jnp.float32), -6.0, 6.0).astype(jnp.bfloat16)


def draw_key_rows(key, part):
    key = jax.random.fold_in(key, 7)
    return jnp.clip(jax.random.normal(key, (S, C), jnp.float32), -6.0, 6.0).astype(jnp.bfloat16)


def steps_of(stream_key, extent, pieces, smallest, high):
    level = 1.0
    for axis_at, shards_of in pieces:
        draws = jax.random.uniform(jax.random.fold_in(jax.random.fold_in(stream_key, 6), axis_at), (shards_of,), jnp.float32, smallest / len(pieces), high / len(pieces))
        level = level * jnp.repeat(jnp.exp(draws), extent[axis_at] // shards_of).reshape((-1,) + (1,) * (len(extent) - 1 - axis_at))
    return level


def centred(key, dims, deviation, bound, shards=(), kind=jnp.bfloat16):
    values = jax.random.normal(key, dims, jnp.float32) * deviation
    if len(shards) > 0:
        values = steps_of(key, dims, shards, -0.22, 0.18) * values
    return jnp.clip(values, min=-bound, max=bound).astype(kind)


def setup_inputs(seed: int = 0) -> dict:
    keys = jax.random.split(jax.random.key(seed), 8)
    return {
        "tokens": centred(keys[0], (S, C), 1.0, 6.0, ((0, 16), (1, 8))),
        "w_feat": centred(keys[1], (C, 3, C), C ** -0.5, 0.09375, ((2, 8),)),
        "short_filter": centred(keys[2], (SHORT, 3, C), SHORT ** -0.5, 2.0, ((2, 8),), jnp.float32),
        "mr_filter": centred(keys[3], (MRLEN, C), MRLEN ** -0.5, 0.5, ((1, 8),), jnp.float32),
        "queries": draw_queries(jax.random.fold_in(keys[7], 71), 0),
        "key_rows": draw_key_rows(jax.random.fold_in(keys[7], 71), 0),
        "cotangent": centred(keys[6], (S, C), 1.0, 6.0, ((0, 16), (1, 8))),
    }


def causal_mix(padded, filter_taps):
    tap_count = filter_taps.shape[0]
    out_rows = padded.shape[0] - tap_count + 1

    def add_tap(step, total):
        index = jnp.asarray(step).astype(jnp.int32)
        start = (tap_count - 1 - index).astype(jnp.int32)
        window = lax.dynamic_slice_in_dim(padded, start, out_rows, 0)
        weight = lax.dynamic_index_in_dim(filter_taps, index, 0, keepdims=True)
        return total + weight * window

    return lax.fori_loop(0, tap_count, add_tap, jnp.zeros((out_rows, padded.shape[1]), padded.dtype))


def anti_mix(padded, filter_taps):
    tap_count = filter_taps.shape[0]
    out_rows = padded.shape[0] - tap_count + 1

    def add_tap(step, total):
        index = jnp.asarray(step).astype(jnp.int32)
        window = lax.dynamic_slice_in_dim(padded, index, out_rows, 0)
        weight = lax.dynamic_index_in_dim(filter_taps, index, 0, keepdims=True)
        return total + weight * window

    return lax.fori_loop(0, tap_count, add_tap, jnp.zeros((out_rows, padded.shape[1]), padded.dtype))


def tap_grads(grad_rows, padded, tap_count):
    grad_len = grad_rows.shape[0]

    def one_tap(step, result):
        index = jnp.asarray(step).astype(jnp.int32)
        start = (tap_count - 1 - index).astype(jnp.int32)
        window = lax.dynamic_slice_in_dim(padded, start, grad_len, 0)
        value = jnp.sum(grad_rows * window, axis=0, keepdims=True).astype(result.dtype)
        return lax.dynamic_update_slice_in_dim(result, value, index, 0)

    empty = jnp.zeros((tap_count, grad_rows.shape[1]), grad_rows.dtype)
    return lax.fori_loop(0, tap_count, one_tap, empty)


def reference(tokens, w_feat, short_filter, mr_filter, queries, key_rows, cotangent):
    seq_rows, model_width = tokens.shape
    block_rows = seq_rows // N_CTX
    flat_weight = w_feat.reshape(model_width, 3 * model_width)
    features = jnp.dot(tokens, flat_weight, preferred_element_type=jnp.float32).astype(jnp.bfloat16)
    short_taps = short_filter.reshape(SHORT, 3 * model_width)
    feat_pad = jnp.pad(features.astype(jnp.float32), ((SHORT - 1, 0), (0, 0)))
    mixed_feat = causal_mix(feat_pad, short_taps)
    query_mix = mixed_feat[:, :model_width]
    key_mix = mixed_feat[:, model_width:2 * model_width]
    value_mix = mixed_feat[:, 2 * model_width:]
    product = (key_mix * value_mix).astype(jnp.bfloat16)
    prod_pad = jnp.pad(product.astype(jnp.float32), ((MRLEN - 1, 0), (0, 0)))
    long_mix = causal_mix(prod_pad, mr_filter)
    hyena_out = query_mix * long_mix
    hyena_stream = (tokens.astype(jnp.float32) + hyena_out).astype(jnp.bfloat16)

    head_count = model_width // DH
    score_scale = DH ** -0.5
    positions = jnp.arange(seq_rows, dtype=jnp.int32)
    allowed = positions[:, None] >= positions[None, :]

    def split_heads(array):
        return array.reshape(seq_rows, head_count, DH).transpose(1, 0, 2)

    def merge_heads(array):
        return array.transpose(1, 0, 2).reshape(seq_rows, model_width)

    def head_pass(head_items):
        query_head, key_head, value_head, grad_head = head_items
        scores = jnp.dot(query_head, key_head.T, preferred_element_type=jnp.float32) * score_scale
        scores = jnp.where(allowed, scores, -jnp.inf)
        row_top = jnp.max(scores, axis=1, keepdims=True)
        exponent = jnp.exp(scores - row_top)
        probability = exponent / jnp.sum(exponent, axis=1, keepdims=True)
        prob_half = probability.astype(jnp.bfloat16)
        attended = jnp.dot(prob_half, value_head, preferred_element_type=jnp.float32)
        prob_grad = jnp.dot(grad_head, value_head.T, preferred_element_type=jnp.float32)
        row_delta = jnp.sum(grad_head.astype(jnp.float32) * attended, axis=1, keepdims=True)
        score_grad = (probability * (prob_grad - row_delta)).astype(jnp.bfloat16)
        query_grad = jnp.dot(score_grad, key_head, preferred_element_type=jnp.float32) * score_scale
        score_blocks = score_grad.astype(jnp.float32).reshape(N_CTX, block_rows, seq_rows)
        prob_blocks = prob_half.astype(jnp.float32).reshape(N_CTX, block_rows, seq_rows)
        query_blocks = query_head.astype(jnp.float32).reshape(N_CTX, block_rows, DH)
        grad_blocks = grad_head.astype(jnp.float32).reshape(N_CTX, block_rows, DH)
        key_parts = jnp.einsum("bts,btd->bsd", score_blocks, query_blocks, precision=lax.Precision.HIGHEST) * score_scale
        value_parts = jnp.einsum("bts,btd->bsd", prob_blocks, grad_blocks, precision=lax.Precision.HIGHEST)
        key_parts = lax.optimization_barrier(key_parts.astype(jnp.bfloat16)).astype(jnp.float32)
        value_parts = lax.optimization_barrier(value_parts.astype(jnp.bfloat16)).astype(jnp.float32)
        return attended, query_grad, jnp.sum(key_parts, axis=0), jnp.sum(value_parts, axis=0)

    head_results = lax.map(head_pass, (split_heads(queries), split_heads(key_rows), split_heads(hyena_stream), split_heads(cotangent)))
    attended = merge_heads(head_results[0])
    grad_queries = merge_heads(head_results[1]).astype(jnp.bfloat16)
    grad_keys = merge_heads(head_results[2]).astype(jnp.bfloat16)
    value_sum = merge_heads(head_results[3])
    block_out = (hyena_stream.astype(jnp.float32) + attended).astype(jnp.bfloat16)

    stream_grad = (cotangent.astype(jnp.float32) + value_sum).astype(jnp.bfloat16)
    grad_out = stream_grad.astype(jnp.float32)
    mix_grad = (grad_out * query_mix).astype(jnp.bfloat16)
    mix_pad = jnp.pad(mix_grad.astype(jnp.float32), ((0, MRLEN - 1), (0, 0)))
    prod_grad = anti_mix(mix_pad, mr_filter)
    grad_mr = tap_grads(mix_grad.astype(jnp.float32), prod_pad, MRLEN)
    stack_grad = jnp.concatenate([grad_out * long_mix, prod_grad * value_mix, prod_grad * key_mix], axis=1)
    stack_pad = jnp.pad(stack_grad, ((0, SHORT - 1), (0, 0)))
    feat_grad = anti_mix(stack_pad, short_taps).astype(jnp.bfloat16)
    grad_short = tap_grads(stack_grad, feat_pad, SHORT).reshape(SHORT, 3, model_width)

    group_count = N_ROW * N_COL
    group_width = model_width // group_count
    feat_grad3 = feat_grad.reshape(seq_rows, 3, model_width)
    input_sum = jnp.zeros((seq_rows, model_width), jnp.float32)
    for group_index in range(group_count):
        first_col = group_index * group_width
        grad_cols = feat_grad3[:, :, first_col:first_col + group_width].reshape(seq_rows, 3 * group_width)
        weight_cols = w_feat[:, :, first_col:first_col + group_width].reshape(model_width, 3 * group_width)
        group_part = jnp.dot(grad_cols, weight_cols.T, preferred_element_type=jnp.float32)
        input_sum = input_sum + lax.optimization_barrier(group_part.astype(jnp.bfloat16)).astype(jnp.float32)
    grad_input = (grad_out + input_sum).astype(jnp.bfloat16)

    weight_sum = jnp.zeros((model_width, 3 * model_width), jnp.float32)
    for block_index in range(N_CTX):
        first_row = block_index * block_rows
        block_part = jnp.dot(tokens[first_row:first_row + block_rows].T, feat_grad[first_row:first_row + block_rows], preferred_element_type=jnp.float32)
        weight_sum = weight_sum + lax.optimization_barrier(block_part.astype(jnp.bfloat16)).astype(jnp.float32)
    grad_feat = weight_sum.reshape(model_width, 3, model_width)
    return (block_out, grad_input, grad_feat, grad_short, grad_mr, grad_queries, grad_keys)
```

```python
import functools

import jax
import jax.numpy as jnp
from jax import lax
from jax.experimental import pallas as pl
from jax.experimental.pallas import tpu as pltpu
from jax.sharding import PartitionSpec as P

DH = 128
SHORT = 7
MRLEN = 128
HALO = 144
TAIL = 16
ROWS = 256
HEADS = 4
SLABS = 4
SLAB = ROWS * HEADS
EXT = HALO + SLAB + HALO
WIDTH = HEADS * DH
MESH = pl.DeviceIdType.MESH
BF = jnp.bfloat16
F32 = jnp.float32


def place():
    ctx = lax.axis_index("ctx")
    return lax.div(ctx, HEADS), lax.rem(ctx, HEADS)


def turn(index, step, size):
    return lax.rem(index + (step + size), size)


def at_ctx(z, a):
    return {"ctx": z * HEADS + a}


def cols(index, width=DH):
    return pl.ds(pl.multiple_of(index * width, width), width)


def rows(index, height, offset=0):
    return pl.ds(pl.multiple_of(index * height + offset, 16), height)


def greet(devices):
    barrier = pltpu.get_barrier_semaphore()
    for device in devices:
        pl.semaphore_signal(barrier, inc=1, device_id=device, device_id_type=MESH)
    pl.semaphore_wait(barrier, len(devices))


class Courier:
    def __init__(self, send, recv, local):
        self.send, self.recv, self.local = send, recv, local
        self.remote, self.here = [], []
        self.arrived = set()
        self.settled = 0

    def push(self, src, dst, device):
        k = len(self.remote)
        copy = pltpu.make_async_remote_copy(
            src_ref=src,
            dst_ref=dst,
            send_sem=self.send.at[k],
            recv_sem=self.recv.at[k],
            device_id=device,
            device_id_type=MESH,
        )
        copy.start()
        self.remote.append(copy)
        return k

    def keep(self, src, dst):
        copy = pltpu.make_async_copy(src, dst, self.local.at[len(self.here)])
        copy.start()
        self.here.append(copy)

    def arrive(self, k):
        if k not in self.arrived:
            self.arrived.add(k)
            self.remote[k].wait_recv()

    def finish(self):
        for k in range(len(self.remote)):
            self.arrive(k)
        for copy in self.remote:
            copy.wait_send()
        self.settle()

    def settle(self):
        for copy in self.here[self.settled :]:
            copy.wait()
        self.settled = len(self.here)


def exchange(body, collective_id, outs, remotes, locals_, *ins):
    def kernel(*refs):
        body(Courier(*refs[-3:]), *refs[:-3])

    return pl.pallas_call(
        kernel,
        out_shape=outs,
        in_specs=[pl.BlockSpec(memory_space=pl.ANY)] * len(ins),
        out_specs=[pl.BlockSpec(memory_space=pl.ANY)] * len(outs),
        scratch_shapes=[
            pltpu.SemaphoreType.DMA((remotes,)),
            pltpu.SemaphoreType.DMA((remotes,)),
            pltpu.SemaphoreType.DMA((locals_,)),
        ],
        compiler_params=pltpu.CompilerParams(collective_id=collective_id, has_side_effects=True),
    )(*ins)


def shape(*dims, kind=BF):
    return jax.ShapeDtypeStruct(dims, kind)


def inputs_kernel(mail, tokens, queries, keys, cot, full, th, qh, kh, ch, pieces):
    z, a = place()
    row, col = lax.axis_index("row"), lax.axis_index("col")
    other = 1 - row
    right, left = turn(col, 1, 4), turn(col, -1, 4)
    mates = [at_ctx(z, turn(a, d, HEADS)) for d in range(1, HEADS)]
    greet([{"row": other}, {"col": right}, {"col": left}] + mates)

    def block(r, c):
        return full.at[:, cols(r * 4 + c, WIDTH)]

    def half(r, c, h):
        return full.at[pl.ds(h * (ROWS // 2), ROWS // 2), cols(r * 4 + c, WIDTH)]

    up = mail.push(tokens, block(row, col), {"row": other})
    fr = mail.push(tokens, block(row, col), {"col": right})
    fl = mail.push(tokens, block(row, col), {"col": left})
    mail.keep(tokens, block(row, col))
    for src, dst in ((tokens, th), (queries, qh), (keys, kh), (cot, ch)):
        for d in range(1, HEADS):
            to = turn(a, d, HEADS)
            mail.push(src.at[:, cols(to)], dst.at[rows(a, ROWS)], at_ctx(z, to))
        mail.keep(src.at[:, cols(a)], dst.at[rows(a, ROWS)])
    mail.arrive(up)
    gr = mail.push(block(other, col), block(other, col), {"col": right})
    gl = mail.push(block(other, col), block(other, col), {"col": left})
    for r, from_left, from_right in ((row, fr, fl), (other, gr, gl)):
        mail.arrive(from_left)
        mail.push(half(r, left, 0), half(r, left, 0), {"col": right})
        mail.arrive(from_right)
        mail.push(half(r, right, 1), half(r, right, 1), {"col": left})
    mail.finish()
    for d in range(HEADS):
        for s in range(SLABS):
            mail.keep(
                full.at[:, cols(s * HEADS + turn(a, d, HEADS), ROWS)], pieces.at[d, :, pl.ds(s * ROWS, ROWS)]
            )
    mail.settle()


def slab_gather(mail, part, whole, z, a):
    up, down = turn(z, 1, SLABS), turn(z, -1, SLABS)
    mine = whole.at[rows(z, SLAB)]
    mail.keep(part, mine)
    return mail.push(part, mine, at_ctx(up, a)), mail.push(part, mine, at_ctx(down, a))


def slab_relay(mail, whole, z, a, from_down, from_up):
    up, down = turn(z, 1, SLABS), turn(z, -1, SLABS)
    half = SLAB // 2
    mail.arrive(from_down)
    lower = whole.at[pl.ds(pl.multiple_of(down * SLAB, 16), half)]
    mail.push(lower, lower, at_ctx(up, a))
    mail.arrive(from_up)
    upper = whole.at[pl.ds(pl.multiple_of(up * SLAB + half, 16), half)]
    mail.push(upper, upper, at_ctx(down, a))


def features_kernel(mail, feats, cot, kh, fx, chalo, kfull):
    z, a = place()
    up, down = turn(z, 1, SLABS), turn(z, -1, SLABS)
    peers = [at_ctx(z, turn(a, d, HEADS)) for d in range(1, HEADS)]
    peers += [at_ctx(s, b) for s in (up, down) for b in range(HEADS)]
    greet(peers)
    for d in range(1, HEADS):
        to = turn(a, d, HEADS)
        mail.push(feats.at[:, :, cols(to)], fx.at[:, rows(a, ROWS, HALO)], at_ctx(z, to))
    mail.keep(feats.at[:, :, cols(a)], fx.at[:, rows(a, ROWS, HALO)])
    keys = slab_gather(mail, kh, kfull, z, a)

    n = len(mail.remote)

    def edge(src, dst, k, b, device):
        return pltpu.make_async_remote_copy(
            src_ref=src,
            dst_ref=dst,
            send_sem=mail.send.at[k + 3 * b],
            recv_sem=mail.recv.at[k],
            device_id=device,
            device_id_type=MESH,
        )

    def first(b):
        return (
            edge(feats.at[:, pl.ds(0, HALO), pl.ds(b * DH, DH)], fx.at[:, pl.ds(HALO + SLAB, HALO)], n + 2, b, at_ctx(down, b)),
            edge(cot.at[pl.ds(0, HALO), pl.ds(b * DH, DH)], chalo, n + 3, b, at_ctx(down, b)),
        )

    def last(b):
        return (edge(feats.at[:, pl.ds(ROWS - HALO, HALO), pl.ds(b * DH, DH)], fx.at[:, pl.ds(0, HALO)], n + 4, b, at_ctx(up, b)),)

    @pl.when(a == 0)
    def _():
        for b in range(HEADS):
            for copy in first(b):
                copy.start()

    @pl.when(a == HEADS - 1)
    def _():
        for b in range(HEADS):
            for copy in last(b):
                copy.start()

    slab_relay(mail, kfull, z, a, *keys)
    mail.finish()
    for copy in first(0) + last(0):
        copy.wait_recv()

    @pl.when(a == 0)
    def _():
        for b in range(HEADS):
            for copy in first(b):
                copy.wait_send()

    @pl.when(a == HEADS - 1)
    def _():
        for b in range(HEADS):
            for copy in last(b):
                copy.wait_send()


def stream_kernel(mail, part, whole):
    z, a = place()
    greet([at_ctx(turn(z, 1, SLABS), a), at_ctx(turn(z, -1, SLABS), a)])
    slab_relay(mail, whole, z, a, *slab_gather(mail, part, whole, z, a))
    mail.finish()


def around(z, a):
    return [at_ctx(turn(z, d, SLABS), a) for d in range(1, SLABS)] + [
        at_ctx(z, turn(a, d, HEADS)) for d in range(1, HEADS)
    ]


def home(mail, src, dst, z, a):
    for d in range(1, HEADS):
        to = turn(a, d, HEADS)
        mail.push(src.at[rows(to, ROWS)], dst.at[:, cols(a)], at_ctx(z, to))
    mail.keep(src.at[rows(a, ROWS)], dst.at[:, cols(a)])


def values_kernel(mail, dv, dk, block, dq, dvr, dkr, block_home, dq_home):
    z, a = place()
    greet(around(z, a))
    for d in range(1, SLABS):
        to = turn(z, d, SLABS)
        mail.push(dv.at[pl.ds(pl.multiple_of(to * SLAB, 16), SLAB + HALO)], dvr.at[z], at_ctx(to, a))
    mail.keep(dv.at[pl.ds(pl.multiple_of(z * SLAB, 16), SLAB + HALO)], dvr.at[z])
    for d in range(1, SLABS):
        to = turn(z, d, SLABS)
        mail.push(dk.at[rows(to, SLAB)], dkr.at[z], at_ctx(to, a))
    mail.keep(dk.at[rows(z, SLAB)], dkr.at[z])
    home(mail, block, block_home, z, a)
    home(mail, dq, dq_home, z, a)
    mail.finish()


def finale_kernel(
    fg, sg, dk, small, part0, part1, part2, part3, weights,
    grad_input, grad_feat, dk_home, small_home,
    w, tq, tqt, fgall, fgm, wsend, zr1, zr2, tsend, xr1, xr2, yr, ysend, sgh, slots, total,
    send, recv, loc,
):
    mail = Courier(send, recv, loc)
    z, a = place()
    row, col = lax.axis_index("row"), lax.axis_index("col")
    side, core = lax.div(a, 2), lax.rem(a, 2)
    mate, far, far_mate = side * 2 + 1 - core, (1 - side) * 2 + core, (1 - side) * 2 + 1 - core
    up, down = turn(z, 1, SLABS), turn(z, -1, SLABS)
    right, left = turn(col, 1, 4), turn(col, -1, 4)
    half = ROWS // 2
    pair = 2 * ROWS

    mail.keep(fg, fgall.at[a])
    for d, part in enumerate((part0, part1, part2, part3)):
        mail.keep(part, tq.at[rows(turn(a, -d, HEADS), ROWS)])
    for j in range(3):
        mail.keep(weights.at[j], w.at[j])
    greet(around(z, a) + [{"row": 1 - row}, {"col": right}, {"col": left}])

    near_rows, far_rows = rows(side, pair), rows(1 - side, pair)
    to_mate = mail.push(fg, fgall.at[a], at_ctx(z, mate))
    first = mail.push(fg.at[:, far_rows], fgall.at[a, :, far_rows], at_ctx(z, far))
    second = mail.push(fg.at[:, near_rows], fgall.at[a, :, near_rows], at_ctx(z, far))
    small_in = [mail.push(small, slots.at[d - 1], at_ctx(turn(z, d, SLABS), a)) for d in range(1, SLABS)]
    home_sg = []
    for d in range(1, HEADS):
        to = turn(a, d, HEADS)
        home_sg.append(mail.push(sg.at[rows(to, ROWS)], sgh.at[:, cols(a)], at_ctx(z, to)))
        mail.push(dk.at[rows(to, ROWS)], dk_home.at[:, cols(a)], at_ctx(z, to))
    mail.keep(sg.at[rows(a, ROWS)], sgh.at[:, cols(a)])
    mail.keep(dk.at[rows(a, ROWS)], dk_home.at[:, cols(a)])
    mail.settle()

    for b in range(SLABS):
        tqt[pl.ds(b * ROWS, ROWS)] = tq[:, pl.ds(b * ROWS, ROWS)].T

    def weight_block(n, head, dz):
        rhs = jnp.concatenate([fgall[head, j] for j in range(3)], axis=1)
        lhs = tqt[rows(turn(z, dz, SLABS), ROWS)]
        out = jnp.dot(lhs, rhs, preferred_element_type=F32)
        for j in range(3):
            wsend[n, dz, j] = out[:, j * DH : (j + 1) * DH].astype(BF)

    def weight_first(n, head):
        weight_block(n, head, 2)
        keys = (
            mail.push(wsend.at[n, 2, :, pl.ds(0, half)], zr1.at[n, 0], at_ctx(up, a)),
            mail.push(wsend.at[n, 2, :, pl.ds(half, half)], zr1.at[n, 1], at_ctx(down, a)),
        )
        for dz in (1, 3, 0):
            weight_block(n, head, dz)
        return keys

    def weight_second(n, keys):
        top, bottom = pl.ds(0, half), pl.ds(half, half)
        mail.arrive(keys[0])
        wsend[n, 1, :, top] = (wsend[n, 1, :, top].astype(F32) + zr1[n, 0].astype(F32)).astype(BF)
        one = mail.push(wsend.at[n, 1], zr2.at[n, 0], at_ctx(up, a))
        mail.arrive(keys[1])
        wsend[n, 3, :, bottom] = (wsend[n, 3, :, bottom].astype(F32) + zr1[n, 1].astype(F32)).astype(BF)
        return one, mail.push(wsend.at[n, 3], zr2.at[n, 1], at_ctx(down, a))

    def weight_third(n, head, keys):
        for k in keys:
            mail.arrive(k)
        for j in range(3):
            grad_feat[j, :, cols(head)] = (
                wsend[n, 0, j].astype(F32) + zr2[n, 0, j].astype(F32) + zr2[n, 1, j].astype(F32)
            )

    ring = [weight_first(0, a)]
    mail.arrive(to_mate)
    ring.append(weight_first(1, mate))
    mail.arrive(first)
    relay = mail.push(fgall.at[far, :, near_rows], fgall.at[far, :, near_rows], at_ctx(z, mate))
    ring[0] = weight_second(0, ring[0])
    ring[1] = weight_second(1, ring[1])
    mail.arrive(relay)

    for j in range(3):
        for h in range(HEADS):
            fgm[j, :, pl.ds(h * DH, DH)] = fgall[h, j, rows(a, ROWS)]

    def term_block(dc):
        for r in range(2):
            columns = rows(r * 4 + turn(col, dc, 4), WIDTH)
            out = jnp.zeros((ROWS, WIDTH), F32)
            for j in range(3):
                out += lax.dot_general(
                    fgm[j], w[j, columns], (((1,), (1,)), ((), ())), preferred_element_type=F32
                )
            tsend[dc, r] = out.astype(BF)

    top, bottom = pl.ds(0, half), pl.ds(half, half)
    term_block(2)
    from_left = mail.push(tsend.at[2, :, top], xr1.at[0], {"col": right})
    from_right = mail.push(tsend.at[2, :, bottom], xr1.at[1], {"col": left})
    term_block(1)
    term_block(3)
    mail.arrive(from_left)
    tsend[1, :, top] = (tsend[1, :, top].astype(F32) + xr1[0].astype(F32)).astype(BF)
    from_left = mail.push(tsend.at[1], xr2.at[0], {"col": right})
    mail.arrive(from_right)
    tsend[3, :, bottom] = (tsend[3, :, bottom].astype(F32) + xr1[1].astype(F32)).astype(BF)
    from_right = mail.push(tsend.at[3], xr2.at[1], {"col": left})
    term_block(0)

    mail.arrive(second)
    relay = mail.push(fgall.at[far, :, far_rows], fgall.at[far, :, far_rows], at_ctx(z, mate))
    ring.append(weight_first(2, far))
    mail.arrive(relay)
    ring.append(weight_first(3, far_mate))
    ring[2] = weight_second(2, ring[2])
    ring[3] = weight_second(3, ring[3])

    for k in small_in:
        mail.arrive(k)
    total[...] = (small_sum(small, slots)).astype(BF)
    for d in range(1, HEADS):
        mail.push(total, small_home.at[:, cols(a)], at_ctx(z, turn(a, d, HEADS)))
    mail.keep(total, small_home.at[:, cols(a)])

    mail.arrive(from_left)
    mail.arrive(from_right)

    def term_sum(r):
        return tsend[0, r].astype(F32) + xr2[0, r].astype(F32) + xr2[1, r].astype(F32)

    ysend[...] = term_sum(1 - row).astype(BF)
    across = mail.push(ysend, yr, {"row": 1 - row})
    weight_third(0, a, ring[0])
    weight_third(1, mate, ring[1])
    for k in home_sg:
        mail.arrive(k)
    mail.arrive(across)
    grad_input[...] = (sgh[...].astype(F32) + term_sum(row) + yr[...].astype(F32)).astype(BF)
    weight_third(2, far, ring[2])
    weight_third(3, far_mate, ring[3])
    mail.finish()


def small_sum(small, slots):
    return small[...].astype(F32) + sum(slots[d].astype(F32) for d in range(SLABS - 1))


def finale(fg, sg, dk, small, parts, weights):
    lines = small.shape[0]
    any_space, vmem = pl.BlockSpec(memory_space=pl.ANY), pl.BlockSpec(memory_space=pltpu.VMEM)
    remotes = 3 + 3 + 6 + 16 + 2 + 4 + 3 + 1
    return pl.pallas_call(
        finale_kernel,
        out_shape=[
            shape(ROWS, WIDTH),
            shape(3, ROWS, WIDTH, kind=F32),
            shape(ROWS, WIDTH),
            shape(lines, WIDTH),
        ],
        in_specs=[any_space, any_space, any_space, vmem] + [any_space] * 5,
        out_specs=[vmem, vmem, any_space, any_space],
        scratch_shapes=[
            pltpu.VMEM(weights.shape, BF),
            pltpu.VMEM((SLAB, SLABS * ROWS), BF),
            pltpu.VMEM((SLABS * ROWS, SLAB), BF),
            pltpu.VMEM((HEADS, 3, SLAB, DH), BF),
            pltpu.VMEM((3, ROWS, WIDTH), BF),
            pltpu.VMEM((HEADS, SLABS, 3, ROWS, DH), BF),
            pltpu.VMEM((HEADS, 2, 3, ROWS // 2, DH), BF),
            pltpu.VMEM((HEADS, 2, 3, ROWS, DH), BF),
            pltpu.VMEM((4, 2, ROWS, WIDTH), BF),
            pltpu.VMEM((2, 2, ROWS // 2, WIDTH), BF),
            pltpu.VMEM((2, 2, ROWS, WIDTH), BF),
            pltpu.VMEM((ROWS, WIDTH), BF),
            pltpu.VMEM((ROWS, WIDTH), BF),
            pltpu.VMEM((ROWS, WIDTH), BF),
            pltpu.VMEM((SLABS - 1, lines, DH), BF),
            pltpu.VMEM((lines, DH), BF),
            pltpu.SemaphoreType.DMA((remotes,)),
            pltpu.SemaphoreType.DMA((remotes,)),
            pltpu.SemaphoreType.DMA((11,)),
        ],
        compiler_params=pltpu.CompilerParams(
            collective_id=5, has_side_effects=True, vmem_limit_bytes=56 << 20
        ),
    )(fg, sg, dk, small, *parts, weights)


def compute(body, outs, scratch, *ins, vmem=56 << 20):
    z, a = place()
    return pl.pallas_call(
        body,
        out_shape=outs,
        in_specs=[pl.BlockSpec(memory_space=pltpu.SMEM)] + [pl.BlockSpec(memory_space=pltpu.VMEM)] * len(ins),
        out_specs=[pl.BlockSpec(memory_space=pltpu.VMEM)] * len(outs),
        scratch_shapes=scratch,
        compiler_params=pltpu.CompilerParams(vmem_limit_bytes=vmem),
    )(jnp.stack([z, a]).astype(jnp.int32), *ins)


GROUP = 40


def spread_taps(spread, taps, a):
    for i in range(MRLEN):
        spread[i] = jnp.broadcast_to(taps[pl.ds(i, 1), cols(a)], (8, DH))


def hyena_body(where, fx, short, mr, tok, stream, qm, km, vm, lm, pr, feat, spread):
    z, a = where[0], where[1]
    spread_taps(spread, mr, a)
    keep_head = (z > 0).astype(F32)
    keep_tail = (z < SLABS - 1).astype(F32)
    for j in range(3):
        feat[j, pl.ds(0, HALO)] = fx[j, pl.ds(0, HALO)].astype(F32) * keep_head
        feat[j, pl.ds(HALO, SLAB)] = fx[j, pl.ds(HALO, SLAB)].astype(F32)
        feat[j, pl.ds(HALO + SLAB, HALO)] = fx[j, pl.ds(HALO + SLAB, HALO)].astype(F32) * keep_tail

    taps = [[short[j, pl.ds(s, 1), cols(a)] for s in range(SHORT)] for j in range(3)]

    def mixed(j, base, count):
        total = taps[j][0] * feat[j, pl.ds(base, count)]
        for s in range(1, SHORT):
            total += taps[j][s] * feat[j, pl.ds(base - s, count)]
        return total

    pr[pl.ds(0, 16)] = jnp.zeros((16, DH), F32)

    def head_step(g, carry):
        base = pl.multiple_of(16 + g * 16, 16)
        pr[pl.ds(base, 16)] = (mixed(1, base, 16) * mixed(2, base, 16)).astype(BF).astype(F32)
        return carry

    lax.fori_loop(0, (HALO - 16) // 16, head_step, 0)

    def mix_step(g, carry):
        base = pl.multiple_of(HALO + g * GROUP, 8)
        local = pl.multiple_of(g * GROUP, 8)
        key, value = mixed(1, base, GROUP), mixed(2, base, GROUP)
        km[pl.ds(local, GROUP)] = key
        vm[pl.ds(local, GROUP)] = value
        qm[pl.ds(local, GROUP)] = mixed(0, base, GROUP)
        pr[pl.ds(base, GROUP)] = (key * value).astype(BF).astype(F32)
        return carry

    lax.fori_loop(0, (SLAB + TAIL) // GROUP, mix_step, 0)

    def tail_step(g, carry):
        local = pl.multiple_of(SLAB + TAIL + g * 16, 16)
        qm[pl.ds(local, 16)] = mixed(0, local + HALO, 16)
        return carry

    lax.fori_loop(0, (HALO - TAIL) // 16, tail_step, 0)

    def long_step(g, carry):
        base = pl.multiple_of(HALO + g * GROUP, 8)
        local = pl.multiple_of(g * GROUP, 8)
        total = [jnp.zeros((8, DH), F32) for _ in range(GROUP // 8)]
        for i in range(MRLEN):
            tap = spread[i]
            for n in range(GROUP // 8):
                total[n] += tap * pr[pl.ds(base + (n * 8 - i), 8)]
        for n in range(GROUP // 8):
            lm[pl.ds(local + n * 8, 8)] = total[n]
        return carry

    lax.fori_loop(0, (SLAB + TAIL) // GROUP, long_step, 0)
    own = pl.ds(0, SLAB)
    stream[...] = (tok[...].astype(F32) + qm[own] * lm[own]).astype(BF)


def attention_body(where, q, k, v, ct, own_stream, block, dq, dk, dv, st, pt, kt, vt, dka, dva):
    z = where[0]
    scale = DH ** -0.5
    gain = scale * 1.4426950408889634
    dka[...] = jnp.zeros_like(dka)
    dva[...] = jnp.zeros_like(dva)
    kt[...] = k[...].T
    vt[...] = v[...].T

    def dot(x, y):
        return jnp.dot(x, y, preferred_element_type=F32)

    def dot_t(x, y):
        return lax.dot_general(x, y, (((1,), (1,)), ((), ())), preferred_element_type=F32)

    for i in range(HEADS):
        span = ROWS * (i + 1)
        here = pl.ds(i * ROWS, ROWS)
        qb, cb = q[here], ct[here]
        own = pl.ds(pl.multiple_of(z * SLAB, SLAB), span)
        own_lanes = pl.ds(pl.multiple_of(z * SLAB, SLAB), span)
        scores = dot_t(k[own], qb)
        after = lax.broadcasted_iota(jnp.int32, (ROWS, ROWS), 0) > lax.broadcasted_iota(jnp.int32, (ROWS, ROWS), 1)
        corner = jnp.where(after, -1e30, scores[span - ROWS :])
        top = jnp.max(corner, axis=0, keepdims=True)
        if i:
            top = jnp.maximum(top, jnp.max(scores[: span - ROWS], axis=0, keepdims=True))
            st[pl.ds(0, span - ROWS)] = scores[: span - ROWS]
        st[pl.ds(span - ROWS, ROWS)] = corner

        def score_step(s, top):
            past = dot_t(k[pl.ds(pl.multiple_of(s * SLAB, SLAB), SLAB)], qb)
            st[pl.ds(pl.multiple_of((s + 1) * SLAB, SLAB), SLAB)] = past
            return jnp.maximum(top, jnp.max(past, axis=0, keepdims=True))

        top = lax.fori_loop(0, z, score_step, top) * gain

        def weigh(slots, lanes, total, out):
            p = jnp.exp2(st[slots] * gain - top)
            total += jnp.sum(p, axis=0, keepdims=True)
            p = p.astype(BF)
            pt[slots] = p
            return total, out + dot(vt[:, lanes], p)

        carry = weigh(pl.ds(0, span), own_lanes, jnp.zeros((1, ROWS), F32), jnp.zeros((DH, ROWS), F32))

        def weigh_step(s, carry):
            return weigh(
                pl.ds(pl.multiple_of((s + 1) * SLAB, SLAB), SLAB), pl.ds(pl.multiple_of(s * SLAB, SLAB), SLAB), *carry
            )

        total, out = lax.fori_loop(0, z, weigh_step, carry)
        inverse = 1.0 / total
        out = out * inverse
        block[here] = (own_stream[here].astype(F32) + out.T).astype(BF)
        ctt = (cb.astype(F32).T * inverse).astype(BF)
        delta = jnp.sum(ctt.astype(F32) * out, axis=0, keepdims=True)
        cs = ctt.T

        def grads(slots, lanes, dqt):
            p = pt[slots]
            dva[lanes] += dot(p, cs)
            dp = dot(v[lanes], ctt)
            ds = (p.astype(F32) * (dp - delta)).astype(BF)
            dka[lanes] += dot(ds, qb)
            return dqt + dot(kt[:, lanes], ds)

        dqt = grads(pl.ds(0, span), own, jnp.zeros((DH, ROWS), F32))

        def grad_step(s, dqt):
            return grads(
                pl.ds(pl.multiple_of((s + 1) * SLAB, SLAB), SLAB), pl.ds(pl.multiple_of(s * SLAB, SLAB), SLAB), dqt
            )

        dqt = lax.fori_loop(0, z, grad_step, dqt)
        dq[here] = (dqt.T * scale).astype(BF)
    dk[...] = (dka[...] * scale).astype(BF)
    whole = SLABS * SLAB
    dv[pl.ds(0, whole)] = dva[...].astype(BF)
    dv[pl.ds(whole, HALO)] = jnp.zeros((HALO, DH), BF)


def back_body(where, dvr, dkr, ch, chalo, fx, short, mr, qm, km, vm, lm, pr, sg, fg, dk, small, mg, stack, feat, spread):
    z, a = where[0], where[1]
    spread_taps(spread, mr, a)
    keep_head = (z > 0).astype(F32)
    keep_tail = (z < SLABS - 1).astype(F32)
    own, halo = pl.ds(0, SLAB), pl.ds(SLAB, HALO)

    def value_sum(part):
        return sum(dvr[s, part].astype(F32) for s in range(SLABS))

    dk[...] = sum(dkr[s].astype(F32) for s in range(SLABS)).astype(BF)
    grad = (ch[...].astype(F32) + value_sum(own)).astype(BF)
    sg[...] = grad
    mg[own] = (grad.astype(F32) * qm[own]).astype(BF).astype(F32)
    grad_halo = (chalo[...].astype(F32) + value_sum(halo)).astype(BF).astype(F32) * keep_tail
    mg[halo] = (grad_halo * qm[halo]).astype(BF).astype(F32)
    stack[0, own] = grad.astype(F32) * lm[own]
    stack[0, pl.ds(SLAB, TAIL)] = grad_halo[:TAIL] * lm[pl.ds(SLAB, TAIL)]
    for j in range(3):
        feat[j, pl.ds(0, 16)] = fx[j, pl.ds(HALO - 16, 16)].astype(F32) * keep_head
        feat[j, pl.ds(16, SLAB)] = fx[j, pl.ds(HALO, SLAB)].astype(F32)

    def long_step(g, carry):
        local = pl.multiple_of(g * GROUP, 8)
        total = [jnp.zeros((8, DH), F32) for _ in range(GROUP // 8)]
        for i in range(MRLEN):
            tap = spread[i]
            for n in range(GROUP // 8):
                total[n] += tap * mg[pl.ds(local + (n * 8 + i), 8)]
        for n in range(GROUP // 8):
            part = pl.ds(local + n * 8, 8)
            stack[1, part] = total[n] * vm[part]
            stack[2, part] = total[n] * km[part]
        return carry

    lax.fori_loop(0, (SLAB + TAIL) // GROUP, long_step, 0)

    for j in range(3):
        taps = [short[j, pl.ds(s, 1), cols(a)] for s in range(SHORT)]

        def short_step(g, sums):
            base = pl.multiple_of(g * 32, 32)
            total = taps[0] * stack[j, pl.ds(base, 32)]
            for s in range(1, SHORT):
                total += taps[s] * stack[j, pl.ds(base + s, 32)]
            fg[j, pl.ds(base, 32)] = total.astype(BF)
            out = []
            for s in range(SHORT):
                term = stack[j, pl.ds(base, 32)] * feat[j, pl.ds(base + 16 - s, 32)]
                out.append(sums[s] + (term[0:8] + term[8:16] + term[16:24] + term[24:32]))
            return tuple(out)

        sums = lax.fori_loop(0, SLAB // 32, short_step, tuple(jnp.zeros((8, DH), F32) for _ in range(SHORT)))
        lines = [jnp.sum(t, axis=0, keepdims=True) for t in sums]
        small[pl.ds(MRLEN + 16 * j, 16)] = jnp.concatenate(lines + [jnp.zeros((16 - SHORT, DH), F32)], axis=0).astype(BF)

    def tap_step(c, carry):
        first = c * 16

        def row_step(g, sums):
            base = pl.multiple_of(g * 16, 16)
            out = list(sums)
            for n in range(2):
                line = mg[pl.ds(base + n * 8, 8)]
                for s in range(16):
                    out[s] += line * pr[pl.ds(base + (HALO + n * 8 - s) - first, 8)]
            return tuple(out)

        sums = lax.fori_loop(0, SLAB // 16, row_step, tuple(jnp.zeros((8, DH), F32) for _ in range(16)))
        lines = [jnp.sum(t, axis=0, keepdims=True) for t in sums]
        small[pl.ds(pl.multiple_of(first, 16), 16)] = jnp.concatenate(lines, axis=0).astype(BF)
        return carry

    lax.fori_loop(0, MRLEN // 16, tap_step, 0)


def local(tokens, w_feat, short_filter, mr_filter, queries, key_rows, cotangent):
    weights = w_feat.transpose(1, 0, 2)
    short_taps = short_filter.transpose(1, 0, 2)
    head = shape(SLAB, DH)
    full, th, qh, kh, ch, pieces = exchange(
        inputs_kernel, 0, [shape(ROWS, 8 * WIDTH), head, head, head, head, shape(HEADS, ROWS, SLABS * ROWS)], 21, 5 + HEADS * SLABS, tokens, queries, key_rows, cotangent
    )
    feats = jnp.einsum("tc,jck->jtk", full, weights, preferred_element_type=F32).astype(BF)
    fx, chalo, kfull = exchange(
        features_kernel, 1, [shape(3, EXT, DH), shape(HALO, DH), shape(SLABS * SLAB, DH)], 19, 2, feats, cotangent, kh
    )
    pieces, fx = lax.optimization_barrier((pieces, fx))
    token_parts = [pieces[0]]
    for d in range(1, HEADS):
        route = [(s * HEADS + a, s * HEADS + (a + d) % HEADS) for s in range(SLABS) for a in range(HEADS)]
        token_parts.append(lax.ppermute(pieces[d], "ctx", route))
    filters = [pltpu.VMEM((MRLEN, 8, DH), F32)]
    stream, qm, km, vm, lm, pr = compute(
        hyena_body,
        [
            head,
            shape(SLAB + HALO, DH, kind=F32),
            shape(SLAB + TAIL, DH, kind=F32),
            shape(SLAB + TAIL, DH, kind=F32),
            shape(SLAB + TAIL, DH, kind=F32),
            shape(HALO + SLAB + TAIL, DH, kind=F32),
        ],
        [pltpu.VMEM((3, EXT, DH), F32)] + filters,
        fx,
        short_taps,
        mr_filter,
        th,
    )
    (vfull,) = exchange(stream_kernel, 2, [shape(SLABS * SLAB, DH)], 4, 1, stream)
    whole = SLABS * SLAB
    block, dq, dk, dv = compute(
        attention_body,
        [head, head, shape(whole, DH), shape(whole + HALO, DH)],
        [
            pltpu.VMEM((whole + SLAB, ROWS), F32),
            pltpu.VMEM((whole + SLAB, ROWS), BF),
            pltpu.VMEM((DH, whole), BF),
            pltpu.VMEM((DH, whole), BF),
            pltpu.VMEM((whole, DH), F32),
            pltpu.VMEM((whole, DH), F32),
        ],
        qh,
        kfull,
        vfull,
        ch,
        stream,
    )
    mine = shape(ROWS, WIDTH)
    dvr, dkr, block_out, grad_queries = exchange(
        values_kernel,
        3,
        [shape(SLABS, SLAB + HALO, DH), shape(SLABS, SLAB, DH), mine, mine],
        12,
        4,
        dv,
        dk,
        block,
        dq,
    )
    sg, fg, dk_sum, small = compute(
        back_body,
        [head, shape(3, SLAB, DH), head, shape(MRLEN + 3 * 16, DH)],
        [
            pltpu.VMEM((SLAB + HALO, DH), F32),
            pltpu.VMEM((3, SLAB + TAIL, DH), F32),
            pltpu.VMEM((3, SLAB + 16, DH), F32),
        ]
        + filters,
        dvr,
        dkr,
        ch,
        chalo,
        fx,
        short_taps,
        mr_filter,
        qm,
        km,
        vm,
        lm,
        pr,
    )
    grad_input, grad_feat, grad_keys, small_home = finale(fg, sg, dk_sum, small, token_parts, weights)
    sums = small_home.astype(F32)
    grad_short = sums[MRLEN:].reshape(3, 16, WIDTH)[:, :SHORT].transpose(1, 0, 2)
    grad_feat = grad_feat.transpose(1, 0, 2)
    grad_mr = sums[:MRLEN]
    return (block_out, grad_input, grad_feat, grad_short, grad_mr, grad_queries, grad_keys)


def solution(mesh):
    placed = (
        P("ctx", ("row", "col")),
        P(None, None, ("row", "col")),
        P(None, None, ("row", "col")),
        P(None, ("row", "col")),
        P("ctx", ("row", "col")),
        P("ctx", ("row", "col")),
        P("ctx", ("row", "col")),
    )
    return jax.shard_map(
        local,
        mesh=mesh,
        in_specs=placed,
        out_specs=(
            P("ctx", ("row", "col")),
            P("ctx", ("row", "col")),
            P("ctx", None, ("row", "col")),
            P(None, None, ("row", "col")),
            P(None, ("row", "col")),
            P("ctx", ("row", "col")),
            P("ctx", ("row", "col")),
        ),
        check_vma=False,
    )
```

```python
import functools

import jax
import jax.numpy as jnp
from jax import lax
from jax.experimental import pallas as pl
from jax.experimental.pallas import tpu as pltpu
from jax.sharding import PartitionSpec as P

DH = 128
SHORT = 7
MRLEN = 128
HALO = 144
TAIL = 16
ROWS = 256
HEADS = 4
SLABS = 4
SLAB = ROWS * HEADS
EXT = HALO + SLAB + HALO
WIDTH = HEADS * DH
MESH = pl.DeviceIdType.MESH
BF = jnp.bfloat16
F32 = jnp.float32


def place():
    ctx = lax.axis_index("ctx")
    return lax.div(ctx, HEADS), lax.rem(ctx, HEADS)


def turn(index, step, size):
    return lax.rem(index + (step + size), size)


def at_ctx(z, a):
    return {"ctx": z * HEADS + a}


def cols(index, width=DH):
    return pl.ds(pl.multiple_of(index * width, width), width)


def rows(index, height, offset=0):
    return pl.ds(pl.multiple_of(index * height + offset, 16), height)


def greet(devices):
    barrier = pltpu.get_barrier_semaphore()
    for device in devices:
        pl.semaphore_signal(barrier, inc=1, device_id=device, device_id_type=MESH)
    pl.semaphore_wait(barrier, len(devices))


class Courier:
    def __init__(self, send, recv, local):
        self.send, self.recv, self.local = send, recv, local
        self.remote, self.here = [], []
        self.arrived = set()
        self.settled = 0

    def push(self, src, dst, device):
        k = len(self.remote)
        copy = pltpu.make_async_remote_copy(
            src_ref=src,
            dst_ref=dst,
            send_sem=self.send.at[k],
            recv_sem=self.recv.at[k],
            device_id=device,
            device_id_type=MESH,
        )
        copy.start()
        self.remote.append(copy)
        return k

    def keep(self, src, dst):
        copy = pltpu.make_async_copy(src, dst, self.local.at[len(self.here)])
        copy.start()
        self.here.append(copy)

    def arrive(self, k):
        if k not in self.arrived:
            self.arrived.add(k)
            self.remote[k].wait_recv()

    def finish(self):
        for k in range(len(self.remote)):
            self.arrive(k)
        for copy in self.remote:
            copy.wait_send()
        self.settle()

    def settle(self):
        for copy in self.here[self.settled :]:
            copy.wait()
        self.settled = len(self.here)


def exchange(body, collective_id, outs, remotes, locals_, *ins):
    def kernel(*refs):
        body(Courier(*refs[-3:]), *refs[:-3])

    return pl.pallas_call(
        kernel,
        out_shape=outs,
        in_specs=[pl.BlockSpec(memory_space=pl.ANY)] * len(ins),
        out_specs=[pl.BlockSpec(memory_space=pl.ANY)] * len(outs),
        scratch_shapes=[
            pltpu.SemaphoreType.DMA((remotes,)),
            pltpu.SemaphoreType.DMA((remotes,)),
            pltpu.SemaphoreType.DMA((locals_,)),
        ],
        compiler_params=pltpu.CompilerParams(collective_id=collective_id, has_side_effects=True),
    )(*ins)


def shape(*dims, kind=BF):
    return jax.ShapeDtypeStruct(dims, kind)


def slab_gather(mail, part, whole, z, a):
    up, down = turn(z, 1, SLABS), turn(z, -1, SLABS)
    mine = whole.at[rows(z, SLAB)]
    mail.keep(part, mine)
    return mail.push(part, mine, at_ctx(up, a)), mail.push(part, mine, at_ctx(down, a))


def slab_relay(mail, whole, z, a, from_down, from_up):
    up, down = turn(z, 1, SLABS), turn(z, -1, SLABS)
    half = SLAB // 2
    mail.arrive(from_down)
    lower = whole.at[pl.ds(pl.multiple_of(down * SLAB, 16), half)]
    mail.push(lower, lower, at_ctx(up, a))
    mail.arrive(from_up)
    upper = whole.at[pl.ds(pl.multiple_of(up * SLAB + half, 16), half)]
    mail.push(upper, upper, at_ctx(down, a))


def front_kernel(
    tokens, queries, keys, cot, weights,
    th, qh, ch, chalo, fx, kfull, pieces,
    full, w, acc, feats, kh, send, recv, loc,
):
    mail = Courier(send, recv, loc)
    z, a = place()
    row, col = lax.axis_index("row"), lax.axis_index("col")
    other = 1 - row
    right, left, across = turn(col, 1, 4), turn(col, -1, 4), turn(col, 2, 4)
    up, down = turn(z, 1, SLABS), turn(z, -1, SLABS)
    for j in range(3):
        mail.keep(weights.at[j], w.at[j])
    greet(
        [{"row": other}, {"col": right}, {"col": left}]
        + [at_ctx(z, turn(a, d, HEADS)) for d in range(1, HEADS)]
        + [at_ctx(s, b) for s in (up, down) for b in range(HEADS)]
    )

    def block(r, c):
        return full.at[:, cols(r * 4 + c, WIDTH)]

    def half(r, c, h):
        return full.at[pl.ds(h * (ROWS // 2), ROWS // 2), cols(r * 4 + c, WIDTH)]

    def project(r, c, lhs=None):
        lhs = full[:, cols(r * 4 + c, WIDTH)] if lhs is None else lhs
        for j in range(3):
            acc[j] += jnp.dot(lhs, w[j, rows(r * 4 + c, WIDTH)], preferred_element_type=F32)

    vertical = mail.push(tokens, block(row, col), {"row": other})
    fr = mail.push(tokens, block(row, col), {"col": right})
    fl = mail.push(tokens, block(row, col), {"col": left})
    full[:, cols(row * 4 + col, WIDTH)] = tokens[...]
    kh[rows(a, ROWS)] = keys[:, cols(a)]
    acc[...] = jnp.zeros_like(acc)
    mail.settle()
    project(row, col, tokens[...])
    mail.arrive(vertical)
    gr = mail.push(block(other, col), block(other, col), {"col": right})
    gl = mail.push(block(other, col), block(other, col), {"col": left})
    key_parts = []
    for src, dst in ((keys, kh), (tokens, th), (queries, qh), (cot, ch)):
        for d in range(1, HEADS):
            to = turn(a, d, HEADS)
            k = mail.push(src.at[:, cols(to)], dst.at[rows(a, ROWS)], at_ctx(z, to))
            if dst is kh:
                key_parts.append(k)
        if dst is not kh:
            mail.keep(src.at[:, cols(a)], dst.at[rows(a, ROWS)])
    project(other, col)
    relays = []
    for r, from_left, from_right in ((row, fr, fl), (other, gr, gl)):
        mail.arrive(from_left)
        relays.append(mail.push(half(r, left, 0), half(r, left, 0), {"col": right}))
        mail.arrive(from_right)
        relays.append(mail.push(half(r, right, 1), half(r, right, 1), {"col": left}))
        project(r, left)
        project(r, right)
    for r, first in ((row, 0), (other, 2)):
        mail.arrive(relays[first])
        mail.arrive(relays[first + 1])
        project(r, across)
    feats[...] = acc[...].astype(BF)

    for d in range(1, HEADS):
        to = turn(a, d, HEADS)
        mail.push(feats.at[:, :, cols(to)], fx.at[:, rows(a, ROWS, HALO)], at_ctx(z, to))
    mail.keep(feats.at[:, :, cols(a)], fx.at[:, rows(a, ROWS, HALO)])

    n = len(mail.remote) + 4

    def edge(src, dst, k, b, device):
        return pltpu.make_async_remote_copy(
            src_ref=src,
            dst_ref=dst,
            send_sem=mail.send.at[k + 3 * b],
            recv_sem=mail.recv.at[k],
            device_id=device,
            device_id_type=MESH,
        )

    def first_rows(b):
        lanes = pl.ds(b * DH, DH)
        return (
            edge(feats.at[:, pl.ds(0, HALO), lanes], fx.at[:, pl.ds(HALO + SLAB, HALO)], n, b, at_ctx(down, b)),
            edge(cot.at[pl.ds(0, HALO), lanes], chalo, n + 1, b, at_ctx(down, b)),
        )

    def last_rows(b):
        lanes = pl.ds(b * DH, DH)
        return (edge(feats.at[:, pl.ds(ROWS - HALO, HALO), lanes], fx.at[:, pl.ds(0, HALO)], n + 2, b, at_ctx(up, b)),)

    @pl.when(a == 0)
    def _():
        for b in range(HEADS):
            for copy in first_rows(b):
                copy.start()

    @pl.when(a == HEADS - 1)
    def _():
        for b in range(HEADS):
            for copy in last_rows(b):
                copy.start()

    for k in key_parts:
        mail.arrive(k)
    gathered = slab_gather(mail, kh, kfull, z, a)
    for d in range(HEADS):
        for s in range(SLABS):
            mail.keep(
                full.at[:, cols(s * HEADS + turn(a, d, HEADS), ROWS)], pieces.at[d, :, pl.ds(s * ROWS, ROWS)]
            )
    slab_relay(mail, kfull, z, a, *gathered)
    mail.finish()
    for copy in first_rows(0) + last_rows(0):
        copy.wait_recv()

    @pl.when(a == 0)
    def _():
        for b in range(HEADS):
            for copy in first_rows(b):
                copy.wait_send()

    @pl.when(a == HEADS - 1)
    def _():
        for b in range(HEADS):
            for copy in last_rows(b):
                copy.wait_send()


def front(tokens, queries, keys, cot, weights):
    any_space, vmem = pl.BlockSpec(memory_space=pl.ANY), pl.BlockSpec(memory_space=pltpu.VMEM)
    head = shape(SLAB, DH)
    outs = [
        head,
        head,
        head,
        shape(HALO, DH),
        shape(3, EXT, DH),
        shape(SLABS * SLAB, DH),
        shape(HEADS, ROWS, SLABS * ROWS),
    ]
    remotes = 3 + 2 + 12 + 4 + 3 + 4 + 12
    return pl.pallas_call(
        front_kernel,
        out_shape=outs,
        in_specs=[vmem] * 4 + [any_space],
        out_specs=[any_space] * len(outs),
        scratch_shapes=[
            pltpu.VMEM((ROWS, 8 * WIDTH), BF),
            pltpu.VMEM(weights.shape, BF),
            pltpu.VMEM((3, ROWS, WIDTH), F32),
            pltpu.VMEM((3, ROWS, WIDTH), BF),
            pltpu.VMEM((SLAB, DH), BF),
            pltpu.SemaphoreType.DMA((remotes,)),
            pltpu.SemaphoreType.DMA((remotes,)),
            pltpu.SemaphoreType.DMA((3 + 3 + 1 + 1 + HEADS * SLABS,)),
        ],
        compiler_params=pltpu.CompilerParams(
            collective_id=0, has_side_effects=True, vmem_limit_bytes=56 << 20
        ),
    )(tokens, queries, keys, cot, weights)


def stream_kernel(mail, part, whole):
    z, a = place()
    greet([at_ctx(turn(z, 1, SLABS), a), at_ctx(turn(z, -1, SLABS), a)])
    slab_relay(mail, whole, z, a, *slab_gather(mail, part, whole, z, a))
    mail.finish()


def around(z, a):
    return [at_ctx(turn(z, d, SLABS), a) for d in range(1, SLABS)] + [
        at_ctx(z, turn(a, d, HEADS)) for d in range(1, HEADS)
    ]


def home(mail, src, dst, z, a):
    for d in range(1, HEADS):
        to = turn(a, d, HEADS)
        mail.push(src.at[rows(to, ROWS)], dst.at[:, cols(a)], at_ctx(z, to))
    mail.keep(src.at[rows(a, ROWS)], dst.at[:, cols(a)])


def values_kernel(mail, dv, dk, block, dq, dvr, dkr, block_home, dq_home):
    z, a = place()
    greet(around(z, a))
    for d in range(1, SLABS):
        to = turn(z, d, SLABS)
        mail.push(dv.at[pl.ds(pl.multiple_of(to * SLAB, 16), SLAB + HALO)], dvr.at[z], at_ctx(to, a))
    mail.keep(dv.at[pl.ds(pl.multiple_of(z * SLAB, 16), SLAB + HALO)], dvr.at[z])
    for d in range(1, SLABS):
        to = turn(z, d, SLABS)
        mail.push(dk.at[rows(to, SLAB)], dkr.at[z], at_ctx(to, a))
    mail.keep(dk.at[rows(z, SLAB)], dkr.at[z])
    home(mail, block, block_home, z, a)
    home(mail, dq, dq_home, z, a)
    mail.finish()


def finale_kernel(
    fg, sg, dk, small, part0, part1, part2, part3, weights,
    grad_input, grad_feat, dk_home, small_home,
    w, tq, tqt, fgall, fgm, wsend, zr1, zr2, tsend, xr1, xr2, yr, ysend, sgh, slots, total,
    send, recv, loc,
):
    mail = Courier(send, recv, loc)
    z, a = place()
    row, col = lax.axis_index("row"), lax.axis_index("col")
    side, core = lax.div(a, 2), lax.rem(a, 2)
    mate, far, far_mate = side * 2 + 1 - core, (1 - side) * 2 + core, (1 - side) * 2 + 1 - core
    up, down = turn(z, 1, SLABS), turn(z, -1, SLABS)
    right, left = turn(col, 1, 4), turn(col, -1, 4)
    half = ROWS // 2
    pair = 2 * ROWS

    mail.keep(fg, fgall.at[a])
    for d, part in enumerate((part0, part1, part2, part3)):
        mail.keep(part, tq.at[rows(turn(a, -d, HEADS), ROWS)])
    for j in range(3):
        mail.keep(weights.at[j], w.at[j])
    greet(around(z, a) + [{"row": 1 - row}, {"col": right}, {"col": left}])

    near_rows, far_rows = rows(side, pair), rows(1 - side, pair)
    to_mate = mail.push(fg, fgall.at[a], at_ctx(z, mate))
    first = mail.push(fg.at[:, far_rows], fgall.at[a, :, far_rows], at_ctx(z, far))
    second = mail.push(fg.at[:, near_rows], fgall.at[a, :, near_rows], at_ctx(z, far))
    small_in = [mail.push(small, slots.at[d - 1], at_ctx(turn(z, d, SLABS), a)) for d in range(1, SLABS)]
    home_sg = []
    for d in range(1, HEADS):
        to = turn(a, d, HEADS)
        home_sg.append(mail.push(sg.at[rows(to, ROWS)], sgh.at[:, cols(a)], at_ctx(z, to)))
        mail.push(dk.at[rows(to, ROWS)], dk_home.at[:, cols(a)], at_ctx(z, to))
    mail.keep(sg.at[rows(a, ROWS)], sgh.at[:, cols(a)])
    mail.keep(dk.at[rows(a, ROWS)], dk_home.at[:, cols(a)])
    mail.settle()

    for b in range(SLABS):
        tqt[pl.ds(b * ROWS, ROWS)] = tq[:, pl.ds(b * ROWS, ROWS)].T

    def weight_block(n, head, dz):
        rhs = jnp.concatenate([fgall[head, j] for j in range(3)], axis=1)
        lhs = tqt[rows(turn(z, dz, SLABS), ROWS)]
        out = jnp.dot(lhs, rhs, preferred_element_type=F32)
        for j in range(3):
            wsend[n, dz, j] = out[:, j * DH : (j + 1) * DH].astype(BF)

    def weight_first(n, head):
        weight_block(n, head, 2)
        keys = (
            mail.push(wsend.at[n, 2, :, pl.ds(0, half)], zr1.at[n, 0], at_ctx(up, a)),
            mail.push(wsend.at[n, 2, :, pl.ds(half, half)], zr1.at[n, 1], at_ctx(down, a)),
        )
        for dz in (1, 3, 0):
            weight_block(n, head, dz)
        return keys

    def weight_second(n, keys):
        top, bottom = pl.ds(0, half), pl.ds(half, half)
        mail.arrive(keys[0])
        wsend[n, 1, :, top] = (wsend[n, 1, :, top].astype(F32) + zr1[n, 0].astype(F32)).astype(BF)
        one = mail.push(wsend.at[n, 1], zr2.at[n, 0], at_ctx(up, a))
        mail.arrive(keys[1])
        wsend[n, 3, :, bottom] = (wsend[n, 3, :, bottom].astype(F32) + zr1[n, 1].astype(F32)).astype(BF)
        return one, mail.push(wsend.at[n, 3], zr2.at[n, 1], at_ctx(down, a))

    def weight_third(n, head, keys):
        for k in keys:
            mail.arrive(k)
        for j in range(3):
            grad_feat[j, :, cols(head)] = (
                wsend[n, 0, j].astype(F32) + zr2[n, 0, j].astype(F32) + zr2[n, 1, j].astype(F32)
            )

    ring = [weight_first(0, a)]
    mail.arrive(to_mate)
    ring.append(weight_first(1, mate))
    mail.arrive(first)
    relay = mail.push(fgall.at[far, :, near_rows], fgall.at[far, :, near_rows], at_ctx(z, mate))
    ring[0] = weight_second(0, ring[0])
    ring[1] = weight_second(1, ring[1])
    mail.arrive(relay)

    for j in range(3):
        for h in range(HEADS):
            fgm[j, :, pl.ds(h * DH, DH)] = fgall[h, j, rows(a, ROWS)]

    def term_block(dc):
        for r in range(2):
            columns = rows(r * 4 + turn(col, dc, 4), WIDTH)
            out = jnp.zeros((ROWS, WIDTH), F32)
            for j in range(3):
                out += lax.dot_general(
                    fgm[j], w[j, columns], (((1,), (1,)), ((), ())), preferred_element_type=F32
                )
            tsend[dc, r] = out.astype(BF)

    top, bottom = pl.ds(0, half), pl.ds(half, half)
    term_block(2)
    from_left = mail.push(tsend.at[2, :, top], xr1.at[0], {"col": right})
    from_right = mail.push(tsend.at[2, :, bottom], xr1.at[1], {"col": left})
    term_block(1)
    term_block(3)
    mail.arrive(from_left)
    tsend[1, :, top] = (tsend[1, :, top].astype(F32) + xr1[0].astype(F32)).astype(BF)
    from_left = mail.push(tsend.at[1], xr2.at[0], {"col": right})
    mail.arrive(from_right)
    tsend[3, :, bottom] = (tsend[3, :, bottom].astype(F32) + xr1[1].astype(F32)).astype(BF)
    from_right = mail.push(tsend.at[3], xr2.at[1], {"col": left})
    term_block(0)

    mail.arrive(second)
    relay = mail.push(fgall.at[far, :, far_rows], fgall.at[far, :, far_rows], at_ctx(z, mate))
    ring.append(weight_first(2, far))
    mail.arrive(relay)
    ring.append(weight_first(3, far_mate))
    ring[2] = weight_second(2, ring[2])
    ring[3] = weight_second(3, ring[3])

    for k in small_in:
        mail.arrive(k)
    total[...] = (small_sum(small, slots)).astype(BF)
    for d in range(1, HEADS):
        mail.push(total, small_home.at[:, cols(a)], at_ctx(z, turn(a, d, HEADS)))
    mail.keep(total, small_home.at[:, cols(a)])

    mail.arrive(from_left)
    mail.arrive(from_right)

    def term_sum(r):
        return tsend[0, r].astype(F32) + xr2[0, r].astype(F32) + xr2[1, r].astype(F32)

    ysend[...] = term_sum(1 - row).astype(BF)
    across = mail.push(ysend, yr, {"row": 1 - row})
    weight_third(0, a, ring[0])
    weight_third(1, mate, ring[1])
    for k in home_sg:
        mail.arrive(k)
    mail.arrive(across)
    grad_input[...] = (sgh[...].astype(F32) + term_sum(row) + yr[...].astype(F32)).astype(BF)
    weight_third(2, far, ring[2])
    weight_third(3, far_mate, ring[3])
    mail.finish()


def small_sum(small, slots):
    return small[...].astype(F32) + sum(slots[d].astype(F32) for d in range(SLABS - 1))


def finale(fg, sg, dk, small, parts, weights):
    lines = small.shape[0]
    any_space, vmem = pl.BlockSpec(memory_space=pl.ANY), pl.BlockSpec(memory_space=pltpu.VMEM)
    remotes = 3 + 3 + 6 + 16 + 2 + 4 + 3 + 1
    return pl.pallas_call(
        finale_kernel,
        out_shape=[
            shape(ROWS, WIDTH),
            shape(3, ROWS, WIDTH, kind=F32),
            shape(ROWS, WIDTH),
            shape(lines, WIDTH),
        ],
        in_specs=[any_space, any_space, any_space, vmem] + [any_space] * 5,
        out_specs=[vmem, vmem, any_space, any_space],
        scratch_shapes=[
            pltpu.VMEM(weights.shape, BF),
            pltpu.VMEM((SLAB, SLABS * ROWS), BF),
            pltpu.VMEM((SLABS * ROWS, SLAB), BF),
            pltpu.VMEM((HEADS, 3, SLAB, DH), BF),
            pltpu.VMEM((3, ROWS, WIDTH), BF),
            pltpu.VMEM((HEADS, SLABS, 3, ROWS, DH), BF),
            pltpu.VMEM((HEADS, 2, 3, ROWS // 2, DH), BF),
            pltpu.VMEM((HEADS, 2, 3, ROWS, DH), BF),
            pltpu.VMEM((4, 2, ROWS, WIDTH), BF),
            pltpu.VMEM((2, 2, ROWS // 2, WIDTH), BF),
            pltpu.VMEM((2, 2, ROWS, WIDTH), BF),
            pltpu.VMEM((ROWS, WIDTH), BF),
            pltpu.VMEM((ROWS, WIDTH), BF),
            pltpu.VMEM((ROWS, WIDTH), BF),
            pltpu.VMEM((SLABS - 1, lines, DH), BF),
            pltpu.VMEM((lines, DH), BF),
            pltpu.SemaphoreType.DMA((remotes,)),
            pltpu.SemaphoreType.DMA((remotes,)),
            pltpu.SemaphoreType.DMA((11,)),
        ],
        compiler_params=pltpu.CompilerParams(
            collective_id=5, has_side_effects=True, vmem_limit_bytes=56 << 20
        ),
    )(fg, sg, dk, small, *parts, weights)


def compute(body, outs, scratch, *ins, vmem=56 << 20):
    z, a = place()
    return pl.pallas_call(
        body,
        out_shape=outs,
        in_specs=[pl.BlockSpec(memory_space=pltpu.SMEM)] + [pl.BlockSpec(memory_space=pltpu.VMEM)] * len(ins),
        out_specs=[pl.BlockSpec(memory_space=pltpu.VMEM)] * len(outs),
        scratch_shapes=scratch,
        compiler_params=pltpu.CompilerParams(vmem_limit_bytes=vmem),
    )(jnp.stack([z, a]).astype(jnp.int32), *ins)


GROUP = 40


def spread_taps(spread, taps, a):
    for i in range(MRLEN):
        spread[i] = jnp.broadcast_to(taps[pl.ds(i, 1), cols(a)], (8, DH))


def hyena_body(where, fx, short, mr, tok, stream, qm, km, vm, lm, pr, feat, spread):
    z, a = where[0], where[1]
    spread_taps(spread, mr, a)
    keep_head = (z > 0).astype(F32)
    keep_tail = (z < SLABS - 1).astype(F32)
    for j in range(3):
        feat[j, pl.ds(0, HALO)] = fx[j, pl.ds(0, HALO)].astype(F32) * keep_head
        feat[j, pl.ds(HALO, SLAB)] = fx[j, pl.ds(HALO, SLAB)].astype(F32)
        feat[j, pl.ds(HALO + SLAB, HALO)] = fx[j, pl.ds(HALO + SLAB, HALO)].astype(F32) * keep_tail

    taps = [[short[j, pl.ds(s, 1), cols(a)] for s in range(SHORT)] for j in range(3)]

    def mixed(j, base, count):
        total = taps[j][0] * feat[j, pl.ds(base, count)]
        for s in range(1, SHORT):
            total += taps[j][s] * feat[j, pl.ds(base - s, count)]
        return total

    pr[pl.ds(0, 16)] = jnp.zeros((16, DH), F32)

    def head_step(g, carry):
        base = pl.multiple_of(16 + g * 16, 16)
        pr[pl.ds(base, 16)] = (mixed(1, base, 16) * mixed(2, base, 16)).astype(BF).astype(F32)
        return carry

    lax.fori_loop(0, (HALO - 16) // 16, head_step, 0)

    def mix_step(g, carry):
        base = pl.multiple_of(HALO + g * GROUP, 8)
        local = pl.multiple_of(g * GROUP, 8)
        key, value = mixed(1, base, GROUP), mixed(2, base, GROUP)
        km[pl.ds(local, GROUP)] = key
        vm[pl.ds(local, GROUP)] = value
        qm[pl.ds(local, GROUP)] = mixed(0, base, GROUP)
        pr[pl.ds(base, GROUP)] = (key * value).astype(BF).astype(F32)
        return carry

    lax.fori_loop(0, (SLAB + TAIL) // GROUP, mix_step, 0)

    def tail_step(g, carry):
        local = pl.multiple_of(SLAB + TAIL + g * 16, 16)
        qm[pl.ds(local, 16)] = mixed(0, local + HALO, 16)
        return carry

    lax.fori_loop(0, (HALO - TAIL) // 16, tail_step, 0)

    def long_step(g, carry):
        base = pl.multiple_of(HALO + g * GROUP, 8)
        local = pl.multiple_of(g * GROUP, 8)
        total = [jnp.zeros((8, DH), F32) for _ in range(GROUP // 8)]
        for i in range(MRLEN):
            tap = spread[i]
            for n in range(GROUP // 8):
                total[n] += tap * pr[pl.ds(base + (n * 8 - i), 8)]
        for n in range(GROUP // 8):
            lm[pl.ds(local + n * 8, 8)] = total[n]
        return carry

    lax.fori_loop(0, (SLAB + TAIL) // GROUP, long_step, 0)
    own = pl.ds(0, SLAB)
    stream[...] = (tok[...].astype(F32) + qm[own] * lm[own]).astype(BF)


def attention_body(where, q, k, v, ct, own_stream, block, dq, dk, dv, st, pt, kt, vt, dka, dva):
    z = where[0]
    scale = DH ** -0.5
    gain = scale * 1.4426950408889634
    dka[...] = jnp.zeros_like(dka)
    dva[...] = jnp.zeros_like(dva)
    kt[...] = k[...].T
    vt[...] = v[...].T

    def dot(x, y):
        return jnp.dot(x, y, preferred_element_type=F32)

    def dot_t(x, y):
        return lax.dot_general(x, y, (((1,), (1,)), ((), ())), preferred_element_type=F32)

    for i in range(HEADS):
        span = ROWS * (i + 1)
        here = pl.ds(i * ROWS, ROWS)
        qb, cb = q[here], ct[here]
        own = pl.ds(pl.multiple_of(z * SLAB, SLAB), span)
        own_lanes = pl.ds(pl.multiple_of(z * SLAB, SLAB), span)
        scores = dot_t(k[own], qb)
        after = lax.broadcasted_iota(jnp.int32, (ROWS, ROWS), 0) > lax.broadcasted_iota(jnp.int32, (ROWS, ROWS), 1)
        corner = jnp.where(after, -1e30, scores[span - ROWS :])
        top = jnp.max(corner, axis=0, keepdims=True)
        if i:
            top = jnp.maximum(top, jnp.max(scores[: span - ROWS], axis=0, keepdims=True))
            st[pl.ds(0, span - ROWS)] = scores[: span - ROWS]
        st[pl.ds(span - ROWS, ROWS)] = corner

        def score_step(s, top):
            past = dot_t(k[pl.ds(pl.multiple_of(s * SLAB, SLAB), SLAB)], qb)
            st[pl.ds(pl.multiple_of((s + 1) * SLAB, SLAB), SLAB)] = past
            return jnp.maximum(top, jnp.max(past, axis=0, keepdims=True))

        top = lax.fori_loop(0, z, score_step, top) * gain

        def weigh(slots, lanes, total, out):
            p = jnp.exp2(st[slots] * gain - top)
            total += jnp.sum(p, axis=0, keepdims=True)
            p = p.astype(BF)
            pt[slots] = p
            return total, out + dot(vt[:, lanes], p)

        carry = weigh(pl.ds(0, span), own_lanes, jnp.zeros((1, ROWS), F32), jnp.zeros((DH, ROWS), F32))

        def weigh_step(s, carry):
            return weigh(
                pl.ds(pl.multiple_of((s + 1) * SLAB, SLAB), SLAB), pl.ds(pl.multiple_of(s * SLAB, SLAB), SLAB), *carry
            )

        total, out = lax.fori_loop(0, z, weigh_step, carry)
        inverse = 1.0 / total
        out = out * inverse
        block[here] = (own_stream[here].astype(F32) + out.T).astype(BF)
        ctt = (cb.astype(F32).T * inverse).astype(BF)
        delta = jnp.sum(ctt.astype(F32) * out, axis=0, keepdims=True)
        cs = ctt.T

        def grads(slots, lanes, dqt):
            p = pt[slots]
            dva[lanes] += dot(p, cs)
            dp = dot(v[lanes], ctt)
            ds = (p.astype(F32) * (dp - delta)).astype(BF)
            dka[lanes] += dot(ds, qb)
            return dqt + dot(kt[:, lanes], ds)

        dqt = grads(pl.ds(0, span), own, jnp.zeros((DH, ROWS), F32))

        def grad_step(s, dqt):
            return grads(
                pl.ds(pl.multiple_of((s + 1) * SLAB, SLAB), SLAB), pl.ds(pl.multiple_of(s * SLAB, SLAB), SLAB), dqt
            )

        dqt = lax.fori_loop(0, z, grad_step, dqt)
        dq[here] = (dqt.T * scale).astype(BF)
    dk[...] = (dka[...] * scale).astype(BF)
    whole = SLABS * SLAB
    dv[pl.ds(0, whole)] = dva[...].astype(BF)
    dv[pl.ds(whole, HALO)] = jnp.zeros((HALO, DH), BF)


def back_body(where, dvr, dkr, ch, chalo, fx, short, mr, qm, km, vm, lm, pr, sg, fg, dk, small, mg, stack, feat, spread):
    z, a = where[0], where[1]
    spread_taps(spread, mr, a)
    keep_head = (z > 0).astype(F32)
    keep_tail = (z < SLABS - 1).astype(F32)
    own, halo = pl.ds(0, SLAB), pl.ds(SLAB, HALO)

    def value_sum(part):
        return sum(dvr[s, part].astype(F32) for s in range(SLABS))

    dk[...] = sum(dkr[s].astype(F32) for s in range(SLABS)).astype(BF)
    grad = (ch[...].astype(F32) + value_sum(own)).astype(BF)
    sg[...] = grad
    mg[own] = (grad.astype(F32) * qm[own]).astype(BF).astype(F32)
    grad_halo = (chalo[...].astype(F32) + value_sum(halo)).astype(BF).astype(F32) * keep_tail
    mg[halo] = (grad_halo * qm[halo]).astype(BF).astype(F32)
    stack[0, own] = grad.astype(F32) * lm[own]
    stack[0, pl.ds(SLAB, TAIL)] = grad_halo[:TAIL] * lm[pl.ds(SLAB, TAIL)]
    for j in range(3):
        feat[j, pl.ds(0, 16)] = fx[j, pl.ds(HALO - 16, 16)].astype(F32) * keep_head
        feat[j, pl.ds(16, SLAB)] = fx[j, pl.ds(HALO, SLAB)].astype(F32)

    def long_step(g, carry):
        local = pl.multiple_of(g * GROUP, 8)
        total = [jnp.zeros((8, DH), F32) for _ in range(GROUP // 8)]
        for i in range(MRLEN):
            tap = spread[i]
            for n in range(GROUP // 8):
                total[n] += tap * mg[pl.ds(local + (n * 8 + i), 8)]
        for n in range(GROUP // 8):
            part = pl.ds(local + n * 8, 8)
            stack[1, part] = total[n] * vm[part]
            stack[2, part] = total[n] * km[part]
        return carry

    lax.fori_loop(0, (SLAB + TAIL) // GROUP, long_step, 0)

    for j in range(3):
        taps = [short[j, pl.ds(s, 1), cols(a)] for s in range(SHORT)]

        def short_step(g, sums):
            base = pl.multiple_of(g * 32, 32)
            total = taps[0] * stack[j, pl.ds(base, 32)]
            for s in range(1, SHORT):
                total += taps[s] * stack[j, pl.ds(base + s, 32)]
            fg[j, pl.ds(base, 32)] = total.astype(BF)
            out = []
            for s in range(SHORT):
                term = stack[j, pl.ds(base, 32)] * feat[j, pl.ds(base + 16 - s, 32)]
                out.append(sums[s] + (term[0:8] + term[8:16] + term[16:24] + term[24:32]))
            return tuple(out)

        sums = lax.fori_loop(0, SLAB // 32, short_step, tuple(jnp.zeros((8, DH), F32) for _ in range(SHORT)))
        lines = [jnp.sum(t, axis=0, keepdims=True) for t in sums]
        small[pl.ds(MRLEN + 16 * j, 16)] = jnp.concatenate(lines + [jnp.zeros((16 - SHORT, DH), F32)], axis=0).astype(BF)

    def tap_step(c, carry):
        first = c * 16

        def row_step(g, sums):
            base = pl.multiple_of(g * 16, 16)
            out = list(sums)
            for n in range(2):
                line = mg[pl.ds(base + n * 8, 8)]
                for s in range(16):
                    out[s] += line * pr[pl.ds(base + (HALO + n * 8 - s) - first, 8)]
            return tuple(out)

        sums = lax.fori_loop(0, SLAB // 16, row_step, tuple(jnp.zeros((8, DH), F32) for _ in range(16)))
        lines = [jnp.sum(t, axis=0, keepdims=True) for t in sums]
        small[pl.ds(pl.multiple_of(first, 16), 16)] = jnp.concatenate(lines, axis=0).astype(BF)
        return carry

    lax.fori_loop(0, MRLEN // 16, tap_step, 0)


def local(tokens, w_feat, short_filter, mr_filter, queries, key_rows, cotangent):
    weights = w_feat.transpose(1, 0, 2)
    short_taps = short_filter.transpose(1, 0, 2)
    head = shape(SLAB, DH)
    th, qh, ch, chalo, fx, kfull, pieces = front(tokens, queries, key_rows, cotangent, weights)
    token_parts = [pieces[0]]
    for d in range(1, HEADS):
        route = [(s * HEADS + a, s * HEADS + (a + d) % HEADS) for s in range(SLABS) for a in range(HEADS)]
        token_parts.append(lax.ppermute(pieces[d], "ctx", route))
    filters = [pltpu.VMEM((MRLEN, 8, DH), F32)]
    stream, qm, km, vm, lm, pr = compute(
        hyena_body,
        [
            head,
            shape(SLAB + HALO, DH, kind=F32),
            shape(SLAB + TAIL, DH, kind=F32),
            shape(SLAB + TAIL, DH, kind=F32),
            shape(SLAB + TAIL, DH, kind=F32),
            shape(HALO + SLAB + TAIL, DH, kind=F32),
        ],
        [pltpu.VMEM((3, EXT, DH), F32)] + filters,
        fx,
        short_taps,
        mr_filter,
        th,
    )
    (vfull,) = exchange(stream_kernel, 2, [shape(SLABS * SLAB, DH)], 4, 1, stream)
    whole = SLABS * SLAB
    block, dq, dk, dv = compute(
        attention_body,
        [head, head, shape(whole, DH), shape(whole + HALO, DH)],
        [
            pltpu.VMEM((whole + SLAB, ROWS), F32),
            pltpu.VMEM((whole + SLAB, ROWS), BF),
            pltpu.VMEM((DH, whole), BF),
            pltpu.VMEM((DH, whole), BF),
            pltpu.VMEM((whole, DH), F32),
            pltpu.VMEM((whole, DH), F32),
        ],
        qh,
        kfull,
        vfull,
        ch,
        stream,
    )
    mine = shape(ROWS, WIDTH)
    dvr, dkr, block_out, grad_queries = exchange(
        values_kernel,
        3,
        [shape(SLABS, SLAB + HALO, DH), shape(SLABS, SLAB, DH), mine, mine],
        12,
        4,
        dv,
        dk,
        block,
        dq,
    )
    sg, fg, dk_sum, small = compute(
        back_body,
        [head, shape(3, SLAB, DH), head, shape(MRLEN + 3 * 16, DH)],
        [
            pltpu.VMEM((SLAB + HALO, DH), F32),
            pltpu.VMEM((3, SLAB + TAIL, DH), F32),
            pltpu.VMEM((3, SLAB + 16, DH), F32),
        ]
        + filters,
        dvr,
        dkr,
        ch,
        chalo,
        fx,
        short_taps,
        mr_filter,
        qm,
        km,
        vm,
        lm,
        pr,
    )
    grad_input, grad_feat, grad_keys, small_home = finale(fg, sg, dk_sum, small, token_parts, weights)
    sums = small_home.astype(F32)
    grad_short = sums[MRLEN:].reshape(3, 16, WIDTH)[:, :SHORT].transpose(1, 0, 2)
    grad_feat = grad_feat.transpose(1, 0, 2)
    grad_mr = sums[:MRLEN]
    return (block_out, grad_input, grad_feat, grad_short, grad_mr, grad_queries, grad_keys)


def solution(mesh):
    placed = (
        P("ctx", ("row", "col")),
        P(None, None, ("row", "col")),
        P(None, None, ("row", "col")),
        P(None, ("row", "col")),
        P("ctx", ("row", "col")),
        P("ctx", ("row", "col")),
        P("ctx", ("row", "col")),
    )
    return jax.shard_map(
        local,
        mesh=mesh,
        in_specs=placed,
        out_specs=(
            P("ctx", ("row", "col")),
            P("ctx", ("row", "col")),
            P("ctx", None, ("row", "col")),
            P(None, None, ("row", "col")),
            P(None, ("row", "col")),
            P("ctx", ("row", "col")),
            P("ctx", ("row", "col")),
        ),
        check_vma=False,
    )
```

```python
import functools

import jax
import jax.numpy as jnp
from jax import lax
from jax.experimental import pallas as pl
from jax.experimental.pallas import tpu as pltpu
from jax.sharding import PartitionSpec as P

DH = 128
SHORT = 7
MRLEN = 128
HALO = 144
TAIL = 16
ROWS = 256
HEADS = 4
SLABS = 4
SLAB = ROWS * HEADS
EXT = HALO + SLAB + HALO
WIDTH = HEADS * DH
MESH = pl.DeviceIdType.MESH
BF = jnp.bfloat16
F32 = jnp.float32


def place():
    ctx = lax.axis_index("ctx")
    return lax.div(ctx, HEADS), lax.rem(ctx, HEADS)


def turn(index, step, size):
    return lax.rem(index + (step + size), size)


def at_ctx(z, a):
    return {"ctx": z * HEADS + a}


def cols(index, width=DH):
    return pl.ds(pl.multiple_of(index * width, width), width)


def rows(index, height, offset=0):
    return pl.ds(pl.multiple_of(index * height + offset, 16), height)


def greet(devices):
    barrier = pltpu.get_barrier_semaphore()
    for device in devices:
        pl.semaphore_signal(barrier, inc=1, device_id=device, device_id_type=MESH)
    pl.semaphore_wait(barrier, len(devices))


class Courier:
    def __init__(self, send, recv, local):
        self.send, self.recv, self.local = send, recv, local
        self.remote, self.here = [], []
        self.arrived = set()
        self.settled = 0

    def push(self, src, dst, device):
        k = len(self.remote)
        copy = pltpu.make_async_remote_copy(
            src_ref=src,
            dst_ref=dst,
            send_sem=self.send.at[k],
            recv_sem=self.recv.at[k],
            device_id=device,
            device_id_type=MESH,
        )
        copy.start()
        self.remote.append(copy)
        return k

    def keep(self, src, dst):
        copy = pltpu.make_async_copy(src, dst, self.local.at[len(self.here)])
        copy.start()
        self.here.append(copy)

    def arrive(self, k):
        if k not in self.arrived:
            self.arrived.add(k)
            self.remote[k].wait_recv()

    def finish(self):
        for k in range(len(self.remote)):
            self.arrive(k)
        for copy in self.remote:
            copy.wait_send()
        self.settle()

    def settle(self):
        for copy in self.here[self.settled :]:
            copy.wait()
        self.settled = len(self.here)


def shape(*dims, kind=BF):
    return jax.ShapeDtypeStruct(dims, kind)


def slab_gather(mail, part, whole, z, a):
    up, down = turn(z, 1, SLABS), turn(z, -1, SLABS)
    mine = whole.at[rows(z, SLAB)]
    mail.keep(part, mine)
    return mail.push(part, mine, at_ctx(up, a)), mail.push(part, mine, at_ctx(down, a))


def slab_relay(mail, whole, z, a, from_down, from_up):
    up, down = turn(z, 1, SLABS), turn(z, -1, SLABS)
    half = SLAB // 2
    mail.arrive(from_down)
    lower = whole.at[pl.ds(pl.multiple_of(down * SLAB, 16), half)]
    mail.push(lower, lower, at_ctx(up, a))
    mail.arrive(from_up)
    upper = whole.at[pl.ds(pl.multiple_of(up * SLAB + half, 16), half)]
    mail.push(upper, upper, at_ctx(down, a))


def front_kernel(
    tokens, queries, keys, cot, weights,
    th, qh, ch, chalo, fx, kfull, pieces,
    full, w, acc, feats, kh, send, recv, loc,
):
    mail = Courier(send, recv, loc)
    z, a = place()
    row, col = lax.axis_index("row"), lax.axis_index("col")
    other = 1 - row
    right, left, across = turn(col, 1, 4), turn(col, -1, 4), turn(col, 2, 4)
    up, down = turn(z, 1, SLABS), turn(z, -1, SLABS)
    for j in range(3):
        mail.keep(weights.at[j], w.at[j])
    greet(
        [{"row": other}, {"col": right}, {"col": left}]
        + [at_ctx(z, turn(a, d, HEADS)) for d in range(1, HEADS)]
        + [at_ctx(s, b) for s in (up, down) for b in range(HEADS)]
    )

    def block(r, c):
        return full.at[:, cols(r * 4 + c, WIDTH)]

    def half(r, c, h):
        return full.at[pl.ds(h * (ROWS // 2), ROWS // 2), cols(r * 4 + c, WIDTH)]

    def project(r, c, lhs=None):
        lhs = full[:, cols(r * 4 + c, WIDTH)] if lhs is None else lhs
        for j in range(3):
            acc[j] += jnp.dot(lhs, w[j, rows(r * 4 + c, WIDTH)], preferred_element_type=F32)

    vertical = mail.push(tokens, block(row, col), {"row": other})
    fr = mail.push(tokens, block(row, col), {"col": right})
    fl = mail.push(tokens, block(row, col), {"col": left})
    full[:, cols(row * 4 + col, WIDTH)] = tokens[...]
    kh[rows(a, ROWS)] = keys[:, cols(a)]
    acc[...] = jnp.zeros_like(acc)
    mail.settle()
    project(row, col, tokens[...])
    mail.arrive(vertical)
    gr = mail.push(block(other, col), block(other, col), {"col": right})
    gl = mail.push(block(other, col), block(other, col), {"col": left})
    key_parts = []
    for src, dst in ((keys, kh), (tokens, th), (queries, qh), (cot, ch)):
        for d in range(1, HEADS):
            to = turn(a, d, HEADS)
            k = mail.push(src.at[:, cols(to)], dst.at[rows(a, ROWS)], at_ctx(z, to))
            if dst is kh:
                key_parts.append(k)
        if dst is not kh:
            mail.keep(src.at[:, cols(a)], dst.at[rows(a, ROWS)])
    project(other, col)
    relays = []
    for r, from_left, from_right in ((row, fr, fl), (other, gr, gl)):
        mail.arrive(from_left)
        relays.append(mail.push(half(r, left, 0), half(r, left, 0), {"col": right}))
        mail.arrive(from_right)
        relays.append(mail.push(half(r, right, 1), half(r, right, 1), {"col": left}))
        project(r, left)
        project(r, right)
    for r, first in ((row, 0), (other, 2)):
        mail.arrive(relays[first])
        mail.arrive(relays[first + 1])
        project(r, across)
    feats[...] = acc[...].astype(BF)

    for d in range(1, HEADS):
        to = turn(a, d, HEADS)
        mail.push(feats.at[:, :, cols(to)], fx.at[:, rows(a, ROWS, HALO)], at_ctx(z, to))
    mail.keep(feats.at[:, :, cols(a)], fx.at[:, rows(a, ROWS, HALO)])

    n = len(mail.remote) + 4

    def edge(src, dst, k, b, device):
        return pltpu.make_async_remote_copy(
            src_ref=src,
            dst_ref=dst,
            send_sem=mail.send.at[k + 3 * b],
            recv_sem=mail.recv.at[k],
            device_id=device,
            device_id_type=MESH,
        )

    def first_rows(b):
        lanes = pl.ds(b * DH, DH)
        return (
            edge(feats.at[:, pl.ds(0, HALO), lanes], fx.at[:, pl.ds(HALO + SLAB, HALO)], n, b, at_ctx(down, b)),
            edge(cot.at[pl.ds(0, HALO), lanes], chalo, n + 1, b, at_ctx(down, b)),
        )

    def last_rows(b):
        lanes = pl.ds(b * DH, DH)
        return (edge(feats.at[:, pl.ds(ROWS - HALO, HALO), lanes], fx.at[:, pl.ds(0, HALO)], n + 2, b, at_ctx(up, b)),)

    @pl.when(a == 0)
    def _():
        for b in range(HEADS):
            for copy in first_rows(b):
                copy.start()

    @pl.when(a == HEADS - 1)
    def _():
        for b in range(HEADS):
            for copy in last_rows(b):
                copy.start()

    for k in key_parts:
        mail.arrive(k)
    gathered = slab_gather(mail, kh, kfull, z, a)
    for d in range(HEADS):
        for s in range(SLABS):
            mail.keep(
                full.at[:, cols(s * HEADS + turn(a, d, HEADS), ROWS)], pieces.at[d, :, pl.ds(s * ROWS, ROWS)]
            )
    slab_relay(mail, kfull, z, a, *gathered)
    mail.finish()
    for copy in first_rows(0) + last_rows(0):
        copy.wait_recv()

    @pl.when(a == 0)
    def _():
        for b in range(HEADS):
            for copy in first_rows(b):
                copy.wait_send()

    @pl.when(a == HEADS - 1)
    def _():
        for b in range(HEADS):
            for copy in last_rows(b):
                copy.wait_send()


def front(tokens, queries, keys, cot, weights):
    any_space, vmem = pl.BlockSpec(memory_space=pl.ANY), pl.BlockSpec(memory_space=pltpu.VMEM)
    head = shape(SLAB, DH)
    outs = [
        head,
        head,
        head,
        shape(HALO, DH),
        shape(3, EXT, DH),
        shape(SLABS * SLAB, DH),
        shape(HEADS, ROWS, SLABS * ROWS),
    ]
    remotes = 3 + 2 + 12 + 4 + 3 + 4 + 12
    return pl.pallas_call(
        front_kernel,
        out_shape=outs,
        in_specs=[vmem] * 4 + [any_space],
        out_specs=[any_space] * len(outs),
        scratch_shapes=[
            pltpu.VMEM((ROWS, 8 * WIDTH), BF),
            pltpu.VMEM(weights.shape, BF),
            pltpu.VMEM((3, ROWS, WIDTH), F32),
            pltpu.VMEM((3, ROWS, WIDTH), BF),
            pltpu.VMEM((SLAB, DH), BF),
            pltpu.SemaphoreType.DMA((remotes,)),
            pltpu.SemaphoreType.DMA((remotes,)),
            pltpu.SemaphoreType.DMA((3 + 3 + 1 + 1 + HEADS * SLABS,)),
        ],
        compiler_params=pltpu.CompilerParams(
            collective_id=0, has_side_effects=True, vmem_limit_bytes=56 << 20
        ),
    )(tokens, queries, keys, cot, weights)


def around(z, a):
    return [at_ctx(turn(z, d, SLABS), a) for d in range(1, SLABS)] + [
        at_ctx(z, turn(a, d, HEADS)) for d in range(1, HEADS)
    ]


def home(mail, src, dst, z, a):
    for d in range(1, HEADS):
        to = turn(a, d, HEADS)
        mail.push(src.at[rows(to, ROWS)], dst.at[:, cols(a)], at_ctx(z, to))
    mail.keep(src.at[rows(a, ROWS)], dst.at[:, cols(a)])


CHUNK = 512


def dot(x, y):
    return jnp.dot(x, y, preferred_element_type=F32)


def dot_t(x, y):
    return lax.dot_general(x, y, (((1,), (1,)), ((), ())), preferred_element_type=F32)


def attention_kernel(
    q, k, stream, ct,
    block_home, dq_home, dv, dk,
    v, kt, vt, st, pt, tops, outs, ctt, cs, delta, block, dq, dqt, dva, dka, edge, dv_out, dk_out, dv_in, dk_in,
    dv_send, dv_recv, dk_send, dk_recv, send, recv, loc,
):
    mail = Courier(send, recv, loc)
    z, a = place()
    scale = DH ** -0.5
    gain = scale * 1.4426950408889634
    greet(around(z, a))
    mine = rows(z, SLAB)
    up, down = at_ctx(turn(z, 1, SLABS), a), at_ctx(turn(z, -1, SLABS), a)
    from_down = mail.push(stream, v.at[mine], up)
    from_up = mail.push(stream, v.at[mine], down)
    v[mine] = stream[...]

    def lanes_of(i):
        return pl.ds(i * ROWS, ROWS)

    def slots(c):
        return pl.ds(pl.multiple_of(SLAB + c * CHUNK, CHUNK), CHUNK)

    def keys_of(c):
        return pl.ds(pl.multiple_of(c * CHUNK, CHUNK), CHUNK)

    def turn_keys(s, carry):
        kt[:, cols(s, SLAB)] = k[rows(s, SLAB)].T
        return carry

    lax.fori_loop(0, z + 1, turn_keys, 0)
    after = lax.broadcasted_iota(jnp.int32, (ROWS, ROWS), 0) > lax.broadcasted_iota(jnp.int32, (ROWS, ROWS), 1)
    for i in range(HEADS):
        span = ROWS * (i + 1)
        scores = dot_t(k[pl.ds(pl.multiple_of(z * SLAB, SLAB), span)], q[lanes_of(i)])
        corner = jnp.where(after, -1e30, scores[span - ROWS :])
        top = jnp.max(corner, axis=0, keepdims=True)
        if i:
            top = jnp.maximum(top, jnp.max(scores[: span - ROWS], axis=0, keepdims=True))
            st[pl.ds(0, span - ROWS), lanes_of(i)] = scores[: span - ROWS]
        st[pl.ds(span - ROWS, ROWS), lanes_of(i)] = corner
        tops[:, lanes_of(i)] = top

    def score_step(c, top):
        past = dot_t(k[keys_of(c)], q[...])
        st[slots(c)] = past
        return jnp.maximum(top, jnp.max(past, axis=0, keepdims=True))

    half = SLAB // 2
    mail.arrive(from_down)
    lower = v.at[pl.ds(pl.multiple_of(turn(z, -1, SLABS) * SLAB, SLAB), half)]
    mail.push(lower, lower, up)
    mail.arrive(from_up)
    upper = v.at[pl.ds(pl.multiple_of(turn(z, 1, SLABS) * SLAB + half, half), half)]
    mail.push(upper, upper, down)

    top = lax.fori_loop(0, z * (SLAB // CHUNK), score_step, tops[...]) * gain
    mail.arrive(2)
    mail.arrive(3)

    def turn_values(s, carry):
        vt[:, cols(s, SLAB)] = v[rows(s, SLAB)].T
        return carry

    lax.fori_loop(0, z + 1, turn_values, 0)

    for i in range(HEADS):
        span = ROWS * (i + 1)
        p = jnp.exp2(st[pl.ds(0, span), lanes_of(i)] * gain - top[:, i * ROWS : (i + 1) * ROWS])
        tops[:, lanes_of(i)] = jnp.sum(p, axis=0, keepdims=True)
        p = p.astype(BF)
        pt[pl.ds(0, span), lanes_of(i)] = p
        outs[:, lanes_of(i)] = dot(vt[:, pl.ds(pl.multiple_of(z * SLAB, SLAB), span)], p)

    def weigh_step(c, total):
        p = jnp.exp2(st[slots(c)] * gain - top)
        total += jnp.sum(p, axis=0, keepdims=True)
        p = p.astype(BF)
        pt[slots(c)] = p
        outs[...] += dot(vt[:, keys_of(c)], p)
        return total

    inverse = 1.0 / lax.fori_loop(0, z * (SLAB // CHUNK), weigh_step, tops[...])
    out = outs[...] * inverse
    block[...] = (stream[...].astype(F32) + out.T).astype(BF)
    ctt[...] = (ct[...].astype(F32).T * inverse).astype(BF)
    cs[...] = ctt[...].T
    delta[...] = jnp.sum(ctt[...].astype(F32) * out, axis=0, keepdims=True)
    home(mail, block, block_home, z, a)

    for i in reversed(range(HEADS)):
        span = ROWS * (i + 1)
        here = pl.ds(pl.multiple_of(z * SLAB, SLAB), span)
        p = pt[pl.ds(0, span), lanes_of(i)]
        value_part = dot(p, cs[lanes_of(i)])
        dp = dot(v[here], ctt[:, lanes_of(i)])
        ds = (p.astype(F32) * (dp - delta[:, lanes_of(i)])).astype(BF)
        key_part = dot(ds, q[lanes_of(i)])
        dqt[:, lanes_of(i)] = dot(kt[:, here], ds)
        if i == HEADS - 1:
            dva[...] = value_part
            dka[...] = key_part
        else:
            dva[pl.ds(0, span)] += value_part
            dka[pl.ds(0, span)] += key_part
    edge[...] = dva[pl.ds(0, HALO)].astype(BF)

    def parcels(d, to):
        return (
            pltpu.make_async_remote_copy(
                src_ref=dv_out.at[d - 1],
                dst_ref=dv_in.at[d - 1],
                send_sem=dv_send.at[d - 1],
                recv_sem=dv_recv.at[d - 1],
                device_id=at_ctx(to, a),
                device_id_type=MESH,
            ),
            pltpu.make_async_remote_copy(
                src_ref=dk_out.at[d - 1],
                dst_ref=dk_in.at[d - 1],
                send_sem=dk_send.at[d - 1],
                recv_sem=dk_recv.at[d - 1],
                device_id=at_ctx(to, a),
                device_id_type=MESH,
            ),
        )

    def grad_step(d, carry):
        s = z - d
        dv_out[d - 1, pl.ds(SLAB, HALO)] = edge[...]
        for n in range(SLAB // CHUNK):
            c = s * (SLAB // CHUNK) + n
            p = pt[slots(c)]
            value_part = dot(p, cs[...]).astype(BF)
            dv_out[d - 1, pl.ds(n * CHUNK, CHUNK)] = value_part
            if n == 0:
                edge[...] = value_part[:HALO]
            dp = dot(v[keys_of(c)], ctt[...])
            ds = (p.astype(F32) * (dp - delta[...])).astype(BF)
            dk_out[d - 1, pl.ds(n * CHUNK, CHUNK)] = (dot(ds, q[...]) * scale).astype(BF)
            dqt[...] += dot(kt[:, keys_of(c)], ds)
        for copy in parcels(d, s):
            copy.start()
        return carry

    lax.fori_loop(1, z + 1, grad_step, 0)
    dq[...] = (dqt[...].T * scale).astype(BF)
    home(mail, dq, dq_home, z, a)

    dv[pl.ds(0, SLAB)] = dva[...]
    dv[pl.ds(SLAB, HALO)] = jnp.zeros((HALO, DH), F32)
    dka[...] = dka[...] * scale

    def value_step(d, carry):
        parcels(d, turn(z, d, SLABS))[0].wait_recv()
        dv[...] += dv_in[d - 1].astype(F32)
        return carry

    def key_step(d, carry):
        parcels(d, turn(z, d, SLABS))[1].wait_recv()
        dka[...] += dk_in[d - 1].astype(F32)
        return carry

    lax.fori_loop(1, SLABS - z, value_step, 0)
    lax.fori_loop(1, SLABS - z, key_step, 0)
    dk[...] = dka[...].astype(BF)
    mail.finish()

    def sent_step(d, carry):
        for copy in parcels(d, turn(z, -d, SLABS)):
            copy.wait_send()
        return carry

    lax.fori_loop(1, z + 1, sent_step, 0)


def attention(q, k, stream, ct):
    any_space, vmem = pl.BlockSpec(memory_space=pl.ANY), pl.BlockSpec(memory_space=pltpu.VMEM)
    whole = SLABS * SLAB
    mine = shape(ROWS, WIDTH)
    dma = pltpu.SemaphoreType.DMA
    return pl.pallas_call(
        attention_kernel,
        out_shape=[mine, mine, shape(SLAB + HALO, DH, kind=F32), shape(SLAB, DH)],
        in_specs=[vmem] * 4,
        out_specs=[any_space, any_space, vmem, vmem],
        scratch_shapes=[
            pltpu.VMEM((whole, DH), BF),
            pltpu.VMEM((DH, whole), BF),
            pltpu.VMEM((DH, whole), BF),
            pltpu.VMEM((whole, SLAB), F32),
            pltpu.VMEM((whole, SLAB), BF),
            pltpu.VMEM((1, SLAB), F32),
            pltpu.VMEM((DH, SLAB), F32),
            pltpu.VMEM((DH, SLAB), BF),
            pltpu.VMEM((SLAB, DH), BF),
            pltpu.VMEM((1, SLAB), F32),
            pltpu.VMEM((SLAB, DH), BF),
            pltpu.VMEM((SLAB, DH), BF),
            pltpu.VMEM((DH, SLAB), F32),
            pltpu.VMEM((SLAB, DH), F32),
            pltpu.VMEM((SLAB, DH), F32),
            pltpu.VMEM((HALO, DH), BF),
            pltpu.VMEM((SLABS - 1, SLAB + HALO, DH), BF),
            pltpu.VMEM((SLABS - 1, SLAB, DH), BF),
            pltpu.VMEM((SLABS - 1, SLAB + HALO, DH), BF),
            pltpu.VMEM((SLABS - 1, SLAB, DH), BF),
            dma((SLABS - 1,)),
            dma((SLABS - 1,)),
            dma((SLABS - 1,)),
            dma((SLABS - 1,)),
            dma((10,)),
            dma((10,)),
            dma((2,)),
        ],
        compiler_params=pltpu.CompilerParams(
            collective_id=2, has_side_effects=True, vmem_limit_bytes=58 << 20
        ),
    )(q, k, stream, ct)


def finale_kernel(
    fg, sg, dk, small, part0, part1, part2, part3, weights,
    grad_input, grad_feat, dk_home, small_home,
    w, tq, tqt, fgall, fgm, wsend, zr1, zr2, tsend, xr1, xr2, yr, ysend, sgh, slots, total,
    send, recv, loc,
):
    mail = Courier(send, recv, loc)
    z, a = place()
    row, col = lax.axis_index("row"), lax.axis_index("col")
    side, core = lax.div(a, 2), lax.rem(a, 2)
    mate, far, far_mate = side * 2 + 1 - core, (1 - side) * 2 + core, (1 - side) * 2 + 1 - core
    up, down = turn(z, 1, SLABS), turn(z, -1, SLABS)
    right, left = turn(col, 1, 4), turn(col, -1, 4)
    half = ROWS // 2
    pair = 2 * ROWS

    mail.keep(fg, fgall.at[a])
    for d, part in enumerate((part0, part1, part2, part3)):
        mail.keep(part, tq.at[rows(turn(a, -d, HEADS), ROWS)])
    for j in range(3):
        mail.keep(weights.at[j], w.at[j])
    greet(around(z, a) + [{"row": 1 - row}, {"col": right}, {"col": left}])

    near_rows, far_rows = rows(side, pair), rows(1 - side, pair)
    to_mate = mail.push(fg, fgall.at[a], at_ctx(z, mate))
    first = mail.push(fg.at[:, far_rows], fgall.at[a, :, far_rows], at_ctx(z, far))
    second = mail.push(fg.at[:, near_rows], fgall.at[a, :, near_rows], at_ctx(z, far))
    small_in = [mail.push(small, slots.at[d - 1], at_ctx(turn(z, d, SLABS), a)) for d in range(1, SLABS)]
    home_sg = []
    for d in range(1, HEADS):
        to = turn(a, d, HEADS)
        home_sg.append(mail.push(sg.at[rows(to, ROWS)], sgh.at[:, cols(a)], at_ctx(z, to)))
        mail.push(dk.at[rows(to, ROWS)], dk_home.at[:, cols(a)], at_ctx(z, to))
    mail.keep(sg.at[rows(a, ROWS)], sgh.at[:, cols(a)])
    mail.keep(dk.at[rows(a, ROWS)], dk_home.at[:, cols(a)])
    mail.settle()

    for b in range(SLABS):
        tqt[pl.ds(b * ROWS, ROWS)] = tq[:, pl.ds(b * ROWS, ROWS)].T

    def weight_block(n, head, dz):
        rhs = jnp.concatenate([fgall[head, j] for j in range(3)], axis=1)
        lhs = tqt[rows(turn(z, dz, SLABS), ROWS)]
        out = jnp.dot(lhs, rhs, preferred_element_type=F32)
        for j in range(3):
            wsend[n, dz, j] = out[:, j * DH : (j + 1) * DH].astype(BF)

    def weight_first(n, head):
        weight_block(n, head, 2)
        keys = (
            mail.push(wsend.at[n, 2, :, pl.ds(0, half)], zr1.at[n, 0], at_ctx(up, a)),
            mail.push(wsend.at[n, 2, :, pl.ds(half, half)], zr1.at[n, 1], at_ctx(down, a)),
        )
        for dz in (1, 3, 0):
            weight_block(n, head, dz)
        return keys

    def weight_second(n, keys):
        top, bottom = pl.ds(0, half), pl.ds(half, half)
        mail.arrive(keys[0])
        wsend[n, 1, :, top] = (wsend[n, 1, :, top].astype(F32) + zr1[n, 0].astype(F32)).astype(BF)
        one = mail.push(wsend.at[n, 1], zr2.at[n, 0], at_ctx(up, a))
        mail.arrive(keys[1])
        wsend[n, 3, :, bottom] = (wsend[n, 3, :, bottom].astype(F32) + zr1[n, 1].astype(F32)).astype(BF)
        return one, mail.push(wsend.at[n, 3], zr2.at[n, 1], at_ctx(down, a))

    def weight_third(n, head, keys):
        for k in keys:
            mail.arrive(k)
        for j in range(3):
            grad_feat[j, :, cols(head)] = (
                wsend[n, 0, j].astype(F32) + zr2[n, 0, j].astype(F32) + zr2[n, 1, j].astype(F32)
            )

    ring = [weight_first(0, a)]
    mail.arrive(to_mate)
    ring.append(weight_first(1, mate))
    mail.arrive(first)
    relay = mail.push(fgall.at[far, :, near_rows], fgall.at[far, :, near_rows], at_ctx(z, mate))
    ring[0] = weight_second(0, ring[0])
    ring[1] = weight_second(1, ring[1])
    mail.arrive(relay)

    for j in range(3):
        for h in range(HEADS):
            fgm[j, :, pl.ds(h * DH, DH)] = fgall[h, j, rows(a, ROWS)]

    def term_block(dc):
        for r in range(2):
            columns = rows(r * 4 + turn(col, dc, 4), WIDTH)
            out = jnp.zeros((ROWS, WIDTH), F32)
            for j in range(3):
                out += lax.dot_general(
                    fgm[j], w[j, columns], (((1,), (1,)), ((), ())), preferred_element_type=F32
                )
            tsend[dc, r] = out.astype(BF)

    top, bottom = pl.ds(0, half), pl.ds(half, half)
    term_block(2)
    from_left = mail.push(tsend.at[2, :, top], xr1.at[0], {"col": right})
    from_right = mail.push(tsend.at[2, :, bottom], xr1.at[1], {"col": left})
    term_block(1)
    term_block(3)
    mail.arrive(from_left)
    tsend[1, :, top] = (tsend[1, :, top].astype(F32) + xr1[0].astype(F32)).astype(BF)
    from_left = mail.push(tsend.at[1], xr2.at[0], {"col": right})
    mail.arrive(from_right)
    tsend[3, :, bottom] = (tsend[3, :, bottom].astype(F32) + xr1[1].astype(F32)).astype(BF)
    from_right = mail.push(tsend.at[3], xr2.at[1], {"col": left})
    term_block(0)

    mail.arrive(second)
    relay = mail.push(fgall.at[far, :, far_rows], fgall.at[far, :, far_rows], at_ctx(z, mate))
    ring.append(weight_first(2, far))
    mail.arrive(relay)
    ring.append(weight_first(3, far_mate))
    ring[2] = weight_second(2, ring[2])
    ring[3] = weight_second(3, ring[3])

    for k in small_in:
        mail.arrive(k)
    total[...] = (small_sum(small, slots)).astype(BF)
    for d in range(1, HEADS):
        mail.push(total, small_home.at[:, cols(a)], at_ctx(z, turn(a, d, HEADS)))
    mail.keep(total, small_home.at[:, cols(a)])

    mail.arrive(from_left)
    mail.arrive(from_right)

    def term_sum(r):
        return tsend[0, r].astype(F32) + xr2[0, r].astype(F32) + xr2[1, r].astype(F32)

    ysend[...] = term_sum(1 - row).astype(BF)
    across = mail.push(ysend, yr, {"row": 1 - row})
    weight_third(0, a, ring[0])
    weight_third(1, mate, ring[1])
    for k in home_sg:
        mail.arrive(k)
    mail.arrive(across)
    grad_input[...] = (sgh[...].astype(F32) + term_sum(row) + yr[...].astype(F32)).astype(BF)
    weight_third(2, far, ring[2])
    weight_third(3, far_mate, ring[3])
    mail.finish()


def small_sum(small, slots):
    return small[...].astype(F32) + sum(slots[d].astype(F32) for d in range(SLABS - 1))


def finale(fg, sg, dk, small, parts, weights):
    lines = small.shape[0]
    any_space, vmem = pl.BlockSpec(memory_space=pl.ANY), pl.BlockSpec(memory_space=pltpu.VMEM)
    remotes = 3 + 3 + 6 + 16 + 2 + 4 + 3 + 1
    return pl.pallas_call(
        finale_kernel,
        out_shape=[
            shape(ROWS, WIDTH),
            shape(3, ROWS, WIDTH, kind=F32),
            shape(ROWS, WIDTH),
            shape(lines, WIDTH),
        ],
        in_specs=[any_space, any_space, any_space, vmem] + [any_space] * 5,
        out_specs=[vmem, vmem, any_space, any_space],
        scratch_shapes=[
            pltpu.VMEM(weights.shape, BF),
            pltpu.VMEM((SLAB, SLABS * ROWS), BF),
            pltpu.VMEM((SLABS * ROWS, SLAB), BF),
            pltpu.VMEM((HEADS, 3, SLAB, DH), BF),
            pltpu.VMEM((3, ROWS, WIDTH), BF),
            pltpu.VMEM((HEADS, SLABS, 3, ROWS, DH), BF),
            pltpu.VMEM((HEADS, 2, 3, ROWS // 2, DH), BF),
            pltpu.VMEM((HEADS, 2, 3, ROWS, DH), BF),
            pltpu.VMEM((4, 2, ROWS, WIDTH), BF),
            pltpu.VMEM((2, 2, ROWS // 2, WIDTH), BF),
            pltpu.VMEM((2, 2, ROWS, WIDTH), BF),
            pltpu.VMEM((ROWS, WIDTH), BF),
            pltpu.VMEM((ROWS, WIDTH), BF),
            pltpu.VMEM((ROWS, WIDTH), BF),
            pltpu.VMEM((SLABS - 1, lines, DH), BF),
            pltpu.VMEM((lines, DH), BF),
            pltpu.SemaphoreType.DMA((remotes,)),
            pltpu.SemaphoreType.DMA((remotes,)),
            pltpu.SemaphoreType.DMA((11,)),
        ],
        compiler_params=pltpu.CompilerParams(
            collective_id=5, has_side_effects=True, vmem_limit_bytes=56 << 20
        ),
    )(fg, sg, dk, small, *parts, weights)


def compute(body, outs, scratch, *ins, vmem=56 << 20):
    z, a = place()
    return pl.pallas_call(
        body,
        out_shape=outs,
        in_specs=[pl.BlockSpec(memory_space=pltpu.SMEM)] + [pl.BlockSpec(memory_space=pltpu.VMEM)] * len(ins),
        out_specs=[pl.BlockSpec(memory_space=pltpu.VMEM)] * len(outs),
        scratch_shapes=scratch,
        compiler_params=pltpu.CompilerParams(vmem_limit_bytes=vmem),
    )(jnp.stack([z, a]).astype(jnp.int32), *ins)


GROUP = 40


def spread_taps(spread, taps, a):
    for i in range(MRLEN):
        spread[i] = jnp.broadcast_to(taps[pl.ds(i, 1), cols(a)], (8, DH))


def hyena_body(where, fx, short, mr, tok, stream, qm, km, vm, lm, pr, feat, spread):
    z, a = where[0], where[1]
    spread_taps(spread, mr, a)
    keep_head = (z > 0).astype(F32)
    keep_tail = (z < SLABS - 1).astype(F32)
    for j in range(3):
        feat[j, pl.ds(0, HALO)] = fx[j, pl.ds(0, HALO)].astype(F32) * keep_head
        feat[j, pl.ds(HALO, SLAB)] = fx[j, pl.ds(HALO, SLAB)].astype(F32)
        feat[j, pl.ds(HALO + SLAB, HALO)] = fx[j, pl.ds(HALO + SLAB, HALO)].astype(F32) * keep_tail

    taps = [[short[j, pl.ds(s, 1), cols(a)] for s in range(SHORT)] for j in range(3)]

    def mixed(j, base, count):
        total = taps[j][0] * feat[j, pl.ds(base, count)]
        for s in range(1, SHORT):
            total += taps[j][s] * feat[j, pl.ds(base - s, count)]
        return total

    pr[pl.ds(0, 16)] = jnp.zeros((16, DH), F32)

    def head_step(g, carry):
        base = pl.multiple_of(16 + g * 16, 16)
        pr[pl.ds(base, 16)] = (mixed(1, base, 16) * mixed(2, base, 16)).astype(BF).astype(F32)
        return carry

    lax.fori_loop(0, (HALO - 16) // 16, head_step, 0)

    def mix_step(g, carry):
        base = pl.multiple_of(HALO + g * GROUP, 8)
        local = pl.multiple_of(g * GROUP, 8)
        key, value = mixed(1, base, GROUP), mixed(2, base, GROUP)
        km[pl.ds(local, GROUP)] = key
        vm[pl.ds(local, GROUP)] = value
        qm[pl.ds(local, GROUP)] = mixed(0, base, GROUP)
        pr[pl.ds(base, GROUP)] = (key * value).astype(BF).astype(F32)
        return carry

    lax.fori_loop(0, (SLAB + TAIL) // GROUP, mix_step, 0)

    def tail_step(g, carry):
        local = pl.multiple_of(SLAB + TAIL + g * 16, 16)
        qm[pl.ds(local, 16)] = mixed(0, local + HALO, 16)
        return carry

    lax.fori_loop(0, (HALO - TAIL) // 16, tail_step, 0)

    def long_step(g, carry):
        base = pl.multiple_of(HALO + g * GROUP, 8)
        local = pl.multiple_of(g * GROUP, 8)
        total = [jnp.zeros((8, DH), F32) for _ in range(GROUP // 8)]
        for i in range(MRLEN):
            tap = spread[i]
            for n in range(GROUP // 8):
                total[n] += tap * pr[pl.ds(base + (n * 8 - i), 8)]
        for n in range(GROUP // 8):
            lm[pl.ds(local + n * 8, 8)] = total[n]
        return carry

    lax.fori_loop(0, (SLAB + TAIL) // GROUP, long_step, 0)
    own = pl.ds(0, SLAB)
    stream[...] = (tok[...].astype(F32) + qm[own] * lm[own]).astype(BF)


def back_body(where, dv, ch, chalo, fx, short, mr, qm, km, vm, lm, pr, sg, fg, small, mg, stack, feat, spread):
    z, a = where[0], where[1]
    spread_taps(spread, mr, a)
    keep_head = (z > 0).astype(F32)
    keep_tail = (z < SLABS - 1).astype(F32)
    own, halo = pl.ds(0, SLAB), pl.ds(SLAB, HALO)

    grad = (ch[...].astype(F32) + dv[own]).astype(BF)
    sg[...] = grad
    mg[own] = (grad.astype(F32) * qm[own]).astype(BF).astype(F32)
    grad_halo = (chalo[...].astype(F32) + dv[halo]).astype(BF).astype(F32) * keep_tail
    mg[halo] = (grad_halo * qm[halo]).astype(BF).astype(F32)
    stack[0, own] = grad.astype(F32) * lm[own]
    stack[0, pl.ds(SLAB, TAIL)] = grad_halo[:TAIL] * lm[pl.ds(SLAB, TAIL)]
    for j in range(3):
        feat[j, pl.ds(0, 16)] = fx[j, pl.ds(HALO - 16, 16)].astype(F32) * keep_head
        feat[j, pl.ds(16, SLAB)] = fx[j, pl.ds(HALO, SLAB)].astype(F32)

    def long_step(g, carry):
        local = pl.multiple_of(g * GROUP, 8)
        total = [jnp.zeros((8, DH), F32) for _ in range(GROUP // 8)]
        for i in range(MRLEN):
            tap = spread[i]
            for n in range(GROUP // 8):
                total[n] += tap * mg[pl.ds(local + (n * 8 + i), 8)]
        for n in range(GROUP // 8):
            part = pl.ds(local + n * 8, 8)
            stack[1, part] = total[n] * vm[part]
            stack[2, part] = total[n] * km[part]
        return carry

    lax.fori_loop(0, (SLAB + TAIL) // GROUP, long_step, 0)

    for j in range(3):
        taps = [short[j, pl.ds(s, 1), cols(a)] for s in range(SHORT)]

        def short_step(g, sums):
            base = pl.multiple_of(g * 32, 32)
            total = taps[0] * stack[j, pl.ds(base, 32)]
            for s in range(1, SHORT):
                total += taps[s] * stack[j, pl.ds(base + s, 32)]
            fg[j, pl.ds(base, 32)] = total.astype(BF)
            out = []
            for s in range(SHORT):
                term = stack[j, pl.ds(base, 32)] * feat[j, pl.ds(base + 16 - s, 32)]
                out.append(sums[s] + (term[0:8] + term[8:16] + term[16:24] + term[24:32]))
            return tuple(out)

        sums = lax.fori_loop(0, SLAB // 32, short_step, tuple(jnp.zeros((8, DH), F32) for _ in range(SHORT)))
        lines = [jnp.sum(t, axis=0, keepdims=True) for t in sums]
        small[pl.ds(MRLEN + 16 * j, 16)] = jnp.concatenate(lines + [jnp.zeros((16 - SHORT, DH), F32)], axis=0).astype(BF)

    def tap_step(c, carry):
        first = c * 16

        def row_step(g, sums):
            base = pl.multiple_of(g * 16, 16)
            out = list(sums)
            for n in range(2):
                line = mg[pl.ds(base + n * 8, 8)]
                for s in range(16):
                    out[s] += line * pr[pl.ds(base + (HALO + n * 8 - s) - first, 8)]
            return tuple(out)

        sums = lax.fori_loop(0, SLAB // 16, row_step, tuple(jnp.zeros((8, DH), F32) for _ in range(16)))
        lines = [jnp.sum(t, axis=0, keepdims=True) for t in sums]
        small[pl.ds(pl.multiple_of(first, 16), 16)] = jnp.concatenate(lines, axis=0).astype(BF)
        return carry

    lax.fori_loop(0, MRLEN // 16, tap_step, 0)


def local(tokens, w_feat, short_filter, mr_filter, queries, key_rows, cotangent):
    weights = w_feat.transpose(1, 0, 2)
    short_taps = short_filter.transpose(1, 0, 2)
    head = shape(SLAB, DH)
    th, qh, ch, chalo, fx, kfull, pieces = front(tokens, queries, key_rows, cotangent, weights)
    token_parts = [pieces[0]]
    for d in range(1, HEADS):
        route = [(s * HEADS + a, s * HEADS + (a + d) % HEADS) for s in range(SLABS) for a in range(HEADS)]
        token_parts.append(lax.ppermute(pieces[d], "ctx", route))
    filters = [pltpu.VMEM((MRLEN, 8, DH), F32)]
    stream, qm, km, vm, lm, pr = compute(
        hyena_body,
        [
            head,
            shape(SLAB + HALO, DH, kind=F32),
            shape(SLAB + TAIL, DH, kind=F32),
            shape(SLAB + TAIL, DH, kind=F32),
            shape(SLAB + TAIL, DH, kind=F32),
            shape(HALO + SLAB + TAIL, DH, kind=F32),
        ],
        [pltpu.VMEM((3, EXT, DH), F32)] + filters,
        fx,
        short_taps,
        mr_filter,
        th,
    )
    block_out, grad_queries, dv, dk = attention(qh, kfull, stream, ch)
    sg, fg, small = compute(
        back_body,
        [head, shape(3, SLAB, DH), shape(MRLEN + 3 * 16, DH)],
        [
            pltpu.VMEM((SLAB + HALO, DH), F32),
            pltpu.VMEM((3, SLAB + TAIL, DH), F32),
            pltpu.VMEM((3, SLAB + 16, DH), F32),
        ]
        + filters,
        dv,
        ch,
        chalo,
        fx,
        short_taps,
        mr_filter,
        qm,
        km,
        vm,
        lm,
        pr,
    )
    grad_input, grad_feat, grad_keys, small_home = finale(fg, sg, dk, small, token_parts, weights)
    sums = small_home.astype(F32)
    grad_short = sums[MRLEN:].reshape(3, 16, WIDTH)[:, :SHORT].transpose(1, 0, 2)
    grad_feat = grad_feat.transpose(1, 0, 2)
    grad_mr = sums[:MRLEN]
    return (block_out, grad_input, grad_feat, grad_short, grad_mr, grad_queries, grad_keys)


def solution(mesh):
    placed = (
        P("ctx", ("row", "col")),
        P(None, None, ("row", "col")),
        P(None, None, ("row", "col")),
        P(None, ("row", "col")),
        P("ctx", ("row", "col")),
        P("ctx", ("row", "col")),
        P("ctx", ("row", "col")),
    )
    return jax.shard_map(
        local,
        mesh=mesh,
        in_specs=placed,
        out_specs=(
            P("ctx", ("row", "col")),
            P("ctx", ("row", "col")),
            P("ctx", None, ("row", "col")),
            P(None, None, ("row", "col")),
            P(None, ("row", "col")),
            P("ctx", ("row", "col")),
            P("ctx", ("row", "col")),
        ),
        check_vma=False,
    )
```

```python
import functools

import jax
import jax.numpy as jnp
from jax import lax
from jax.experimental import pallas as pl
from jax.experimental.pallas import tpu as pltpu
from jax.sharding import PartitionSpec as P

DH = 128
SHORT = 7
MRLEN = 128
HALO = 144
TAIL = 16
ROWS = 256
HEADS = 4
SLABS = 4
SLAB = ROWS * HEADS
EXT = HALO + SLAB + HALO
WIDTH = HEADS * DH
MESH = pl.DeviceIdType.MESH
BF = jnp.bfloat16
F32 = jnp.float32


def place():
    ctx = lax.axis_index("ctx")
    return lax.div(ctx, HEADS), lax.rem(ctx, HEADS)


def turn(index, step, size):
    return lax.rem(index + (step + size), size)


def at_ctx(z, a):
    return {"ctx": z * HEADS + a}


def cols(index, width=DH):
    return pl.ds(pl.multiple_of(index * width, width), width)


def rows(index, height, offset=0):
    return pl.ds(pl.multiple_of(index * height + offset, 16), height)


def greet(devices):
    barrier = pltpu.get_barrier_semaphore()
    for device in devices:
        pl.semaphore_signal(barrier, inc=1, device_id=device, device_id_type=MESH)
    pl.semaphore_wait(barrier, len(devices))


class Courier:
    def __init__(self, send, recv, local):
        self.send, self.recv, self.local = send, recv, local
        self.remote, self.here = [], []
        self.arrived = set()
        self.settled = 0

    def push(self, src, dst, device):
        k = len(self.remote)
        copy = pltpu.make_async_remote_copy(
            src_ref=src,
            dst_ref=dst,
            send_sem=self.send.at[k],
            recv_sem=self.recv.at[k],
            device_id=device,
            device_id_type=MESH,
        )
        copy.start()
        self.remote.append(copy)
        return k

    def keep(self, src, dst):
        copy = pltpu.make_async_copy(src, dst, self.local.at[len(self.here)])
        copy.start()
        self.here.append(copy)

    def arrive(self, k):
        if k not in self.arrived:
            self.arrived.add(k)
            self.remote[k].wait_recv()

    def finish(self):
        for k in range(len(self.remote)):
            self.arrive(k)
        for copy in self.remote:
            copy.wait_send()
        self.settle()

    def settle(self):
        for copy in self.here[self.settled :]:
            copy.wait()
        self.settled = len(self.here)


def shape(*dims, kind=BF):
    return jax.ShapeDtypeStruct(dims, kind)


def slab_gather(mail, part, whole, z, a):
    up, down = turn(z, 1, SLABS), turn(z, -1, SLABS)
    mine = whole.at[rows(z, SLAB)]
    mail.keep(part, mine)
    return mail.push(part, mine, at_ctx(up, a)), mail.push(part, mine, at_ctx(down, a))


def slab_relay(mail, whole, z, a, from_down, from_up):
    up, down = turn(z, 1, SLABS), turn(z, -1, SLABS)
    half = SLAB // 2
    mail.arrive(from_down)
    lower = whole.at[pl.ds(pl.multiple_of(down * SLAB, 16), half)]
    mail.push(lower, lower, at_ctx(up, a))
    mail.arrive(from_up)
    upper = whole.at[pl.ds(pl.multiple_of(up * SLAB + half, 16), half)]
    mail.push(upper, upper, at_ctx(down, a))


def front_kernel(
    tokens, queries, keys, cot, weights,
    th, qh, ch, chalo, fx, kfull, piece0, piece1, piece2, piece3,
    full, w, acc, feats, kh, send, recv, loc,
):
    mail = Courier(send, recv, loc)
    z, a = place()
    row, col = lax.axis_index("row"), lax.axis_index("col")
    other = 1 - row
    right, left, across = turn(col, 1, 4), turn(col, -1, 4), turn(col, 2, 4)
    up, down = turn(z, 1, SLABS), turn(z, -1, SLABS)
    for j in range(3):
        mail.keep(weights.at[j], w.at[j])
    greet(
        [{"row": other}, {"col": right}, {"col": left}]
        + [at_ctx(z, turn(a, d, HEADS)) for d in range(1, HEADS)]
        + [at_ctx(s, b) for s in (up, down) for b in range(HEADS)]
    )

    def block(r, c):
        return full.at[:, cols(r * 4 + c, WIDTH)]

    def half(r, c, h):
        return full.at[pl.ds(h * (ROWS // 2), ROWS // 2), cols(r * 4 + c, WIDTH)]

    def project(r, c, lhs=None):
        lhs = full[:, cols(r * 4 + c, WIDTH)] if lhs is None else lhs
        for j in range(3):
            acc[j] += jnp.dot(lhs, w[j, rows(r * 4 + c, WIDTH)], preferred_element_type=F32)

    vertical = mail.push(tokens, block(row, col), {"row": other})
    fr = mail.push(tokens, block(row, col), {"col": right})
    fl = mail.push(tokens, block(row, col), {"col": left})
    full[:, cols(row * 4 + col, WIDTH)] = tokens[...]
    kh[rows(a, ROWS)] = keys[:, cols(a)]
    acc[...] = jnp.zeros_like(acc)
    mail.settle()
    project(row, col, tokens[...])
    mail.arrive(vertical)
    gr = mail.push(block(other, col), block(other, col), {"col": right})
    gl = mail.push(block(other, col), block(other, col), {"col": left})
    key_parts = []
    for src, dst in ((keys, kh), (tokens, th), (queries, qh), (cot, ch)):
        for d in range(1, HEADS):
            to = turn(a, d, HEADS)
            k = mail.push(src.at[:, cols(to)], dst.at[rows(a, ROWS)], at_ctx(z, to))
            if dst is kh:
                key_parts.append(k)
        if dst is not kh:
            mail.keep(src.at[:, cols(a)], dst.at[rows(a, ROWS)])
    project(other, col)
    relays = []
    for r, from_left, from_right in ((row, fr, fl), (other, gr, gl)):
        mail.arrive(from_left)
        relays.append(mail.push(half(r, left, 0), half(r, left, 0), {"col": right}))
        mail.arrive(from_right)
        relays.append(mail.push(half(r, right, 1), half(r, right, 1), {"col": left}))
        project(r, left)
        project(r, right)
        if r is row:
            for k in key_parts:
                mail.arrive(k)
            gathered = slab_gather(mail, kh, kfull, z, a)
    for r, first in ((row, 0), (other, 2)):
        mail.arrive(relays[first])
        mail.arrive(relays[first + 1])
        project(r, across)
    slab_relay(mail, kfull, z, a, *gathered)
    feats[...] = acc[...].astype(BF)

    for d in range(1, HEADS):
        to = turn(a, d, HEADS)
        mail.push(feats.at[:, :, cols(to)], fx.at[:, rows(a, ROWS, HALO)], at_ctx(z, to))
    mail.keep(feats.at[:, :, cols(a)], fx.at[:, rows(a, ROWS, HALO)])

    n = len(mail.remote)

    def edge(src, dst, k, b, device):
        return pltpu.make_async_remote_copy(
            src_ref=src,
            dst_ref=dst,
            send_sem=mail.send.at[k + 3 * b],
            recv_sem=mail.recv.at[k],
            device_id=device,
            device_id_type=MESH,
        )

    def first_rows(b):
        lanes = pl.ds(b * DH, DH)
        return (
            edge(feats.at[:, pl.ds(0, HALO), lanes], fx.at[:, pl.ds(HALO + SLAB, HALO)], n, b, at_ctx(down, b)),
            edge(cot.at[pl.ds(0, HALO), lanes], chalo, n + 1, b, at_ctx(down, b)),
        )

    def last_rows(b):
        lanes = pl.ds(b * DH, DH)
        return (edge(feats.at[:, pl.ds(ROWS - HALO, HALO), lanes], fx.at[:, pl.ds(0, HALO)], n + 2, b, at_ctx(up, b)),)

    @pl.when(a == 0)
    def _():
        for b in range(HEADS):
            for copy in first_rows(b):
                copy.start()

    @pl.when(a == HEADS - 1)
    def _():
        for b in range(HEADS):
            for copy in last_rows(b):
                copy.start()

    for d, piece in enumerate((piece0, piece1, piece2, piece3)):
        for s in range(SLABS):
            mail.keep(full.at[:, cols(s * HEADS + turn(a, d, HEADS), ROWS)], piece.at[:, pl.ds(s * ROWS, ROWS)])
    mail.finish()
    for copy in first_rows(0) + last_rows(0):
        copy.wait_recv()

    @pl.when(a == 0)
    def _():
        for b in range(HEADS):
            for copy in first_rows(b):
                copy.wait_send()

    @pl.when(a == HEADS - 1)
    def _():
        for b in range(HEADS):
            for copy in last_rows(b):
                copy.wait_send()


def front(tokens, queries, keys, cot, weights):
    any_space, vmem = pl.BlockSpec(memory_space=pl.ANY), pl.BlockSpec(memory_space=pltpu.VMEM)
    head = shape(SLAB, DH)
    outs = [
        head,
        head,
        head,
        shape(HALO, DH),
        shape(3, EXT, DH),
        shape(SLABS * SLAB, DH),
    ] + [shape(ROWS, SLABS * ROWS)] * HEADS
    remotes = 3 + 2 + 12 + 4 + 3 + 4 + 12
    return pl.pallas_call(
        front_kernel,
        out_shape=outs,
        in_specs=[vmem] * 4 + [any_space],
        out_specs=[any_space] * len(outs),
        scratch_shapes=[
            pltpu.VMEM((ROWS, 8 * WIDTH), BF),
            pltpu.VMEM(weights.shape, BF),
            pltpu.VMEM((3, ROWS, WIDTH), F32),
            pltpu.VMEM((3, ROWS, WIDTH), BF),
            pltpu.VMEM((SLAB, DH), BF),
            pltpu.SemaphoreType.DMA((remotes,)),
            pltpu.SemaphoreType.DMA((remotes,)),
            pltpu.SemaphoreType.DMA((3 + 3 + 1 + 1 + HEADS * SLABS,)),
        ],
        compiler_params=pltpu.CompilerParams(
            collective_id=0, has_side_effects=True, vmem_limit_bytes=56 << 20
        ),
    )(tokens, queries, keys, cot, weights)


def around(z, a):
    return [at_ctx(turn(z, d, SLABS), a) for d in range(1, SLABS)] + [
        at_ctx(z, turn(a, d, HEADS)) for d in range(1, HEADS)
    ]


def home(mail, src, dst, z, a):
    for d in range(1, HEADS):
        to = turn(a, d, HEADS)
        mail.push(src.at[rows(to, ROWS)], dst.at[:, cols(a)], at_ctx(z, to))
    mail.keep(src.at[rows(a, ROWS)], dst.at[:, cols(a)])


CHUNK = 512


def dot(x, y):
    return jnp.dot(x, y, preferred_element_type=F32)


def dot_t(x, y):
    return lax.dot_general(x, y, (((1,), (1,)), ((), ())), preferred_element_type=F32)


GROUP = 40
TILE = 8
TAPS = MRLEN // TILE
SPAN = 13


def spread_taps(spread, taps, a):
    for i in range(MRLEN):
        spread[i % TILE, i // TILE] = jnp.broadcast_to(taps[pl.ds(i, 1), cols(a)], (TILE, DH))


def spread_shifts(shifts, rows_of, first, sign):
    count = shifts.shape[1]
    for r in range(TILE):
        shifts[r] = rows_of[pl.ds(first + sign * r, count)]


def long_filter(shifts, spread, backward, store):
    def step(g, carry):
        base = pl.multiple_of(g * (SPAN * TILE), TILE)

        def shift(r, totals):
            totals = list(totals)
            taps = [spread[r, m] for m in range(TAPS)]
            for t in range(SPAN + TAPS - 1):
                tile = shifts[r, pl.ds(base + t * TILE, TILE)]
                for n in range(SPAN):
                    m = t - n if backward else n + TAPS - 1 - t
                    if 0 <= m < TAPS:
                        totals[n] += taps[m] * tile
            return tuple(totals)

        totals = lax.fori_loop(0, TILE, shift, tuple(jnp.zeros((TILE, DH), F32) for _ in range(SPAN)))
        for n in range(SPAN):
            store(pl.ds(base + n * TILE, TILE), totals[n])
        return carry

    lax.fori_loop(0, (SLAB + TAIL) // (SPAN * TILE), step, 0)


def tap_grads(shifts, grads, lines):
    count = 16

    def shift(r, carry):
        def step(g, sums):
            sums = list(sums)
            base = pl.multiple_of(g * (count * TILE), TILE)
            own = [grads[pl.ds(base + n * TILE, TILE)] for n in range(count)]
            for t in range(count + TAPS - 1):
                tile = shifts[r, pl.ds(base + t * TILE, TILE)]
                for n in range(count):
                    m = n + TAPS - 1 - t
                    if 0 <= m < TAPS:
                        sums[m] += own[n] * tile
            return tuple(sums)

        zero = tuple(jnp.zeros((TILE, DH), F32) for _ in range(TAPS))
        sums = lax.fori_loop(0, SLAB // (count * TILE), step, zero)
        for m in range(TAPS):
            lines[m, pl.ds(r, 1)] = jnp.sum(sums[m], axis=0, keepdims=True)
        return carry

    lax.fori_loop(0, TILE, shift, 0)


def hyena(z, a, fx, short, tok, stream, qm, km, vm, lm, pr, feat, shifts, spread):
    keep_head = (z > 0).astype(F32)
    keep_tail = (z < SLABS - 1).astype(F32)
    for j in range(3):
        feat[j, pl.ds(0, HALO)] = fx[j, pl.ds(0, HALO)].astype(F32) * keep_head
        feat[j, pl.ds(HALO, SLAB)] = fx[j, pl.ds(HALO, SLAB)].astype(F32)
        feat[j, pl.ds(HALO + SLAB, HALO)] = fx[j, pl.ds(HALO + SLAB, HALO)].astype(F32) * keep_tail

    taps = [[short[j, pl.ds(s, 1), cols(a)] for s in range(SHORT)] for j in range(3)]

    def mixed(j, base, count):
        total = taps[j][0] * feat[j, pl.ds(base, count)]
        for s in range(1, SHORT):
            total += taps[j][s] * feat[j, pl.ds(base - s, count)]
        return total

    pr[pl.ds(0, 16)] = jnp.zeros((16, DH), F32)

    def head_step(g, carry):
        base = pl.multiple_of(16 + g * 16, 16)
        pr[pl.ds(base, 16)] = (mixed(1, base, 16) * mixed(2, base, 16)).astype(BF).astype(F32)
        return carry

    lax.fori_loop(0, (HALO - 16) // 16, head_step, 0)

    def mix_step(g, carry):
        base = pl.multiple_of(HALO + g * GROUP, 8)
        here = pl.ds(pl.multiple_of(g * GROUP, 8), GROUP)
        key, value = mixed(1, base, GROUP), mixed(2, base, GROUP)
        km[here] = key
        vm[here] = value
        qm[here] = mixed(0, base, GROUP)
        pr[pl.ds(base, GROUP)] = (key * value).astype(BF).astype(F32)
        return carry

    lax.fori_loop(0, (SLAB + TAIL) // GROUP, mix_step, 0)

    def tail_step(g, carry):
        here = pl.multiple_of(SLAB + TAIL + g * 16, 16)
        qm[pl.ds(here, 16)] = mixed(0, here + HALO, 16)
        return carry

    lax.fori_loop(0, (HALO - TAIL) // 16, tail_step, 0)
    spread_shifts(shifts, pr, HALO - MRLEN + TILE, -1)

    def store(here, total):
        lm[here] = total

    long_filter(shifts, spread, False, store)
    own = pl.ds(0, SLAB)
    stream[...] = (tok[...].astype(F32) + qm[own] * lm[own]).astype(BF)


def back(z, a, dv, ch, chalo, short, qm, km, vm, lm, feat, sg, fg, short_part, mg, stack, shifts, spread):
    keep_tail = (z < SLABS - 1).astype(F32)
    own, halo = pl.ds(0, SLAB), pl.ds(SLAB, HALO)
    grad = (ch[...].astype(F32) + dv[own]).astype(BF)
    sg[...] = grad
    mg[own] = (grad.astype(F32) * qm[own]).astype(BF).astype(F32)
    grad_halo = (chalo[...].astype(F32) + dv[halo]).astype(BF).astype(F32) * keep_tail
    mg[halo] = (grad_halo * qm[halo]).astype(BF).astype(F32)
    stack[0, own] = grad.astype(F32) * lm[own]
    stack[0, pl.ds(SLAB, TAIL)] = grad_halo[:TAIL] * lm[pl.ds(SLAB, TAIL)]
    spread_shifts(shifts, mg, 0, 1)

    def store(here, total):
        stack[1, here] = total * vm[here]
        stack[2, here] = total * km[here]

    long_filter(shifts, spread, True, store)
    for j in range(3):
        taps = [short[j, pl.ds(s, 1), cols(a)] for s in range(SHORT)]

        def short_step(g, sums):
            base = pl.multiple_of(g * 32, 32)
            line = stack[j, pl.ds(base, 32)]
            total = taps[0] * line
            for s in range(1, SHORT):
                total += taps[s] * stack[j, pl.ds(base + s, 32)]
            fg[j, pl.ds(base, 32)] = total.astype(BF)
            out = []
            for s in range(SHORT):
                term = line * feat[j, pl.ds(base + HALO - s, 32)]
                out.append(sums[s] + (term[0:8] + term[8:16] + term[16:24] + term[24:32]))
            return tuple(out)

        sums = lax.fori_loop(0, SLAB // 32, short_step, tuple(jnp.zeros((8, DH), F32) for _ in range(SHORT)))
        lines = [jnp.sum(t, axis=0, keepdims=True) for t in sums]
        short_part[pl.ds(16 * j, 16)] = jnp.concatenate(lines + [jnp.zeros((16 - SHORT, DH), F32)], axis=0).astype(BF)


def middle_kernel(
    fx, tok, q, k, ct, chalo, short, mr,
    block_home, dq_home, sg, fg, dk, short_part, mg, pr,
    stream, v, kt, vt, st, pt, tops, outs, ctt, cs, delta, block, dq, dqt, dv, dka, edge, dv_out, dk_out, dv_in, dk_in,
    qm, km, vm, lm, feat, stack, shifts, spread,
    dv_send, dv_recv, dk_send, dk_recv, send, recv, loc,
):
    mail = Courier(send, recv, loc)
    z, a = place()
    scale = DH ** -0.5
    gain = scale * 1.4426950408889634
    mine = rows(z, SLAB)
    up, down = at_ctx(turn(z, 1, SLABS), a), at_ctx(turn(z, -1, SLABS), a)
    spread_taps(spread, mr, a)

    def turn_keys(s, carry):
        kt[:, cols(s, SLAB)] = k[rows(s, SLAB)].T
        return carry

    hyena(z, a, fx, short, tok, stream, qm, km, vm, lm, pr, feat, shifts, spread)
    greet(around(z, a))
    from_down = mail.push(stream, v.at[mine], up)
    from_up = mail.push(stream, v.at[mine], down)
    v[mine] = stream[...]

    def lanes_of(i):
        return pl.ds(i * ROWS, ROWS)

    def slots(c):
        return pl.ds(pl.multiple_of(SLAB + c * CHUNK, CHUNK), CHUNK)

    def keys_of(c):
        return pl.ds(pl.multiple_of(c * CHUNK, CHUNK), CHUNK)

    after = lax.broadcasted_iota(jnp.int32, (ROWS, ROWS), 0) > lax.broadcasted_iota(jnp.int32, (ROWS, ROWS), 1)
    for i in range(HEADS):
        span = ROWS * (i + 1)
        scores = dot_t(k[pl.ds(pl.multiple_of(z * SLAB, SLAB), span)], q[lanes_of(i)])
        corner = jnp.where(after, -1e30, scores[span - ROWS :])
        top = jnp.max(corner, axis=0, keepdims=True)
        if i:
            top = jnp.maximum(top, jnp.max(scores[: span - ROWS], axis=0, keepdims=True))
            st[pl.ds(0, span - ROWS), lanes_of(i)] = scores[: span - ROWS]
        st[pl.ds(span - ROWS, ROWS), lanes_of(i)] = corner
        tops[:, lanes_of(i)] = top

    def score_step(c, top):
        past = dot_t(k[keys_of(c)], q[...])
        st[slots(c)] = past
        return jnp.maximum(top, jnp.max(past, axis=0, keepdims=True))

    top = lax.fori_loop(0, z * (SLAB // CHUNK), score_step, tops[...]) * gain

    half = SLAB // 2
    mail.arrive(from_down)
    lower = v.at[pl.ds(pl.multiple_of(turn(z, -1, SLABS) * SLAB, SLAB), half)]
    mail.push(lower, lower, up)
    mail.arrive(from_up)
    upper = v.at[pl.ds(pl.multiple_of(turn(z, 1, SLABS) * SLAB + half, half), half)]
    mail.push(upper, upper, down)

    for i in range(HEADS):
        span = ROWS * (i + 1)
        p = jnp.exp2(st[pl.ds(0, span), lanes_of(i)] * gain - top[:, i * ROWS : (i + 1) * ROWS])
        tops[:, lanes_of(i)] = jnp.sum(p, axis=0, keepdims=True)
        pt[pl.ds(0, span), lanes_of(i)] = p.astype(BF)

    def weigh_step(c, total):
        p = jnp.exp2(st[slots(c)] * gain - top)
        pt[slots(c)] = p.astype(BF)
        return total + jnp.sum(p, axis=0, keepdims=True)

    inverse = 1.0 / lax.fori_loop(0, z * (SLAB // CHUNK), weigh_step, tops[...])
    lax.fori_loop(0, z + 1, turn_keys, 0)
    mail.arrive(2)
    mail.arrive(3)

    def turn_values(s, carry):
        vt[:, cols(s, SLAB)] = v[rows(s, SLAB)].T
        return carry

    lax.fori_loop(0, z + 1, turn_values, 0)
    for i in range(HEADS):
        span = ROWS * (i + 1)
        outs[:, lanes_of(i)] = dot(vt[:, pl.ds(pl.multiple_of(z * SLAB, SLAB), span)], pt[pl.ds(0, span), lanes_of(i)])

    def attend_step(c, carry):
        outs[...] += dot(vt[:, keys_of(c)], pt[slots(c)])
        return carry

    lax.fori_loop(0, z * (SLAB // CHUNK), attend_step, 0)
    out = outs[...] * inverse
    ctt[...] = (ct[...].astype(F32).T * inverse).astype(BF)
    cs[...] = ctt[...].T
    delta[...] = jnp.sum(ctt[...].astype(F32) * out, axis=0, keepdims=True)

    for i in reversed(range(HEADS)):
        span = ROWS * (i + 1)
        part = dot(pt[pl.ds(0, span), lanes_of(i)], cs[lanes_of(i)])
        if i == HEADS - 1:
            dv[pl.ds(0, SLAB)] = part
        else:
            dv[pl.ds(0, span)] += part
    dv[pl.ds(SLAB, HALO)] = jnp.zeros((HALO, DH), F32)
    edge[...] = dv[pl.ds(0, HALO)].astype(BF)

    def parcel(d, to, kind):
        src, dst, sent, got = ((dv_out, dv_in, dv_send, dv_recv), (dk_out, dk_in, dk_send, dk_recv))[kind]
        return pltpu.make_async_remote_copy(
            src_ref=src.at[d - 1],
            dst_ref=dst.at[d - 1],
            send_sem=sent.at[d - 1],
            recv_sem=got.at[d - 1],
            device_id=at_ctx(to, a),
            device_id_type=MESH,
        )

    def value_step(d, carry):
        s = z - d
        dv_out[d - 1, pl.ds(SLAB, HALO)] = edge[...]
        for n in range(SLAB // CHUNK):
            part = dot(pt[slots(s * (SLAB // CHUNK) + n)], cs[...]).astype(BF)
            dv_out[d - 1, pl.ds(n * CHUNK, CHUNK)] = part
            if n == 0:
                edge[...] = part[:HALO]
        parcel(d, s, 0).start()
        return carry

    lax.fori_loop(1, z + 1, value_step, 0)
    block[...] = (stream[...].astype(F32) + out.T).astype(BF)
    home(mail, block, block_home, z, a)

    for i in reversed(range(HEADS)):
        span = ROWS * (i + 1)
        here = pl.ds(pl.multiple_of(z * SLAB, SLAB), span)
        p = pt[pl.ds(0, span), lanes_of(i)]
        dp = dot(v[here], ctt[:, lanes_of(i)])
        ds = (p.astype(F32) * (dp - delta[:, lanes_of(i)])).astype(BF)
        part = dot(ds, q[lanes_of(i)])
        dqt[:, lanes_of(i)] = dot(kt[:, here], ds)
        if i == HEADS - 1:
            dka[...] = part
        else:
            dka[pl.ds(0, span)] += part

    def key_step(d, carry):
        s = z - d
        for n in range(SLAB // CHUNK):
            c = s * (SLAB // CHUNK) + n
            dp = dot(v[keys_of(c)], ctt[...])
            ds = (pt[slots(c)].astype(F32) * (dp - delta[...])).astype(BF)
            dk_out[d - 1, pl.ds(n * CHUNK, CHUNK)] = (dot(ds, q[...]) * scale).astype(BF)
            dqt[...] += dot(kt[:, keys_of(c)], ds)
        parcel(d, s, 1).start()
        return carry

    lax.fori_loop(1, z + 1, key_step, 0)
    dq[...] = (dqt[...].T * scale).astype(BF)
    home(mail, dq, dq_home, z, a)

    def add_values(d, carry):
        parcel(d, turn(z, d, SLABS), 0).wait_recv()
        dv[...] += dv_in[d - 1].astype(F32)
        return carry

    lax.fori_loop(1, SLABS - z, add_values, 0)
    back(z, a, dv, ct, chalo, short, qm, km, vm, lm, feat, sg, fg, short_part, mg, stack, shifts, spread)
    dka[...] = dka[...] * scale

    def add_keys(d, carry):
        parcel(d, turn(z, d, SLABS), 1).wait_recv()
        dka[...] += dk_in[d - 1].astype(F32)
        return carry

    lax.fori_loop(1, SLABS - z, add_keys, 0)
    dk[...] = dka[...].astype(BF)
    mail.finish()

    def sent_step(d, carry):
        for kind in range(2):
            parcel(d, turn(z, -d, SLABS), kind).wait_send()
        return carry

    lax.fori_loop(1, z + 1, sent_step, 0)


def middle(fx, tok, q, k, ct, chalo, short, mr):
    any_space, vmem = pl.BlockSpec(memory_space=pl.ANY), pl.BlockSpec(memory_space=pltpu.VMEM)
    whole = SLABS * SLAB
    mine, head = shape(ROWS, WIDTH), shape(SLAB, DH)
    dma = pltpu.SemaphoreType.DMA
    return pl.pallas_call(
        middle_kernel,
        out_shape=[
            mine,
            mine,
            head,
            shape(3, SLAB, DH),
            head,
            shape(3 * 16, DH),
            shape(SLAB + HALO, DH, kind=F32),
            shape(HALO + SLAB + TAIL, DH, kind=F32),
        ],
        in_specs=[vmem] * 8,
        out_specs=[any_space] * 2 + [vmem] * 6,
        scratch_shapes=[
            pltpu.VMEM((SLAB, DH), BF),
            pltpu.VMEM((whole, DH), BF),
            pltpu.VMEM((DH, whole), BF),
            pltpu.VMEM((DH, whole), BF),
            pltpu.VMEM((whole, SLAB), F32),
            pltpu.VMEM((whole, SLAB), BF),
            pltpu.VMEM((1, SLAB), F32),
            pltpu.VMEM((DH, SLAB), F32),
            pltpu.VMEM((DH, SLAB), BF),
            pltpu.VMEM((SLAB, DH), BF),
            pltpu.VMEM((1, SLAB), F32),
            pltpu.VMEM((SLAB, DH), BF),
            pltpu.VMEM((SLAB, DH), BF),
            pltpu.VMEM((DH, SLAB), F32),
            pltpu.VMEM((SLAB + HALO, DH), F32),
            pltpu.VMEM((SLAB, DH), F32),
            pltpu.VMEM((HALO, DH), BF),
            pltpu.VMEM((SLABS - 1, SLAB + HALO, DH), BF),
            pltpu.VMEM((SLABS - 1, SLAB, DH), BF),
            pltpu.VMEM((SLABS - 1, SLAB + HALO, DH), BF),
            pltpu.VMEM((SLABS - 1, SLAB, DH), BF),
            pltpu.VMEM((SLAB + HALO, DH), F32),
            pltpu.VMEM((SLAB + TAIL, DH), F32),
            pltpu.VMEM((SLAB + TAIL, DH), F32),
            pltpu.VMEM((SLAB + TAIL, DH), F32),
            pltpu.VMEM((3, EXT, DH), F32),
            pltpu.VMEM((3, SLAB + TAIL, DH), F32),
            pltpu.VMEM((TILE, SLAB + TAIL + MRLEN - TILE, DH), F32),
            pltpu.VMEM((TILE, TAPS, TILE, DH), F32),
            dma((SLABS - 1,)),
            dma((SLABS - 1,)),
            dma((SLABS - 1,)),
            dma((SLABS - 1,)),
            dma((10,)),
            dma((10,)),
            dma((2,)),
        ],
        compiler_params=pltpu.CompilerParams(
            collective_id=2, has_side_effects=True, vmem_limit_bytes=58 << 20
        ),
    )(fx, tok, q, k, ct, chalo, short, mr)


def finale_kernel(
    fg, sg, dk, short_part, mg, pr, part0, part1, part2, part3, weights,
    grad_input, grad_feat, dk_home, small_home,
    w, tq, tqt, fgall, fgm, wsend, zr1, zr2, tsend, xr1, xr2, yr, ysend, sgh, slots, small, total, shifts, lines,
    send, recv, loc,
):
    mail = Courier(send, recv, loc)
    z, a = place()
    row, col = lax.axis_index("row"), lax.axis_index("col")
    side, core = lax.div(a, 2), lax.rem(a, 2)
    mate, far, far_mate = side * 2 + 1 - core, (1 - side) * 2 + core, (1 - side) * 2 + 1 - core
    up, down = turn(z, 1, SLABS), turn(z, -1, SLABS)
    right, left = turn(col, 1, 4), turn(col, -1, 4)
    half = ROWS // 2
    pair = 2 * ROWS

    mail.keep(fg, fgall.at[a])
    for d, part in enumerate((part0, part1, part2, part3)):
        mail.keep(part, tq.at[rows(turn(a, -d, HEADS), ROWS)])
    loads = [pltpu.make_async_copy(weights.at[j], w.at[j], loc.at[8 + j]) for j in range(3)]
    for load in loads:
        load.start()
    greet(around(z, a) + [{"row": 1 - row}, {"col": right}, {"col": left}])

    near_rows, far_rows = rows(side, pair), rows(1 - side, pair)
    to_mate = mail.push(fg, fgall.at[a], at_ctx(z, mate))
    first = mail.push(fg.at[:, far_rows], fgall.at[a, :, far_rows], at_ctx(z, far))
    mail.settle()

    for b in range(SLABS):
        tqt[pl.ds(b * ROWS, ROWS)] = tq[:, pl.ds(b * ROWS, ROWS)].T

    def weight_block(n, head, dz):
        rhs = jnp.concatenate([fgall[head, j] for j in range(3)], axis=1)
        lhs = tqt[rows(turn(z, dz, SLABS), ROWS)]
        out = jnp.dot(lhs, rhs, preferred_element_type=F32)
        for j in range(3):
            wsend[n, dz, j] = out[:, j * DH : (j + 1) * DH].astype(BF)

    def weight_first(n, head):
        weight_block(n, head, 2)
        keys = (
            mail.push(wsend.at[n, 2, :, pl.ds(0, half)], zr1.at[n, 0], at_ctx(up, a)),
            mail.push(wsend.at[n, 2, :, pl.ds(half, half)], zr1.at[n, 1], at_ctx(down, a)),
        )
        for dz in (1, 3, 0):
            weight_block(n, head, dz)
        return keys

    def weight_second(n, keys):
        top, bottom = pl.ds(0, half), pl.ds(half, half)
        mail.arrive(keys[0])
        wsend[n, 1, :, top] = (wsend[n, 1, :, top].astype(F32) + zr1[n, 0].astype(F32)).astype(BF)
        one = mail.push(wsend.at[n, 1], zr2.at[n, 0], at_ctx(up, a))
        mail.arrive(keys[1])
        wsend[n, 3, :, bottom] = (wsend[n, 3, :, bottom].astype(F32) + zr1[n, 1].astype(F32)).astype(BF)
        return one, mail.push(wsend.at[n, 3], zr2.at[n, 1], at_ctx(down, a))

    def weight_third(n, head, keys):
        for k in keys:
            mail.arrive(k)
        for j in range(3):
            grad_feat[j, :, cols(head)] = (
                wsend[n, 0, j].astype(F32) + zr2[n, 0, j].astype(F32) + zr2[n, 1, j].astype(F32)
            )

    ring = [weight_first(0, a)]
    mail.arrive(to_mate)
    ring.append(weight_first(1, mate))
    spread_shifts(shifts, pr, HALO - MRLEN + TILE, -1)
    tap_grads(shifts, mg, lines)
    small[pl.ds(0, MRLEN)] = lines[...].reshape(MRLEN, DH).astype(BF)
    small[pl.ds(MRLEN, short_part.shape[0])] = short_part[...]
    mail.arrive(first)
    relay = mail.push(fgall.at[far, :, near_rows], fgall.at[far, :, near_rows], at_ctx(z, mate))
    second = mail.push(fg.at[:, near_rows], fgall.at[a, :, near_rows], at_ctx(z, far))
    small_in = [mail.push(small, slots.at[d - 1], at_ctx(turn(z, d, SLABS), a)) for d in range(1, SLABS)]
    ring[0] = weight_second(0, ring[0])
    ring[1] = weight_second(1, ring[1])
    mail.arrive(relay)

    for j in range(3):
        for h in range(HEADS):
            fgm[j, :, pl.ds(h * DH, DH)] = fgall[h, j, rows(a, ROWS)]

    for load in loads:
        load.wait()

    def term_block(dc):
        for r in range(2):
            columns = rows(r * 4 + turn(col, dc, 4), WIDTH)
            out = jnp.zeros((ROWS, WIDTH), F32)
            for j in range(3):
                out += lax.dot_general(
                    fgm[j], w[j, columns], (((1,), (1,)), ((), ())), preferred_element_type=F32
                )
            tsend[dc, r] = out.astype(BF)

    top, bottom = pl.ds(0, half), pl.ds(half, half)
    term_block(2)
    from_left = mail.push(tsend.at[2, :, top], xr1.at[0], {"col": right})
    from_right = mail.push(tsend.at[2, :, bottom], xr1.at[1], {"col": left})
    term_block(1)
    term_block(3)
    mail.arrive(from_left)
    tsend[1, :, top] = (tsend[1, :, top].astype(F32) + xr1[0].astype(F32)).astype(BF)
    from_left = mail.push(tsend.at[1], xr2.at[0], {"col": right})
    mail.arrive(from_right)
    tsend[3, :, bottom] = (tsend[3, :, bottom].astype(F32) + xr1[1].astype(F32)).astype(BF)
    from_right = mail.push(tsend.at[3], xr2.at[1], {"col": left})
    home_sg = []
    for d in range(1, HEADS):
        to = turn(a, d, HEADS)
        home_sg.append(mail.push(sg.at[rows(to, ROWS)], sgh.at[:, cols(a)], at_ctx(z, to)))
        mail.push(dk.at[rows(to, ROWS)], dk_home.at[:, cols(a)], at_ctx(z, to))
    mail.keep(sg.at[rows(a, ROWS)], sgh.at[:, cols(a)])
    mail.keep(dk.at[rows(a, ROWS)], dk_home.at[:, cols(a)])
    term_block(0)

    mail.arrive(second)
    relay = mail.push(fgall.at[far, :, far_rows], fgall.at[far, :, far_rows], at_ctx(z, mate))
    ring.append(weight_first(2, far))
    mail.arrive(relay)
    ring.append(weight_first(3, far_mate))
    ring[2] = weight_second(2, ring[2])
    ring[3] = weight_second(3, ring[3])

    for k in small_in:
        mail.arrive(k)
    total[...] = (small_sum(small, slots)).astype(BF)
    for d in range(1, HEADS):
        mail.push(total, small_home.at[:, cols(a)], at_ctx(z, turn(a, d, HEADS)))
    mail.keep(total, small_home.at[:, cols(a)])

    mail.arrive(from_left)
    mail.arrive(from_right)

    def term_sum(r):
        return tsend[0, r].astype(F32) + xr2[0, r].astype(F32) + xr2[1, r].astype(F32)

    ysend[...] = term_sum(1 - row).astype(BF)
    across = mail.push(ysend, yr, {"row": 1 - row})
    weight_third(0, a, ring[0])
    weight_third(1, mate, ring[1])
    for k in home_sg:
        mail.arrive(k)
    mail.settle()
    mail.arrive(across)
    grad_input[...] = (sgh[...].astype(F32) + term_sum(row) + yr[...].astype(F32)).astype(BF)
    weight_third(2, far, ring[2])
    weight_third(3, far_mate, ring[3])
    mail.finish()


def small_sum(small, slots):
    return small[...].astype(F32) + sum(slots[d].astype(F32) for d in range(SLABS - 1))


def finale(fg, sg, dk, short_part, mg, pr, parts, weights):
    lines = MRLEN + short_part.shape[0]
    any_space, vmem = pl.BlockSpec(memory_space=pl.ANY), pl.BlockSpec(memory_space=pltpu.VMEM)
    remotes = 3 + 3 + 6 + 16 + 2 + 4 + 3 + 1
    return pl.pallas_call(
        finale_kernel,
        out_shape=[
            shape(ROWS, WIDTH),
            shape(3, ROWS, WIDTH, kind=F32),
            shape(ROWS, WIDTH),
            shape(lines, WIDTH),
        ],
        in_specs=[any_space] * 3 + [vmem] * 3 + [any_space] * 5,
        out_specs=[vmem, vmem, any_space, any_space],
        scratch_shapes=[
            pltpu.VMEM(weights.shape, BF),
            pltpu.VMEM((SLAB, SLABS * ROWS), BF),
            pltpu.VMEM((SLABS * ROWS, SLAB), BF),
            pltpu.VMEM((HEADS, 3, SLAB, DH), BF),
            pltpu.VMEM((3, ROWS, WIDTH), BF),
            pltpu.VMEM((HEADS, SLABS, 3, ROWS, DH), BF),
            pltpu.VMEM((HEADS, 2, 3, ROWS // 2, DH), BF),
            pltpu.VMEM((HEADS, 2, 3, ROWS, DH), BF),
            pltpu.VMEM((4, 2, ROWS, WIDTH), BF),
            pltpu.VMEM((2, 2, ROWS // 2, WIDTH), BF),
            pltpu.VMEM((2, 2, ROWS, WIDTH), BF),
            pltpu.VMEM((ROWS, WIDTH), BF),
            pltpu.VMEM((ROWS, WIDTH), BF),
            pltpu.VMEM((ROWS, WIDTH), BF),
            pltpu.VMEM((SLABS - 1, lines, DH), BF),
            pltpu.VMEM((lines, DH), BF),
            pltpu.VMEM((lines, DH), BF),
            pltpu.VMEM((TILE, SLAB + TAIL + MRLEN - TILE, DH), F32),
            pltpu.VMEM((TAPS, TILE, DH), F32),
            pltpu.SemaphoreType.DMA((remotes,)),
            pltpu.SemaphoreType.DMA((remotes,)),
            pltpu.SemaphoreType.DMA((11,)),
        ],
        compiler_params=pltpu.CompilerParams(
            collective_id=5, has_side_effects=True, vmem_limit_bytes=56 << 20
        ),
    )(fg, sg, dk, short_part, mg, pr, *parts, weights)


def deliver_kernel(block, grad_q, grad_k, grad_in, grad_feat, small, block_o, in_o, feat_o, short_o, mr_o, q_o, k_o):
    feat_o[...] = grad_feat[...]

    @pl.when(pl.program_id(0) == 0)
    def _():
        block_o[...] = block[...]
        in_o[...] = grad_in[...]
        q_o[...] = grad_q[...]
        k_o[...] = grad_k[...]
        mr_o[...] = small[pl.ds(0, MRLEN)].astype(F32)
        for j in range(3):
            short_o[j] = small[pl.ds(MRLEN + 16 * j, 16)].astype(F32)[:SHORT]


def deliver(*ins):
    def fixed(*dims):
        return pl.BlockSpec(dims, lambda j: (0,) * len(dims))

    mine = fixed(ROWS, WIDTH)
    feat = pl.BlockSpec((1, ROWS, WIDTH), lambda j: (j, 0, 0))
    out = shape(ROWS, WIDTH)
    return pl.pallas_call(
        deliver_kernel,
        grid=(3,),
        out_shape=[
            out,
            out,
            shape(3, ROWS, WIDTH, kind=F32),
            shape(3, SHORT, WIDTH, kind=F32),
            shape(MRLEN, WIDTH, kind=F32),
            out,
            out,
        ],
        in_specs=[mine] * 4 + [feat, fixed(*ins[-1].shape)],
        out_specs=[mine, mine, feat, fixed(3, SHORT, WIDTH), fixed(MRLEN, WIDTH), mine, mine],
        compiler_params=pltpu.CompilerParams(vmem_limit_bytes=32 << 20),
    )(*ins)


def local(tokens, w_feat, short_filter, mr_filter, queries, key_rows, cotangent):
    weights = w_feat.transpose(1, 0, 2)
    short_taps = short_filter.transpose(1, 0, 2)
    th, qh, ch, chalo, fx, kfull, *pieces = front(tokens, queries, key_rows, cotangent, weights)
    token_parts = [pieces[0]]
    for d in range(1, HEADS):
        route = [(s * HEADS + a, s * HEADS + (a + d) % HEADS) for s in range(SLABS) for a in range(HEADS)]
        token_parts.append(lax.ppermute(pieces[d], "ctx", route))
    block, grad_queries, sg, fg, dk, short_part, mg, pr = middle(
        fx, th, qh, kfull, ch, chalo, short_taps, mr_filter
    )
    grad_input, grad_feat, grad_keys, small = finale(fg, sg, dk, short_part, mg, pr, token_parts, weights)
    block_out, grad_input, grad_feat, grad_short, grad_mr, grad_queries, grad_keys = deliver(
        block, grad_queries, grad_keys, grad_input, grad_feat, small
    )
    grad_feat, grad_short = grad_feat.transpose(1, 0, 2), grad_short.transpose(1, 0, 2)
    return (block_out, grad_input, grad_feat, grad_short, grad_mr, grad_queries, grad_keys)


def solution(mesh):
    placed = (
        P("ctx", ("row", "col")),
        P(None, None, ("row", "col")),
        P(None, None, ("row", "col")),
        P(None, ("row", "col")),
        P("ctx", ("row", "col")),
        P("ctx", ("row", "col")),
        P("ctx", ("row", "col")),
    )
    return jax.shard_map(
        local,
        mesh=mesh,
        in_specs=placed,
        out_specs=(
            P("ctx", ("row", "col")),
            P("ctx", ("row", "col")),
            P("ctx", None, ("row", "col")),
            P(None, None, ("row", "col")),
            P(None, ("row", "col")),
            P("ctx", ("row", "col")),
            P("ctx", ("row", "col")),
        ),
        check_vma=False,
    )
```

```python
import functools

import jax
import jax.numpy as jnp
from jax import lax
from jax.experimental import pallas as pl
from jax.experimental.pallas import tpu as pltpu
from jax.sharding import PartitionSpec as P

DH = 128
SHORT = 7
MRLEN = 128
HALO = 144
TAIL = 16
ROWS = 256
HEADS = 4
SLABS = 4
SLAB = ROWS * HEADS
EXT = HALO + SLAB + HALO
WIDTH = HEADS * DH
MESH = pl.DeviceIdType.MESH
BF = jnp.bfloat16
F32 = jnp.float32


def place():
    ctx = lax.axis_index("ctx")
    return lax.div(ctx, HEADS), lax.rem(ctx, HEADS)


def turn(index, step, size):
    return lax.rem(index + (step + size), size)


def at_ctx(z, a):
    return {"ctx": z * HEADS + a}


def cols(index, width=DH):
    return pl.ds(pl.multiple_of(index * width, width), width)


def rows(index, height, offset=0):
    return pl.ds(pl.multiple_of(index * height + offset, 16), height)


def greet(devices):
    barrier = pltpu.get_barrier_semaphore()
    for device in devices:
        pl.semaphore_signal(barrier, inc=1, device_id=device, device_id_type=MESH)
    return functools.partial(pl.semaphore_wait, barrier, len(devices))


class Courier:
    def __init__(self, send, recv, local):
        self.send, self.recv, self.local = send, recv, local
        self.remote, self.here = [], []
        self.arrived = set()
        self.settled = 0

    def push(self, src, dst, device):
        k = len(self.remote)
        copy = pltpu.make_async_remote_copy(
            src_ref=src,
            dst_ref=dst,
            send_sem=self.send.at[k],
            recv_sem=self.recv.at[k],
            device_id=device,
            device_id_type=MESH,
        )
        copy.start()
        self.remote.append(copy)
        return k

    def keep(self, src, dst):
        copy = pltpu.make_async_copy(src, dst, self.local.at[len(self.here)])
        copy.start()
        self.here.append(copy)

    def arrive(self, k):
        if k not in self.arrived:
            self.arrived.add(k)
            self.remote[k].wait_recv()

    def finish(self):
        for k in range(len(self.remote)):
            self.arrive(k)
        for copy in self.remote:
            copy.wait_send()
        self.settle()

    def settle(self):
        for copy in self.here[self.settled :]:
            copy.wait()
        self.settled = len(self.here)


def shape(*dims, kind=BF):
    return jax.ShapeDtypeStruct(dims, kind)


def slab_gather(mail, part, whole, z, a):
    up, down = turn(z, 1, SLABS), turn(z, -1, SLABS)
    mine = whole.at[rows(z, SLAB)]
    mail.keep(part, mine)
    return mail.push(part, mine, at_ctx(up, a)), mail.push(part, mine, at_ctx(down, a))


def slab_relay(mail, whole, z, a, from_down, from_up):
    up, down = turn(z, 1, SLABS), turn(z, -1, SLABS)
    half = SLAB // 2
    mail.arrive(from_down)
    lower = whole.at[pl.ds(pl.multiple_of(down * SLAB, 16), half)]
    mail.push(lower, lower, at_ctx(up, a))
    mail.arrive(from_up)
    upper = whole.at[pl.ds(pl.multiple_of(up * SLAB + half, 16), half)]
    mail.push(upper, upper, at_ctx(down, a))


def front_kernel(
    tokens, queries, keys, cot, weights,
    th, qh, ch, chalo, fx, kfull, piece0, piece1, piece2, piece3,
    full, w, acc, feats, kh, send, recv, loc,
):
    mail = Courier(send, recv, loc)
    z, a = place()
    row, col = lax.axis_index("row"), lax.axis_index("col")
    other = 1 - row
    right, left, across = turn(col, 1, 4), turn(col, -1, 4), turn(col, 2, 4)
    up, down = turn(z, 1, SLABS), turn(z, -1, SLABS)
    greeted = greet(
        [{"row": other}, {"col": right}, {"col": left}]
        + [at_ctx(z, turn(a, d, HEADS)) for d in range(1, HEADS)]
        + [at_ctx(s, b) for s in (up, down) for b in range(HEADS)]
    )
    for j in range(3):
        mail.keep(weights.at[j], w.at[j])
    full[:, cols(row * 4 + col, WIDTH)] = tokens[...]
    kh[rows(a, ROWS)] = keys[:, cols(a)]
    acc[...] = jnp.zeros_like(acc)
    greeted()

    def block(r, c):
        return full.at[:, cols(r * 4 + c, WIDTH)]

    def half(r, c, h):
        return full.at[pl.ds(h * (ROWS // 2), ROWS // 2), cols(r * 4 + c, WIDTH)]

    def project(r, c, lhs=None):
        lhs = full[:, cols(r * 4 + c, WIDTH)] if lhs is None else lhs
        for j in range(3):
            acc[j] += jnp.dot(lhs, w[j, rows(r * 4 + c, WIDTH)], preferred_element_type=F32)

    vertical = mail.push(tokens, block(row, col), {"row": other})
    fr = mail.push(tokens, block(row, col), {"col": right})
    fl = mail.push(tokens, block(row, col), {"col": left})
    mail.settle()
    project(row, col, tokens[...])
    mail.arrive(vertical)
    gr = mail.push(block(other, col), block(other, col), {"col": right})
    gl = mail.push(block(other, col), block(other, col), {"col": left})
    key_parts = []
    for src, dst in ((keys, kh), (tokens, th), (queries, qh), (cot, ch)):
        for d in range(1, HEADS):
            to = turn(a, d, HEADS)
            k = mail.push(src.at[:, cols(to)], dst.at[rows(a, ROWS)], at_ctx(z, to))
            if dst is kh:
                key_parts.append(k)
        if dst is not kh:
            mail.keep(src.at[:, cols(a)], dst.at[rows(a, ROWS)])
    project(other, col)
    relays = []
    for r, from_left, from_right in ((row, fr, fl), (other, gr, gl)):
        mail.arrive(from_left)
        relays.append(mail.push(half(r, left, 0), half(r, left, 0), {"col": right}))
        mail.arrive(from_right)
        relays.append(mail.push(half(r, right, 1), half(r, right, 1), {"col": left}))
        project(r, left)
        project(r, right)
        if r is row:
            for k in key_parts:
                mail.arrive(k)
            gathered = slab_gather(mail, kh, kfull, z, a)
    for r, first in ((row, 0), (other, 2)):
        mail.arrive(relays[first])
        mail.arrive(relays[first + 1])
        project(r, across)
    slab_relay(mail, kfull, z, a, *gathered)
    feats[...] = acc[...].astype(BF)

    for d in range(1, HEADS):
        to = turn(a, d, HEADS)
        mail.push(feats.at[:, :, cols(to)], fx.at[:, rows(a, ROWS, HALO)], at_ctx(z, to))
    mail.keep(feats.at[:, :, cols(a)], fx.at[:, rows(a, ROWS, HALO)])

    n = len(mail.remote)

    def edge(src, dst, k, b, device):
        return pltpu.make_async_remote_copy(
            src_ref=src,
            dst_ref=dst,
            send_sem=mail.send.at[k + 3 * b],
            recv_sem=mail.recv.at[k],
            device_id=device,
            device_id_type=MESH,
        )

    def first_rows(b):
        lanes = pl.ds(b * DH, DH)
        return (
            edge(feats.at[:, pl.ds(0, HALO), lanes], fx.at[:, pl.ds(HALO + SLAB, HALO)], n, b, at_ctx(down, b)),
            edge(cot.at[pl.ds(0, HALO), lanes], chalo, n + 1, b, at_ctx(down, b)),
        )

    def last_rows(b):
        lanes = pl.ds(b * DH, DH)
        return (edge(feats.at[:, pl.ds(ROWS - HALO, HALO), lanes], fx.at[:, pl.ds(0, HALO)], n + 2, b, at_ctx(up, b)),)

    @pl.when(a == 0)
    def _():
        for b in range(HEADS):
            for copy in first_rows(b):
                copy.start()

    @pl.when(a == HEADS - 1)
    def _():
        for b in range(HEADS):
            for copy in last_rows(b):
                copy.start()

    for d, piece in enumerate((piece0, piece1, piece2, piece3)):
        for s in range(SLABS):
            mail.keep(full.at[:, cols(s * HEADS + turn(a, d, HEADS), ROWS)], piece.at[:, pl.ds(s * ROWS, ROWS)])
    mail.finish()
    for copy in first_rows(0) + last_rows(0):
        copy.wait_recv()

    @pl.when(a == 0)
    def _():
        for b in range(HEADS):
            for copy in first_rows(b):
                copy.wait_send()

    @pl.when(a == HEADS - 1)
    def _():
        for b in range(HEADS):
            for copy in last_rows(b):
                copy.wait_send()


def front(tokens, queries, keys, cot, weights):
    any_space, vmem = pl.BlockSpec(memory_space=pl.ANY), pl.BlockSpec(memory_space=pltpu.VMEM)
    head = shape(SLAB, DH)
    outs = [
        head,
        head,
        head,
        shape(HALO, DH),
        shape(3, EXT, DH),
        shape(SLABS * SLAB, DH),
    ] + [shape(ROWS, SLABS * ROWS)] * HEADS
    remotes = 3 + 2 + 12 + 4 + 3 + 4 + 12
    return pl.pallas_call(
        front_kernel,
        out_shape=outs,
        in_specs=[vmem] * 4 + [any_space],
        out_specs=[any_space] * len(outs),
        scratch_shapes=[
            pltpu.VMEM((ROWS, 8 * WIDTH), BF),
            pltpu.VMEM(weights.shape, BF),
            pltpu.VMEM((3, ROWS, WIDTH), F32),
            pltpu.VMEM((3, ROWS, WIDTH), BF),
            pltpu.VMEM((SLAB, DH), BF),
            pltpu.SemaphoreType.DMA((remotes,)),
            pltpu.SemaphoreType.DMA((remotes,)),
            pltpu.SemaphoreType.DMA((3 + 3 + 1 + 1 + HEADS * SLABS,)),
        ],
        compiler_params=pltpu.CompilerParams(
            collective_id=0, has_side_effects=True, vmem_limit_bytes=56 << 20
        ),
    )(tokens, queries, keys, cot, weights)


def around(z, a):
    return [at_ctx(turn(z, d, SLABS), a) for d in range(1, SLABS)] + [
        at_ctx(z, turn(a, d, HEADS)) for d in range(1, HEADS)
    ]


def home(mail, src, dst, z, a):
    for d in range(1, HEADS):
        to = turn(a, d, HEADS)
        mail.push(src.at[rows(to, ROWS)], dst.at[:, cols(a)], at_ctx(z, to))
    mail.keep(src.at[rows(a, ROWS)], dst.at[:, cols(a)])


CHUNK = 512


def dot(x, y):
    return jnp.dot(x, y, preferred_element_type=F32)


def dot_t(x, y):
    return lax.dot_general(x, y, (((1,), (1,)), ((), ())), preferred_element_type=F32)


GROUP = 40
TILE = 8
TAPS = MRLEN // TILE
SPAN = 13


def spread_taps(spread, taps, a):
    for i in range(MRLEN):
        spread[i % TILE, i // TILE] = jnp.broadcast_to(taps[pl.ds(i, 1), cols(a)], (TILE, DH))


def spread_shifts(shifts, rows_of, first, sign):
    count = shifts.shape[1]
    for r in range(TILE):
        shifts[r] = rows_of[pl.ds(first + sign * r, count)]


def long_filter(shifts, spread, backward, store):
    def step(g, carry):
        base = pl.multiple_of(g * (SPAN * TILE), TILE)

        def shift(r, totals):
            totals = list(totals)
            taps = [spread[r, m] for m in range(TAPS)]
            for t in range(SPAN + TAPS - 1):
                tile = shifts[r, pl.ds(base + t * TILE, TILE)]
                for n in range(SPAN):
                    m = t - n if backward else n + TAPS - 1 - t
                    if 0 <= m < TAPS:
                        totals[n] += taps[m] * tile
            return tuple(totals)

        totals = lax.fori_loop(0, TILE, shift, tuple(jnp.zeros((TILE, DH), F32) for _ in range(SPAN)))
        for n in range(SPAN):
            store(pl.ds(base + n * TILE, TILE), totals[n])
        return carry

    lax.fori_loop(0, (SLAB + TAIL) // (SPAN * TILE), step, 0)


def tap_grads(shifts, grads, lines):
    count = 16

    def shift(r, carry):
        def step(g, sums):
            sums = list(sums)
            base = pl.multiple_of(g * (count * TILE), TILE)
            own = [grads[pl.ds(base + n * TILE, TILE)] for n in range(count)]
            for t in range(count + TAPS - 1):
                tile = shifts[r, pl.ds(base + t * TILE, TILE)]
                for n in range(count):
                    m = n + TAPS - 1 - t
                    if 0 <= m < TAPS:
                        sums[m] += own[n] * tile
            return tuple(sums)

        zero = tuple(jnp.zeros((TILE, DH), F32) for _ in range(TAPS))
        sums = lax.fori_loop(0, SLAB // (count * TILE), step, zero)
        for m in range(TAPS):
            lines[m, pl.ds(r, 1)] = jnp.sum(sums[m], axis=0, keepdims=True)
        return carry

    lax.fori_loop(0, TILE, shift, 0)


def hyena(z, a, fx, short, tok, stream, qm, km, vm, lm, pr, feat, shifts, spread):
    keep_head = (z > 0).astype(F32)
    keep_tail = (z < SLABS - 1).astype(F32)
    for j in range(3):
        feat[j, pl.ds(0, HALO)] = fx[j, pl.ds(0, HALO)].astype(F32) * keep_head
        feat[j, pl.ds(HALO, SLAB)] = fx[j, pl.ds(HALO, SLAB)].astype(F32)
        feat[j, pl.ds(HALO + SLAB, HALO)] = fx[j, pl.ds(HALO + SLAB, HALO)].astype(F32) * keep_tail

    taps = [[short[j, pl.ds(s, 1), cols(a)] for s in range(SHORT)] for j in range(3)]

    def mixed(j, base, count):
        total = taps[j][0] * feat[j, pl.ds(base, count)]
        for s in range(1, SHORT):
            total += taps[j][s] * feat[j, pl.ds(base - s, count)]
        return total

    pr[pl.ds(0, 16)] = jnp.zeros((16, DH), F32)

    def head_step(g, carry):
        base = pl.multiple_of(16 + g * 16, 16)
        pr[pl.ds(base, 16)] = (mixed(1, base, 16) * mixed(2, base, 16)).astype(BF).astype(F32)
        return carry

    lax.fori_loop(0, (HALO - 16) // 16, head_step, 0)

    def mix_step(g, carry):
        base = pl.multiple_of(HALO + g * GROUP, 8)
        here = pl.ds(pl.multiple_of(g * GROUP, 8), GROUP)
        key, value = mixed(1, base, GROUP), mixed(2, base, GROUP)
        km[here] = key
        vm[here] = value
        qm[here] = mixed(0, base, GROUP)
        pr[pl.ds(base, GROUP)] = (key * value).astype(BF).astype(F32)
        return carry

    lax.fori_loop(0, (SLAB + TAIL) // GROUP, mix_step, 0)

    def tail_step(g, carry):
        here = pl.multiple_of(SLAB + TAIL + g * 16, 16)
        qm[pl.ds(here, 16)] = mixed(0, here + HALO, 16)
        return carry

    lax.fori_loop(0, (HALO - TAIL) // 16, tail_step, 0)
    spread_shifts(shifts, pr, HALO - MRLEN + TILE, -1)

    def store(here, total):
        lm[here] = total

    long_filter(shifts, spread, False, store)
    own = pl.ds(0, SLAB)
    stream[...] = (tok[...].astype(F32) + qm[own] * lm[own]).astype(BF)


def back(z, a, dv, ch, chalo, short, qm, km, vm, lm, feat, sg, fg, short_part, mg, stack, shifts, spread):
    keep_tail = (z < SLABS - 1).astype(F32)
    own, halo = pl.ds(0, SLAB), pl.ds(SLAB, HALO)
    grad = (ch[...].astype(F32) + dv[own]).astype(BF)
    sg[...] = grad
    mg[own] = (grad.astype(F32) * qm[own]).astype(BF).astype(F32)
    grad_halo = (chalo[...].astype(F32) + dv[halo]).astype(BF).astype(F32) * keep_tail
    mg[halo] = (grad_halo * qm[halo]).astype(BF).astype(F32)
    stack[0, own] = grad.astype(F32) * lm[own]
    stack[0, pl.ds(SLAB, TAIL)] = grad_halo[:TAIL] * lm[pl.ds(SLAB, TAIL)]
    spread_shifts(shifts, mg, 0, 1)

    def store(here, total):
        stack[1, here] = total * vm[here]
        stack[2, here] = total * km[here]

    long_filter(shifts, spread, True, store)
    for j in range(3):
        taps = [short[j, pl.ds(s, 1), cols(a)] for s in range(SHORT)]

        def short_step(g, sums):
            base = pl.multiple_of(g * 32, 32)
            line = stack[j, pl.ds(base, 32)]
            total = taps[0] * line
            for s in range(1, SHORT):
                total += taps[s] * stack[j, pl.ds(base + s, 32)]
            fg[j, pl.ds(base, 32)] = total.astype(BF)
            out = []
            for s in range(SHORT):
                term = line * feat[j, pl.ds(base + HALO - s, 32)]
                out.append(sums[s] + (term[0:8] + term[8:16] + term[16:24] + term[24:32]))
            return tuple(out)

        sums = lax.fori_loop(0, SLAB // 32, short_step, tuple(jnp.zeros((8, DH), F32) for _ in range(SHORT)))
        lines = [jnp.sum(t, axis=0, keepdims=True) for t in sums]
        short_part[pl.ds(16 * j, 16)] = jnp.concatenate(lines + [jnp.zeros((16 - SHORT, DH), F32)], axis=0).astype(BF)


def middle_kernel(
    fx, tok, q, k, ct, chalo, short, mr, piece1, piece2, piece3,
    block_home, dq_home, part1, part2, part3, sg, fg, dk, short_part, mg, pr,
    stream, v, kt, vt, st, pt, tops, outs, ctt, cs, delta, block, dq, dqt, dv, dka, edge, dv_out, dk_out, dv_in, dk_in,
    qm, km, vm, lm, feat, stack, shifts, spread,
    dv_send, dv_recv, dk_send, dk_recv, send, recv, loc,
):
    mail = Courier(send, recv, loc)
    z, a = place()
    scale = DH ** -0.5
    gain = scale * 1.4426950408889634
    mine = rows(z, SLAB)
    up, down = at_ctx(turn(z, 1, SLABS), a), at_ctx(turn(z, -1, SLABS), a)
    greeted = greet(around(z, a))
    spread_taps(spread, mr, a)

    def turn_keys(s, carry):
        kt[:, cols(s, SLAB)] = k[rows(s, SLAB)].T
        return carry

    hyena(z, a, fx, short, tok, stream, qm, km, vm, lm, pr, feat, shifts, spread)
    greeted()
    from_down = mail.push(stream, v.at[mine], up)
    from_up = mail.push(stream, v.at[mine], down)
    v[mine] = stream[...]
    for d, (piece, part) in enumerate(((piece1, part1), (piece2, part2), (piece3, part3)), 1):
        mail.push(piece, part, at_ctx(z, turn(a, d, HEADS)))

    def lanes_of(i):
        return pl.ds(i * ROWS, ROWS)

    def slots(c):
        return pl.ds(pl.multiple_of(SLAB + c * CHUNK, CHUNK), CHUNK)

    def keys_of(c):
        return pl.ds(pl.multiple_of(c * CHUNK, CHUNK), CHUNK)

    after = lax.broadcasted_iota(jnp.int32, (ROWS, ROWS), 0) > lax.broadcasted_iota(jnp.int32, (ROWS, ROWS), 1)
    for i in range(HEADS):
        span = ROWS * (i + 1)
        scores = dot_t(k[pl.ds(pl.multiple_of(z * SLAB, SLAB), span)], q[lanes_of(i)])
        corner = jnp.where(after, -1e30, scores[span - ROWS :])
        top = jnp.max(corner, axis=0, keepdims=True)
        if i:
            top = jnp.maximum(top, jnp.max(scores[: span - ROWS], axis=0, keepdims=True))
            st[pl.ds(0, span - ROWS), lanes_of(i)] = scores[: span - ROWS]
        st[pl.ds(span - ROWS, ROWS), lanes_of(i)] = corner
        tops[:, lanes_of(i)] = top

    def score_step(c, top):
        past = dot_t(k[keys_of(c)], q[...])
        st[slots(c)] = past
        return jnp.maximum(top, jnp.max(past, axis=0, keepdims=True))

    top = lax.fori_loop(0, z * (SLAB // CHUNK), score_step, tops[...]) * gain

    half = SLAB // 2
    mail.arrive(from_down)
    lower = v.at[pl.ds(pl.multiple_of(turn(z, -1, SLABS) * SLAB, SLAB), half)]
    low = mail.push(lower, lower, up)
    mail.arrive(from_up)
    upper = v.at[pl.ds(pl.multiple_of(turn(z, 1, SLABS) * SLAB + half, half), half)]
    high = mail.push(upper, upper, down)

    for i in range(HEADS):
        span = ROWS * (i + 1)
        p = jnp.exp2(st[pl.ds(0, span), lanes_of(i)] * gain - top[:, i * ROWS : (i + 1) * ROWS])
        tops[:, lanes_of(i)] = jnp.sum(p, axis=0, keepdims=True)
        pt[pl.ds(0, span), lanes_of(i)] = p.astype(BF)

    def weigh_step(c, total):
        p = jnp.exp2(st[slots(c)] * gain - top)
        pt[slots(c)] = p.astype(BF)
        return total + jnp.sum(p, axis=0, keepdims=True)

    inverse = 1.0 / lax.fori_loop(0, z * (SLAB // CHUNK), weigh_step, tops[...])
    lax.fori_loop(0, z + 1, turn_keys, 0)
    mail.arrive(low)
    mail.arrive(high)

    def turn_values(s, carry):
        vt[:, cols(s, SLAB)] = v[rows(s, SLAB)].T
        return carry

    lax.fori_loop(0, z + 1, turn_values, 0)
    for i in range(HEADS):
        span = ROWS * (i + 1)
        outs[:, lanes_of(i)] = dot(vt[:, pl.ds(pl.multiple_of(z * SLAB, SLAB), span)], pt[pl.ds(0, span), lanes_of(i)])

    def attend_step(c, carry):
        outs[...] += dot(vt[:, keys_of(c)], pt[slots(c)])
        return carry

    lax.fori_loop(0, z * (SLAB // CHUNK), attend_step, 0)
    out = outs[...] * inverse
    ctt[...] = (ct[...].astype(F32).T * inverse).astype(BF)
    cs[...] = ctt[...].T
    delta[...] = jnp.sum(ctt[...].astype(F32) * out, axis=0, keepdims=True)

    for i in reversed(range(HEADS)):
        span = ROWS * (i + 1)
        part = dot(pt[pl.ds(0, span), lanes_of(i)], cs[lanes_of(i)])
        if i == HEADS - 1:
            dv[pl.ds(0, SLAB)] = part
        else:
            dv[pl.ds(0, span)] += part
    dv[pl.ds(SLAB, HALO)] = jnp.zeros((HALO, DH), F32)
    edge[...] = dv[pl.ds(0, HALO)].astype(BF)

    def parcel(d, to, kind):
        src, dst, sent, got = ((dv_out, dv_in, dv_send, dv_recv), (dk_out, dk_in, dk_send, dk_recv))[kind]
        return pltpu.make_async_remote_copy(
            src_ref=src.at[d - 1],
            dst_ref=dst.at[d - 1],
            send_sem=sent.at[d - 1],
            recv_sem=got.at[d - 1],
            device_id=at_ctx(to, a),
            device_id_type=MESH,
        )

    def value_step(d, carry):
        s = z - d
        dv_out[d - 1, pl.ds(SLAB, HALO)] = edge[...]
        for n in range(SLAB // CHUNK):
            part = dot(pt[slots(s * (SLAB // CHUNK) + n)], cs[...]).astype(BF)
            dv_out[d - 1, pl.ds(n * CHUNK, CHUNK)] = part
            if n == 0:
                edge[...] = part[:HALO]
        parcel(d, s, 0).start()
        return carry

    lax.fori_loop(1, z + 1, value_step, 0)
    block[...] = (stream[...].astype(F32) + out.T).astype(BF)
    home(mail, block, block_home, z, a)

    for i in reversed(range(HEADS)):
        span = ROWS * (i + 1)
        here = pl.ds(pl.multiple_of(z * SLAB, SLAB), span)
        p = pt[pl.ds(0, span), lanes_of(i)]
        dp = dot(v[here], ctt[:, lanes_of(i)])
        ds = (p.astype(F32) * (dp - delta[:, lanes_of(i)])).astype(BF)
        part = dot(ds, q[lanes_of(i)])
        dqt[:, lanes_of(i)] = dot(kt[:, here], ds)
        if i == HEADS - 1:
            dka[...] = part
        else:
            dka[pl.ds(0, span)] += part

    def key_step(d, carry):
        s = z - d
        for n in range(SLAB // CHUNK):
            c = s * (SLAB // CHUNK) + n
            dp = dot(v[keys_of(c)], ctt[...])
            ds = (pt[slots(c)].astype(F32) * (dp - delta[...])).astype(BF)
            dk_out[d - 1, pl.ds(n * CHUNK, CHUNK)] = (dot(ds, q[...]) * scale).astype(BF)
            dqt[...] += dot(kt[:, keys_of(c)], ds)
        parcel(d, s, 1).start()
        return carry

    lax.fori_loop(1, z + 1, key_step, 0)
    dq[...] = (dqt[...].T * scale).astype(BF)
    home(mail, dq, dq_home, z, a)

    def add_values(d, carry):
        parcel(d, turn(z, d, SLABS), 0).wait_recv()
        dv[...] += dv_in[d - 1].astype(F32)
        return carry

    lax.fori_loop(1, SLABS - z, add_values, 0)
    back(z, a, dv, ct, chalo, short, qm, km, vm, lm, feat, sg, fg, short_part, mg, stack, shifts, spread)
    dka[...] = dka[...] * scale

    def add_keys(d, carry):
        parcel(d, turn(z, d, SLABS), 1).wait_recv()
        dka[...] += dk_in[d - 1].astype(F32)
        return carry

    lax.fori_loop(1, SLABS - z, add_keys, 0)
    dk[...] = dka[...].astype(BF)
    mail.finish()

    def sent_step(d, carry):
        for kind in range(2):
            parcel(d, turn(z, -d, SLABS), kind).wait_send()
        return carry

    lax.fori_loop(1, z + 1, sent_step, 0)


def middle(fx, tok, q, k, ct, chalo, short, mr, *pieces):
    any_space, vmem = pl.BlockSpec(memory_space=pl.ANY), pl.BlockSpec(memory_space=pltpu.VMEM)
    whole = SLABS * SLAB
    mine, head = shape(ROWS, WIDTH), shape(SLAB, DH)
    dma = pltpu.SemaphoreType.DMA
    return pl.pallas_call(
        middle_kernel,
        out_shape=[
            mine,
            mine,
            *pieces,
            head,
            shape(3, SLAB, DH),
            head,
            shape(3 * 16, DH),
            shape(SLAB + HALO, DH, kind=F32),
            shape(HALO + SLAB + TAIL, DH, kind=F32),
        ],
        in_specs=[vmem] * 8 + [any_space] * 3,
        out_specs=[any_space] * 5 + [vmem] * 6,
        scratch_shapes=[
            pltpu.VMEM((SLAB, DH), BF),
            pltpu.VMEM((whole, DH), BF),
            pltpu.VMEM((DH, whole), BF),
            pltpu.VMEM((DH, whole), BF),
            pltpu.VMEM((whole, SLAB), F32),
            pltpu.VMEM((whole, SLAB), BF),
            pltpu.VMEM((1, SLAB), F32),
            pltpu.VMEM((DH, SLAB), F32),
            pltpu.VMEM((DH, SLAB), BF),
            pltpu.VMEM((SLAB, DH), BF),
            pltpu.VMEM((1, SLAB), F32),
            pltpu.VMEM((SLAB, DH), BF),
            pltpu.VMEM((SLAB, DH), BF),
            pltpu.VMEM((DH, SLAB), F32),
            pltpu.VMEM((SLAB + HALO, DH), F32),
            pltpu.VMEM((SLAB, DH), F32),
            pltpu.VMEM((HALO, DH), BF),
            pltpu.VMEM((SLABS - 1, SLAB + HALO, DH), BF),
            pltpu.VMEM((SLABS - 1, SLAB, DH), BF),
            pltpu.VMEM((SLABS - 1, SLAB + HALO, DH), BF),
            pltpu.VMEM((SLABS - 1, SLAB, DH), BF),
            pltpu.VMEM((SLAB + HALO, DH), F32),
            pltpu.VMEM((SLAB + TAIL, DH), F32),
            pltpu.VMEM((SLAB + TAIL, DH), F32),
            pltpu.VMEM((SLAB + TAIL, DH), F32),
            pltpu.VMEM((3, EXT, DH), F32),
            pltpu.VMEM((3, SLAB + TAIL, DH), F32),
            pltpu.VMEM((TILE, SLAB + TAIL + MRLEN - TILE, DH), F32),
            pltpu.VMEM((TILE, TAPS, TILE, DH), F32),
            dma((SLABS - 1,)),
            dma((SLABS - 1,)),
            dma((SLABS - 1,)),
            dma((SLABS - 1,)),
            dma((13,)),
            dma((13,)),
            dma((2,)),
        ],
        compiler_params=pltpu.CompilerParams(
            collective_id=2, has_side_effects=True, vmem_limit_bytes=58 << 20
        ),
    )(fx, tok, q, k, ct, chalo, short, mr, *pieces)


def finale_kernel(
    fg, sg, dk, short_part, mg, pr, part0, part1, part2, part3, weights,
    grad_input, grad_feat, dk_home, small_home,
    w, tq, tqt, fgall, fgm, wsend, zr1, zr2, tsend, xr1, xr2, yr, ysend, sgh, slots, small, total, shifts, lines,
    send, recv, loc,
):
    mail = Courier(send, recv, loc)
    z, a = place()
    row, col = lax.axis_index("row"), lax.axis_index("col")
    side, core = lax.div(a, 2), lax.rem(a, 2)
    mate, far, far_mate = side * 2 + 1 - core, (1 - side) * 2 + core, (1 - side) * 2 + 1 - core
    up, down = turn(z, 1, SLABS), turn(z, -1, SLABS)
    right, left = turn(col, 1, 4), turn(col, -1, 4)
    half = ROWS // 2
    pair = 2 * ROWS

    mail.keep(fg, fgall.at[a])
    for d, part in enumerate((part0, part1, part2, part3)):
        mail.keep(part, tq.at[rows(turn(a, -d, HEADS), ROWS)])
    greeted = greet(around(z, a) + [{"row": 1 - row}, {"col": right}, {"col": left}])
    loads = [pltpu.make_async_copy(weights.at[j], w.at[j], loc.at[8 + j]) for j in range(3)]
    for load in loads:
        load.start()
    greeted()

    near_rows, far_rows = rows(side, pair), rows(1 - side, pair)
    direct = [
        mail.push(fg.at[:, rows(to, ROWS)], fgall.at[a, :, rows(to, ROWS)], at_ctx(z, to)) for to in (far, far_mate)
    ]
    to_mate = mail.push(fg, fgall.at[a], at_ctx(z, mate))
    second = mail.push(fg.at[:, near_rows], fgall.at[a, :, near_rows], at_ctx(z, far))
    mail.settle()

    for b in range(SLABS):
        tqt[pl.ds(b * ROWS, ROWS)] = tq[:, pl.ds(b * ROWS, ROWS)].T

    def weight_block(n, head, dz):
        rhs = jnp.concatenate([fgall[head, j] for j in range(3)], axis=1)
        lhs = tqt[rows(turn(z, dz, SLABS), ROWS)]
        out = jnp.dot(lhs, rhs, preferred_element_type=F32)
        for j in range(3):
            wsend[n, dz, j] = out[:, j * DH : (j + 1) * DH].astype(BF)

    def weight_first(n, head):
        weight_block(n, head, 2)
        keys = (
            mail.push(wsend.at[n, 2, :, pl.ds(0, half)], zr1.at[n, 0], at_ctx(up, a)),
            mail.push(wsend.at[n, 2, :, pl.ds(half, half)], zr1.at[n, 1], at_ctx(down, a)),
        )
        for dz in (1, 3, 0):
            weight_block(n, head, dz)
        return keys

    def weight_second(n, keys):
        top, bottom = pl.ds(0, half), pl.ds(half, half)
        mail.arrive(keys[0])
        wsend[n, 1, :, top] = (wsend[n, 1, :, top].astype(F32) + zr1[n, 0].astype(F32)).astype(BF)
        one = mail.push(wsend.at[n, 1], zr2.at[n, 0], at_ctx(up, a))
        mail.arrive(keys[1])
        wsend[n, 3, :, bottom] = (wsend[n, 3, :, bottom].astype(F32) + zr1[n, 1].astype(F32)).astype(BF)
        return one, mail.push(wsend.at[n, 3], zr2.at[n, 1], at_ctx(down, a))

    def weight_third(n, head, keys):
        for k in keys:
            mail.arrive(k)
        for j in range(3):
            grad_feat[j, :, cols(head)] = (
                wsend[n, 0, j].astype(F32) + zr2[n, 0, j].astype(F32) + zr2[n, 1, j].astype(F32)
            )

    ring = [weight_first(0, a)]
    mail.arrive(to_mate)
    ring.append(weight_first(1, mate))
    spread_shifts(shifts, pr, HALO - MRLEN + TILE, -1)
    tap_grads(shifts, mg, lines)
    small[pl.ds(0, MRLEN)] = lines[...].reshape(MRLEN, DH).astype(BF)
    small[pl.ds(MRLEN, short_part.shape[0])] = short_part[...]
    small_in = [mail.push(small, slots.at[d - 1], at_ctx(turn(z, d, SLABS), a)) for d in range(1, SLABS)]
    for k in direct:
        mail.arrive(k)
    relays = [
        mail.push(fgall.at[h, :, rows(a, ROWS)], fgall.at[h, :, rows(a, ROWS)], at_ctx(z, mate))
        for h in (far, far_mate)
    ]

    for n in range(2):
        ring[n] = weight_second(n, ring[n])
    for j in range(3):
        for h in range(HEADS):
            fgm[j, :, pl.ds(h * DH, DH)] = fgall[h, j, rows(a, ROWS)]
    for load in loads:
        load.wait()

    top, bottom = pl.ds(0, half), pl.ds(half, half)
    shares = (1 - row, row)

    def term_block(dc, n):
        columns = rows(shares[n] * 4 + turn(col, dc, 4), WIDTH)
        out = jnp.zeros((ROWS, WIDTH), F32)
        for j in range(3):
            out += lax.dot_general(fgm[j], w[j, columns], (((1,), (1,)), ((), ())), preferred_element_type=F32)
        tsend[dc, n] = out.astype(BF)

    firsts, seconds = [], []
    for n in range(2):
        term_block(2, n)
        firsts.append(
            (
                mail.push(tsend.at[2, n, top], xr1.at[0, n], {"col": right}),
                mail.push(tsend.at[2, n, bottom], xr1.at[1, n], {"col": left}),
            )
        )
    for n in range(2):
        term_block(1, n)
        term_block(3, n)
        mail.arrive(firsts[n][0])
        tsend[1, n, top] = (tsend[1, n, top].astype(F32) + xr1[0, n].astype(F32)).astype(BF)
        from_left = mail.push(tsend.at[1, n], xr2.at[0, n], {"col": right})
        mail.arrive(firsts[n][1])
        tsend[3, n, bottom] = (tsend[3, n, bottom].astype(F32) + xr1[1, n].astype(F32)).astype(BF)
        seconds.append((from_left, mail.push(tsend.at[3, n], xr2.at[1, n], {"col": left})))
    home_sg = []
    for d in range(1, HEADS):
        to = turn(a, d, HEADS)
        home_sg.append(mail.push(sg.at[rows(to, ROWS)], sgh.at[:, cols(a)], at_ctx(z, to)))
        mail.push(dk.at[rows(to, ROWS)], dk_home.at[:, cols(a)], at_ctx(z, to))
    mail.keep(sg.at[rows(a, ROWS)], sgh.at[:, cols(a)])
    mail.keep(dk.at[rows(a, ROWS)], dk_home.at[:, cols(a)])
    term_block(0, 0)
    term_block(0, 1)
    mail.arrive(second)
    relays.append(mail.push(fgall.at[far, :, far_rows], fgall.at[far, :, far_rows], at_ctx(z, mate)))
    for k in relays[:2]:
        mail.arrive(k)
    ring.append(weight_first(2, far))
    mail.arrive(relays[2])
    ring.append(weight_first(3, far_mate))

    def term_sum(n):
        for k in seconds[n]:
            mail.arrive(k)
        return tsend[0, n].astype(F32) + xr2[0, n].astype(F32) + xr2[1, n].astype(F32)

    ysend[...] = term_sum(0).astype(BF)
    across = mail.push(ysend, yr, {"row": 1 - row})
    ring[2] = weight_second(2, ring[2])
    ring[3] = weight_second(3, ring[3])

    for k in small_in:
        mail.arrive(k)
    total[...] = (small_sum(small, slots)).astype(BF)
    for d in range(1, HEADS):
        mail.push(total, small_home.at[:, cols(a)], at_ctx(z, turn(a, d, HEADS)))
    mail.keep(total, small_home.at[:, cols(a)])

    weight_third(0, a, ring[0])
    weight_third(1, mate, ring[1])
    for k in home_sg:
        mail.arrive(k)
    mail.settle()
    mail.arrive(across)
    grad_input[...] = (sgh[...].astype(F32) + term_sum(1) + yr[...].astype(F32)).astype(BF)
    weight_third(2, far, ring[2])
    weight_third(3, far_mate, ring[3])
    mail.finish()


def small_sum(small, slots):
    return small[...].astype(F32) + sum(slots[d].astype(F32) for d in range(SLABS - 1))


def finale(fg, sg, dk, short_part, mg, pr, parts, weights):
    lines = MRLEN + short_part.shape[0]
    any_space, vmem = pl.BlockSpec(memory_space=pl.ANY), pl.BlockSpec(memory_space=pltpu.VMEM)
    remotes = 1 + 3 + 3 + 6 + 6 + 16 + 8 + 1
    return pl.pallas_call(
        finale_kernel,
        out_shape=[
            shape(ROWS, WIDTH),
            shape(3, ROWS, WIDTH, kind=F32),
            shape(ROWS, WIDTH),
            shape(lines, WIDTH),
        ],
        in_specs=[any_space] * 3 + [vmem] * 3 + [any_space] * 5,
        out_specs=[vmem, vmem, any_space, any_space],
        scratch_shapes=[
            pltpu.VMEM(weights.shape, BF),
            pltpu.VMEM((SLAB, SLABS * ROWS), BF),
            pltpu.VMEM((SLABS * ROWS, SLAB), BF),
            pltpu.VMEM((HEADS, 3, SLAB, DH), BF),
            pltpu.VMEM((3, ROWS, WIDTH), BF),
            pltpu.VMEM((HEADS, SLABS, 3, ROWS, DH), BF),
            pltpu.VMEM((HEADS, 2, 3, ROWS // 2, DH), BF),
            pltpu.VMEM((HEADS, 2, 3, ROWS, DH), BF),
            pltpu.VMEM((4, 2, ROWS, WIDTH), BF),
            pltpu.VMEM((2, 2, ROWS // 2, WIDTH), BF),
            pltpu.VMEM((2, 2, ROWS, WIDTH), BF),
            pltpu.VMEM((ROWS, WIDTH), BF),
            pltpu.VMEM((ROWS, WIDTH), BF),
            pltpu.VMEM((ROWS, WIDTH), BF),
            pltpu.VMEM((SLABS - 1, lines, DH), BF),
            pltpu.VMEM((lines, DH), BF),
            pltpu.VMEM((lines, DH), BF),
            pltpu.VMEM((TILE, SLAB + TAIL + MRLEN - TILE, DH), F32),
            pltpu.VMEM((TAPS, TILE, DH), F32),
            pltpu.SemaphoreType.DMA((remotes,)),
            pltpu.SemaphoreType.DMA((remotes,)),
            pltpu.SemaphoreType.DMA((11,)),
        ],
        compiler_params=pltpu.CompilerParams(
            collective_id=5, has_side_effects=True, vmem_limit_bytes=56 << 20
        ),
    )(fg, sg, dk, short_part, mg, pr, *parts, weights)


def deliver_kernel(block, grad_q, grad_k, grad_in, grad_feat, small, block_o, in_o, feat_o, short_o, mr_o, q_o, k_o):
    feat_o[...] = grad_feat[...]

    @pl.when(pl.program_id(0) == 0)
    def _():
        block_o[...] = block[...]
        in_o[...] = grad_in[...]
        q_o[...] = grad_q[...]
        k_o[...] = grad_k[...]
        mr_o[...] = small[pl.ds(0, MRLEN)].astype(F32)
        for j in range(3):
            short_o[j] = small[pl.ds(MRLEN + 16 * j, 16)].astype(F32)[:SHORT]


def deliver(*ins):
    def fixed(*dims):
        return pl.BlockSpec(dims, lambda j: (0,) * len(dims))

    mine = fixed(ROWS, WIDTH)
    feat = pl.BlockSpec((1, ROWS, WIDTH), lambda j: (j, 0, 0))
    out = shape(ROWS, WIDTH)
    return pl.pallas_call(
        deliver_kernel,
        grid=(3,),
        out_shape=[
            out,
            out,
            shape(3, ROWS, WIDTH, kind=F32),
            shape(3, SHORT, WIDTH, kind=F32),
            shape(MRLEN, WIDTH, kind=F32),
            out,
            out,
        ],
        in_specs=[mine] * 4 + [feat, fixed(*ins[-1].shape)],
        out_specs=[mine, mine, feat, fixed(3, SHORT, WIDTH), fixed(MRLEN, WIDTH), mine, mine],
        compiler_params=pltpu.CompilerParams(vmem_limit_bytes=60 << 20),
    )(*ins)


def local(tokens, w_feat, short_filter, mr_filter, queries, key_rows, cotangent):
    weights = w_feat.transpose(1, 0, 2)
    short_taps = short_filter.transpose(1, 0, 2)
    th, qh, ch, chalo, fx, kfull, *pieces = front(tokens, queries, key_rows, cotangent, weights)
    block, grad_queries, *token_parts, sg, fg, dk, short_part, mg, pr = middle(
        fx, th, qh, kfull, ch, chalo, short_taps, mr_filter, *pieces[1:]
    )
    grad_input, grad_feat, grad_keys, small = finale(fg, sg, dk, short_part, mg, pr, [pieces[0], *token_parts], weights)
    block_out, grad_input, grad_feat, grad_short, grad_mr, grad_queries, grad_keys = deliver(
        block, grad_queries, grad_keys, grad_input, grad_feat, small
    )
    grad_feat, grad_short = grad_feat.transpose(1, 0, 2), grad_short.transpose(1, 0, 2)
    return (block_out, grad_input, grad_feat, grad_short, grad_mr, grad_queries, grad_keys)


def solution(mesh):
    placed = (
        P("ctx", ("row", "col")),
        P(None, None, ("row", "col")),
        P(None, None, ("row", "col")),
        P(None, ("row", "col")),
        P("ctx", ("row", "col")),
        P("ctx", ("row", "col")),
        P("ctx", ("row", "col")),
    )
    return jax.shard_map(
        local,
        mesh=mesh,
        in_specs=placed,
        out_specs=(
            P("ctx", ("row", "col")),
            P("ctx", ("row", "col")),
            P("ctx", None, ("row", "col")),
            P(None, None, ("row", "col")),
            P(None, ("row", "col")),
            P("ctx", ("row", "col")),
            P("ctx", ("row", "col")),
        ),
        check_vma=False,
    )
```

```python
import functools

import jax
import jax.numpy as jnp
from jax import lax
from jax.experimental import pallas as pl
from jax.experimental.pallas import tpu as pltpu
from jax.sharding import PartitionSpec as P

DH = 128
SHORT = 7
MRLEN = 128
HALO = 144
TAIL = 16
ROWS = 256
HEADS = 4
SLABS = 4
SLAB = ROWS * HEADS
EXT = HALO + SLAB + HALO
WIDTH = HEADS * DH
MESH = pl.DeviceIdType.MESH
BF = jnp.bfloat16
F32 = jnp.float32


def place():
    ctx = lax.axis_index("ctx")
    return lax.div(ctx, HEADS), lax.rem(ctx, HEADS)


def turn(index, step, size):
    return lax.rem(index + (step + size), size)


def at_ctx(z, a):
    return {"ctx": z * HEADS + a}


def cols(index, width=DH):
    return pl.ds(pl.multiple_of(index * width, width), width)


def rows(index, height, offset=0):
    return pl.ds(pl.multiple_of(index * height + offset, 16), height)


def greet(devices):
    barrier = pltpu.get_barrier_semaphore()
    for device in devices:
        pl.semaphore_signal(barrier, inc=1, device_id=device, device_id_type=MESH)
    return functools.partial(pl.semaphore_wait, barrier, len(devices))


class Courier:
    def __init__(self, send, recv, local):
        self.send, self.recv, self.local = send, recv, local
        self.remote, self.here = [], []
        self.arrived = set()
        self.settled = 0

    def push(self, src, dst, device):
        k = len(self.remote)
        copy = pltpu.make_async_remote_copy(
            src_ref=src,
            dst_ref=dst,
            send_sem=self.send.at[k],
            recv_sem=self.recv.at[k],
            device_id=device,
            device_id_type=MESH,
        )
        copy.start()
        self.remote.append(copy)
        return k

    def keep(self, src, dst):
        copy = pltpu.make_async_copy(src, dst, self.local.at[len(self.here)])
        copy.start()
        self.here.append(copy)

    def arrive(self, k):
        if k not in self.arrived:
            self.arrived.add(k)
            self.remote[k].wait_recv()

    def finish(self):
        for k in range(len(self.remote)):
            self.arrive(k)
        for copy in self.remote:
            copy.wait_send()
        self.settle()

    def settle(self):
        for copy in self.here[self.settled :]:
            copy.wait()
        self.settled = len(self.here)


def shape(*dims, kind=BF):
    return jax.ShapeDtypeStruct(dims, kind)


def slab_gather(mail, part, whole, z, a):
    up, down = turn(z, 1, SLABS), turn(z, -1, SLABS)
    mine = whole.at[rows(z, SLAB)]
    mail.keep(part, mine)
    return mail.push(part, mine, at_ctx(up, a)), mail.push(part, mine, at_ctx(down, a))


def slab_relay(mail, whole, z, a, from_down, from_up):
    up, down = turn(z, 1, SLABS), turn(z, -1, SLABS)
    half = SLAB // 2
    mail.arrive(from_down)
    lower = whole.at[pl.ds(pl.multiple_of(down * SLAB, 16), half)]
    mail.push(lower, lower, at_ctx(up, a))
    mail.arrive(from_up)
    upper = whole.at[pl.ds(pl.multiple_of(up * SLAB + half, 16), half)]
    mail.push(upper, upper, at_ctx(down, a))


def front_phase(
    greeted, w, tokens, queries, keys, cot, weights, th, qh, ch, chalo, fx, kfull, full, acc, feats, kh, send, recv, loc,
):
    mail = Courier(send, recv, loc)
    z, a = place()
    row, col = lax.axis_index("row"), lax.axis_index("col")
    other = 1 - row
    right, left, across = turn(col, 1, 4), turn(col, -1, 4), turn(col, 2, 4)
    up, down = turn(z, 1, SLABS), turn(z, -1, SLABS)
    for j in range(3):
        mail.keep(weights.at[j], w.at[j])
    full[:, cols(row * 4 + col, WIDTH)] = tokens[...]
    kh[rows(a, ROWS)] = keys[:, cols(a)]
    acc[...] = jnp.zeros_like(acc)
    greeted()

    def block(r, c):
        return full.at[:, cols(r * 4 + c, WIDTH)]

    def half(r, c, h):
        return full.at[pl.ds(h * (ROWS // 2), ROWS // 2), cols(r * 4 + c, WIDTH)]

    def project(r, c, lhs=None):
        lhs = full[:, cols(r * 4 + c, WIDTH)] if lhs is None else lhs
        for j in range(3):
            acc[j] += jnp.dot(lhs, w[j, rows(r * 4 + c, WIDTH)], preferred_element_type=F32)

    vertical = mail.push(tokens, block(row, col), {"row": other})
    fr = mail.push(tokens, block(row, col), {"col": right})
    fl = mail.push(tokens, block(row, col), {"col": left})
    mail.settle()
    project(row, col, tokens[...])
    mail.arrive(vertical)
    gr = mail.push(block(other, col), block(other, col), {"col": right})
    gl = mail.push(block(other, col), block(other, col), {"col": left})
    key_parts = []
    for src, dst in ((keys, kh), (tokens, th), (queries, qh), (cot, ch)):
        for d in range(1, HEADS):
            to = turn(a, d, HEADS)
            k = mail.push(src.at[:, cols(to)], dst.at[rows(a, ROWS)], at_ctx(z, to))
            if dst is kh:
                key_parts.append(k)
        if dst is not kh:
            mail.keep(src.at[:, cols(a)], dst.at[rows(a, ROWS)])
    project(other, col)
    relays = []
    for r, from_left, from_right in ((row, fr, fl), (other, gr, gl)):
        mail.arrive(from_left)
        relays.append(mail.push(half(r, left, 0), half(r, left, 0), {"col": right}))
        mail.arrive(from_right)
        relays.append(mail.push(half(r, right, 1), half(r, right, 1), {"col": left}))
        project(r, left)
        project(r, right)
        if r is row:
            for k in key_parts:
                mail.arrive(k)
            gathered = slab_gather(mail, kh, kfull, z, a)
    for r, first in ((row, 0), (other, 2)):
        mail.arrive(relays[first])
        mail.arrive(relays[first + 1])
        project(r, across)
    slab_relay(mail, kfull, z, a, *gathered)
    feats[...] = acc[...].astype(BF)

    for d in range(1, HEADS):
        to = turn(a, d, HEADS)
        mail.push(feats.at[:, :, cols(to)], fx.at[:, rows(a, ROWS, HALO)], at_ctx(z, to))
    mail.keep(feats.at[:, :, cols(a)], fx.at[:, rows(a, ROWS, HALO)])

    n = len(mail.remote)

    def edge(src, dst, k, b, device):
        return pltpu.make_async_remote_copy(
            src_ref=src,
            dst_ref=dst,
            send_sem=mail.send.at[k + 3 * b],
            recv_sem=mail.recv.at[k],
            device_id=device,
            device_id_type=MESH,
        )

    def first_rows(b):
        lanes = pl.ds(b * DH, DH)
        return (
            edge(feats.at[:, pl.ds(0, HALO), lanes], fx.at[:, pl.ds(HALO + SLAB, HALO)], n, b, at_ctx(down, b)),
            edge(cot.at[pl.ds(0, HALO), lanes], chalo, n + 1, b, at_ctx(down, b)),
        )

    def last_rows(b):
        lanes = pl.ds(b * DH, DH)
        return (edge(feats.at[:, pl.ds(ROWS - HALO, HALO), lanes], fx.at[:, pl.ds(0, HALO)], n + 2, b, at_ctx(up, b)),)

    @pl.when(a == 0)
    def _():
        for b in range(HEADS):
            for copy in first_rows(b):
                copy.start()

    @pl.when(a == HEADS - 1)
    def _():
        for b in range(HEADS):
            for copy in last_rows(b):
                copy.start()

    mail.finish()
    for copy in first_rows(0) + last_rows(0):
        copy.wait_recv()

    @pl.when(a == 0)
    def _():
        for b in range(HEADS):
            for copy in first_rows(b):
                copy.wait_send()

    @pl.when(a == HEADS - 1)
    def _():
        for b in range(HEADS):
            for copy in last_rows(b):
                copy.wait_send()


def around(z, a):
    return [at_ctx(turn(z, d, SLABS), a) for d in range(1, SLABS)] + [
        at_ctx(z, turn(a, d, HEADS)) for d in range(1, HEADS)
    ]


def home(mail, src, dst, z, a):
    for d in range(1, HEADS):
        to = turn(a, d, HEADS)
        mail.push(src.at[rows(to, ROWS)], dst.at[:, cols(a)], at_ctx(z, to))
    mail.keep(src.at[rows(a, ROWS)], dst.at[:, cols(a)])


CHUNK = 512


def dot(x, y):
    return jnp.dot(x, y, preferred_element_type=F32)


def dot_t(x, y):
    return lax.dot_general(x, y, (((1,), (1,)), ((), ())), preferred_element_type=F32)


GROUP = 40
TILE = 8
TAPS = MRLEN // TILE
SPAN = 13


def spread_taps(spread, taps, a):
    for i in range(MRLEN):
        spread[i % TILE, i // TILE] = jnp.broadcast_to(taps[pl.ds(i, 1), cols(a)], (TILE, DH))


def spread_shifts(shifts, rows_of, first, sign):
    count = shifts.shape[1]
    for r in range(TILE):
        shifts[r] = rows_of[pl.ds(first + sign * r, count)]


def long_filter(shifts, spread, backward, store):
    def step(g, carry):
        base = pl.multiple_of(g * (SPAN * TILE), TILE)

        def shift(r, totals):
            totals = list(totals)
            taps = [spread[r, m] for m in range(TAPS)]
            for t in range(SPAN + TAPS - 1):
                tile = shifts[r, pl.ds(base + t * TILE, TILE)]
                for n in range(SPAN):
                    m = t - n if backward else n + TAPS - 1 - t
                    if 0 <= m < TAPS:
                        totals[n] += taps[m] * tile
            return tuple(totals)

        totals = lax.fori_loop(0, TILE, shift, tuple(jnp.zeros((TILE, DH), F32) for _ in range(SPAN)))
        for n in range(SPAN):
            store(pl.ds(base + n * TILE, TILE), totals[n])
        return carry

    lax.fori_loop(0, (SLAB + TAIL) // (SPAN * TILE), step, 0)


def tap_grads(shifts, grads, lines):
    count = 16

    def shift(r, carry):
        def step(g, sums):
            sums = list(sums)
            base = pl.multiple_of(g * (count * TILE), TILE)
            own = [grads[pl.ds(base + n * TILE, TILE)] for n in range(count)]
            for t in range(count + TAPS - 1):
                tile = shifts[r, pl.ds(base + t * TILE, TILE)]
                for n in range(count):
                    m = n + TAPS - 1 - t
                    if 0 <= m < TAPS:
                        sums[m] += own[n] * tile
            return tuple(sums)

        zero = tuple(jnp.zeros((TILE, DH), F32) for _ in range(TAPS))
        sums = lax.fori_loop(0, SLAB // (count * TILE), step, zero)
        for m in range(TAPS):
            lines[m, pl.ds(r, 1)] = jnp.sum(sums[m], axis=0, keepdims=True)
        return carry

    lax.fori_loop(0, TILE, shift, 0)


def hyena(z, a, fx, short, tok, stream, qm, km, vm, lm, pr, feat, shifts, spread):
    keep_head = (z > 0).astype(F32)
    keep_tail = (z < SLABS - 1).astype(F32)
    for j in range(3):
        feat[j, pl.ds(0, HALO)] = fx[j, pl.ds(0, HALO)].astype(F32) * keep_head
        feat[j, pl.ds(HALO, SLAB)] = fx[j, pl.ds(HALO, SLAB)].astype(F32)
        feat[j, pl.ds(HALO + SLAB, HALO)] = fx[j, pl.ds(HALO + SLAB, HALO)].astype(F32) * keep_tail

    taps = [[short[j, pl.ds(s, 1), cols(a)] for s in range(SHORT)] for j in range(3)]

    def mixed(j, base, count):
        total = taps[j][0] * feat[j, pl.ds(base, count)]
        for s in range(1, SHORT):
            total += taps[j][s] * feat[j, pl.ds(base - s, count)]
        return total

    pr[pl.ds(0, 16)] = jnp.zeros((16, DH), F32)

    def head_step(g, carry):
        base = pl.multiple_of(16 + g * 16, 16)
        pr[pl.ds(base, 16)] = (mixed(1, base, 16) * mixed(2, base, 16)).astype(BF).astype(F32)
        return carry

    lax.fori_loop(0, (HALO - 16) // 16, head_step, 0)

    def mix_step(g, carry):
        base = pl.multiple_of(HALO + g * GROUP, 8)
        here = pl.ds(pl.multiple_of(g * GROUP, 8), GROUP)
        key, value = mixed(1, base, GROUP), mixed(2, base, GROUP)
        km[here] = key
        vm[here] = value
        qm[here] = mixed(0, base, GROUP)
        pr[pl.ds(base, GROUP)] = (key * value).astype(BF).astype(F32)
        return carry

    lax.fori_loop(0, (SLAB + TAIL) // GROUP, mix_step, 0)

    def tail_step(g, carry):
        here = pl.multiple_of(SLAB + TAIL + g * 16, 16)
        qm[pl.ds(here, 16)] = mixed(0, here + HALO, 16)
        return carry

    lax.fori_loop(0, (HALO - TAIL) // 16, tail_step, 0)
    spread_shifts(shifts, pr, HALO - MRLEN + TILE, -1)

    def store(here, total):
        lm[here] = total

    long_filter(shifts, spread, False, store)
    own = pl.ds(0, SLAB)
    stream[...] = (tok[...].astype(F32) + qm[own] * lm[own]).astype(BF)


def back(z, a, dv, ch, chalo, short, qm, km, vm, lm, feat, sg, fg, short_part, mg, stack, shifts, spread):
    keep_tail = (z < SLABS - 1).astype(F32)
    own, halo = pl.ds(0, SLAB), pl.ds(SLAB, HALO)
    grad = (ch[...].astype(F32) + dv[own]).astype(BF)
    sg[...] = grad
    mg[own] = (grad.astype(F32) * qm[own]).astype(BF).astype(F32)
    grad_halo = (chalo[...].astype(F32) + dv[halo]).astype(BF).astype(F32) * keep_tail
    mg[halo] = (grad_halo * qm[halo]).astype(BF).astype(F32)
    stack[0, own] = grad.astype(F32) * lm[own]
    stack[0, pl.ds(SLAB, TAIL)] = grad_halo[:TAIL] * lm[pl.ds(SLAB, TAIL)]
    spread_shifts(shifts, mg, 0, 1)

    def store(here, total):
        stack[1, here] = total * vm[here]
        stack[2, here] = total * km[here]

    long_filter(shifts, spread, True, store)
    for j in range(3):
        taps = [short[j, pl.ds(s, 1), cols(a)] for s in range(SHORT)]

        def short_step(g, sums):
            base = pl.multiple_of(g * 32, 32)
            line = stack[j, pl.ds(base, 32)]
            total = taps[0] * line
            for s in range(1, SHORT):
                total += taps[s] * stack[j, pl.ds(base + s, 32)]
            fg[j, pl.ds(base, 32)] = total.astype(BF)
            out = []
            for s in range(SHORT):
                term = line * feat[j, pl.ds(base + HALO - s, 32)]
                out.append(sums[s] + (term[0:8] + term[8:16] + term[16:24] + term[24:32]))
            return tuple(out)

        sums = lax.fori_loop(0, SLAB // 32, short_step, tuple(jnp.zeros((8, DH), F32) for _ in range(SHORT)))
        lines = [jnp.sum(t, axis=0, keepdims=True) for t in sums]
        short_part[pl.ds(16 * j, 16)] = jnp.concatenate(lines + [jnp.zeros((16 - SHORT, DH), F32)], axis=0).astype(BF)


def middle_phase(
    st, full, fx, tok, q, k, ct, chalo, short, mr,
    block_home, dq_home, part0, part1, part2, part3, sg, fg, dk, short_part, mg, pr,
    stream, v, kt, vt, pt, tops, outs, ctt, cs, delta, block, dq, dqt, dv, dka, edge, dv_out, dk_out, dv_in, dk_in,
    qm, km, vm, lm, feat, stack, shifts, spread,
    dv_send, dv_recv, dk_send, dk_recv, send, recv, loc,
):
    mail = Courier(send, recv, loc)
    z, a = place()
    scale = DH ** -0.5
    gain = scale * 1.4426950408889634
    mine = rows(z, SLAB)
    up, down = at_ctx(turn(z, 1, SLABS), a), at_ctx(turn(z, -1, SLABS), a)
    spread_taps(spread, mr, a)

    def turn_keys(s, carry):
        kt[:, cols(s, SLAB)] = k[rows(s, SLAB)].T
        return carry

    hyena(z, a, fx, short, tok, stream, qm, km, vm, lm, pr, feat, shifts, spread)
    from_down = mail.push(stream, v.at[mine], up)
    from_up = mail.push(stream, v.at[mine], down)
    v[mine] = stream[...]
    for d, part in enumerate((part0, part1, part2, part3)):
        to = turn(a, d, HEADS)
        for n in range(SLABS):
            piece, slot = full.at[:, cols(n * HEADS + to, ROWS)], part.at[:, pl.ds(n * ROWS, ROWS)]
            if d:
                mail.push(piece, slot, at_ctx(z, to))
            else:
                mail.keep(piece, slot)

    def lanes_of(i):
        return pl.ds(i * ROWS, ROWS)

    def slots(c):
        return pl.ds(pl.multiple_of(SLAB + c * CHUNK, CHUNK), CHUNK)

    def keys_of(c):
        return pl.ds(pl.multiple_of(c * CHUNK, CHUNK), CHUNK)

    after = lax.broadcasted_iota(jnp.int32, (ROWS, ROWS), 0) > lax.broadcasted_iota(jnp.int32, (ROWS, ROWS), 1)
    for i in range(HEADS):
        span = ROWS * (i + 1)
        scores = dot_t(k[pl.ds(pl.multiple_of(z * SLAB, SLAB), span)], q[lanes_of(i)])
        corner = jnp.where(after, -1e30, scores[span - ROWS :])
        top = jnp.max(corner, axis=0, keepdims=True)
        if i:
            top = jnp.maximum(top, jnp.max(scores[: span - ROWS], axis=0, keepdims=True))
            st[pl.ds(0, span - ROWS), lanes_of(i)] = scores[: span - ROWS]
        st[pl.ds(span - ROWS, ROWS), lanes_of(i)] = corner
        tops[:, lanes_of(i)] = top

    def score_step(c, top):
        past = dot_t(k[keys_of(c)], q[...])
        st[slots(c)] = past
        return jnp.maximum(top, jnp.max(past, axis=0, keepdims=True))

    top = lax.fori_loop(0, z * (SLAB // CHUNK), score_step, tops[...]) * gain

    half = SLAB // 2
    mail.arrive(from_down)
    lower = v.at[pl.ds(pl.multiple_of(turn(z, -1, SLABS) * SLAB, SLAB), half)]
    low = mail.push(lower, lower, up)
    mail.arrive(from_up)
    upper = v.at[pl.ds(pl.multiple_of(turn(z, 1, SLABS) * SLAB + half, half), half)]
    high = mail.push(upper, upper, down)

    for i in range(HEADS):
        span = ROWS * (i + 1)
        p = jnp.exp2(st[pl.ds(0, span), lanes_of(i)] * gain - top[:, i * ROWS : (i + 1) * ROWS])
        tops[:, lanes_of(i)] = jnp.sum(p, axis=0, keepdims=True)
        pt[pl.ds(0, span), lanes_of(i)] = p.astype(BF)

    def weigh_step(c, total):
        p = jnp.exp2(st[slots(c)] * gain - top)
        pt[slots(c)] = p.astype(BF)
        return total + jnp.sum(p, axis=0, keepdims=True)

    inverse = 1.0 / lax.fori_loop(0, z * (SLAB // CHUNK), weigh_step, tops[...])
    lax.fori_loop(0, z + 1, turn_keys, 0)
    mail.arrive(low)
    mail.arrive(high)

    def turn_values(s, carry):
        vt[:, cols(s, SLAB)] = v[rows(s, SLAB)].T
        return carry

    lax.fori_loop(0, z + 1, turn_values, 0)
    for i in range(HEADS):
        span = ROWS * (i + 1)
        outs[:, lanes_of(i)] = dot(vt[:, pl.ds(pl.multiple_of(z * SLAB, SLAB), span)], pt[pl.ds(0, span), lanes_of(i)])

    def attend_step(c, carry):
        outs[...] += dot(vt[:, keys_of(c)], pt[slots(c)])
        return carry

    lax.fori_loop(0, z * (SLAB // CHUNK), attend_step, 0)
    out = outs[...] * inverse
    ctt[...] = (ct[...].astype(F32).T * inverse).astype(BF)
    cs[...] = ctt[...].T
    delta[...] = jnp.sum(ctt[...].astype(F32) * out, axis=0, keepdims=True)

    for i in reversed(range(HEADS)):
        span = ROWS * (i + 1)
        part = dot(pt[pl.ds(0, span), lanes_of(i)], cs[lanes_of(i)])
        if i == HEADS - 1:
            dv[pl.ds(0, SLAB)] = part
        else:
            dv[pl.ds(0, span)] += part
    dv[pl.ds(SLAB, HALO)] = jnp.zeros((HALO, DH), F32)
    edge[...] = dv[pl.ds(0, HALO)].astype(BF)

    def parcel(d, to, kind):
        src, dst, sent, got = ((dv_out, dv_in, dv_send, dv_recv), (dk_out, dk_in, dk_send, dk_recv))[kind]
        return pltpu.make_async_remote_copy(
            src_ref=src.at[d - 1],
            dst_ref=dst.at[d - 1],
            send_sem=sent.at[d - 1],
            recv_sem=got.at[d - 1],
            device_id=at_ctx(to, a),
            device_id_type=MESH,
        )

    def value_step(d, carry):
        s = z - d
        dv_out[d - 1, pl.ds(SLAB, HALO)] = edge[...]
        for n in range(SLAB // CHUNK):
            part = dot(pt[slots(s * (SLAB // CHUNK) + n)], cs[...]).astype(BF)
            dv_out[d - 1, pl.ds(n * CHUNK, CHUNK)] = part
            if n == 0:
                edge[...] = part[:HALO]
        parcel(d, s, 0).start()
        return carry

    lax.fori_loop(1, z + 1, value_step, 0)
    block[...] = (stream[...].astype(F32) + out.T).astype(BF)
    home(mail, block, block_home, z, a)

    for i in reversed(range(HEADS)):
        span = ROWS * (i + 1)
        here = pl.ds(pl.multiple_of(z * SLAB, SLAB), span)
        p = pt[pl.ds(0, span), lanes_of(i)]
        dp = dot(v[here], ctt[:, lanes_of(i)])
        ds = (p.astype(F32) * (dp - delta[:, lanes_of(i)])).astype(BF)
        part = dot(ds, q[lanes_of(i)])
        dqt[:, lanes_of(i)] = dot(kt[:, here], ds)
        if i == HEADS - 1:
            dka[...] = part
        else:
            dka[pl.ds(0, span)] += part

    def key_step(d, carry):
        s = z - d
        for n in range(SLAB // CHUNK):
            c = s * (SLAB // CHUNK) + n
            dp = dot(v[keys_of(c)], ctt[...])
            ds = (pt[slots(c)].astype(F32) * (dp - delta[...])).astype(BF)
            dk_out[d - 1, pl.ds(n * CHUNK, CHUNK)] = (dot(ds, q[...]) * scale).astype(BF)
            dqt[...] += dot(kt[:, keys_of(c)], ds)
        parcel(d, s, 1).start()
        return carry

    lax.fori_loop(1, z + 1, key_step, 0)
    dq[...] = (dqt[...].T * scale).astype(BF)
    home(mail, dq, dq_home, z, a)

    def add_values(d, carry):
        parcel(d, turn(z, d, SLABS), 0).wait_recv()
        dv[...] += dv_in[d - 1].astype(F32)
        return carry

    lax.fori_loop(1, SLABS - z, add_values, 0)
    back(z, a, dv, ct, chalo, short, qm, km, vm, lm, feat, sg, fg, short_part, mg, stack, shifts, spread)
    dka[...] = dka[...] * scale

    def add_keys(d, carry):
        parcel(d, turn(z, d, SLABS), 1).wait_recv()
        dka[...] += dk_in[d - 1].astype(F32)
        return carry

    lax.fori_loop(1, SLABS - z, add_keys, 0)
    dk[...] = dka[...].astype(BF)
    mail.finish()

    def sent_step(d, carry):
        for kind in range(2):
            parcel(d, turn(z, -d, SLABS), kind).wait_send()
        return carry

    lax.fori_loop(1, z + 1, sent_step, 0)


FRONT_REFS = 13
OUT_REFS = 12


def opening_kernel(tokens, queries, keys, cot, weights, short, mr, *refs):
    outs, held, rest = refs[:OUT_REFS], refs[OUT_REFS : OUT_REFS + FRONT_REFS], refs[OUT_REFS + FRONT_REFS :]
    th, qh, ch, chalo, fx, kfull, full = held[:7]
    z, a = place()
    row, col = lax.axis_index("row"), lax.axis_index("col")
    greeted = greet(
        [{"row": 1 - row}, {"col": turn(col, 1, 4)}, {"col": turn(col, -1, 4)}]
        + [at_ctx(z, turn(a, d, HEADS)) for d in range(1, HEADS)]
        + [at_ctx(turn(z, d, SLABS), b) for d in (1, -1) for b in range(HEADS)]
        + [at_ctx(turn(z, 2, SLABS), a)]
    )
    pl.run_scoped(
        lambda w: front_phase(greeted, w, tokens, queries, keys, cot, weights, *held), pltpu.VMEM(weights.shape, BF)
    )
    pl.run_scoped(
        lambda st: middle_phase(st, full, fx, th, qh, kfull, ch, chalo, short, mr, *outs, *rest),
        pltpu.VMEM((SLABS * SLAB, SLAB), F32),
    )


def opening(tokens, queries, keys, cot, weights, short, mr):
    any_space, vmem = pl.BlockSpec(memory_space=pl.ANY), pl.BlockSpec(memory_space=pltpu.VMEM)
    whole = SLABS * SLAB
    mine, head = shape(ROWS, WIDTH), shape(SLAB, DH)
    dma = pltpu.SemaphoreType.DMA
    remotes = 3 + 2 + 12 + 4 + 2 + 2 + 3 + 12
    return pl.pallas_call(
        opening_kernel,
        out_shape=[
            mine,
            mine,
            *[shape(ROWS, SLABS * ROWS)] * HEADS,
            head,
            shape(3, SLAB, DH),
            head,
            shape(3 * 16, DH),
            shape(SLAB + HALO, DH, kind=F32),
            shape(HALO + SLAB + TAIL, DH, kind=F32),
        ],
        in_specs=[vmem] * 4 + [any_space] + [vmem] * 2,
        out_specs=[any_space] * 6 + [vmem] * 6,
        scratch_shapes=[
            pltpu.VMEM((SLAB, DH), BF),
            pltpu.VMEM((SLAB, DH), BF),
            pltpu.VMEM((SLAB, DH), BF),
            pltpu.VMEM((HALO, DH), BF),
            pltpu.VMEM((3, EXT, DH), BF),
            pltpu.VMEM((whole, DH), BF),
            pltpu.VMEM((ROWS, 8 * WIDTH), BF),
            pltpu.VMEM((3, ROWS, WIDTH), F32),
            pltpu.VMEM((3, ROWS, WIDTH), BF),
            pltpu.VMEM((SLAB, DH), BF),
            dma((remotes,)),
            dma((remotes,)),
            dma((3 + 3 + 1 + 1,)),
            pltpu.VMEM((SLAB, DH), BF),
            pltpu.VMEM((whole, DH), BF),
            pltpu.VMEM((DH, whole), BF),
            pltpu.VMEM((DH, whole), BF),
            pltpu.VMEM((whole, SLAB), BF),
            pltpu.VMEM((1, SLAB), F32),
            pltpu.VMEM((DH, SLAB), F32),
            pltpu.VMEM((DH, SLAB), BF),
            pltpu.VMEM((SLAB, DH), BF),
            pltpu.VMEM((1, SLAB), F32),
            pltpu.VMEM((SLAB, DH), BF),
            pltpu.VMEM((SLAB, DH), BF),
            pltpu.VMEM((DH, SLAB), F32),
            pltpu.VMEM((SLAB + HALO, DH), F32),
            pltpu.VMEM((SLAB, DH), F32),
            pltpu.VMEM((HALO, DH), BF),
            pltpu.VMEM((SLABS - 1, SLAB + HALO, DH), BF),
            pltpu.VMEM((SLABS - 1, SLAB, DH), BF),
            pltpu.VMEM((SLABS - 1, SLAB + HALO, DH), BF),
            pltpu.VMEM((SLABS - 1, SLAB, DH), BF),
            pltpu.VMEM((SLAB + HALO, DH), F32),
            pltpu.VMEM((SLAB + TAIL, DH), F32),
            pltpu.VMEM((SLAB + TAIL, DH), F32),
            pltpu.VMEM((SLAB + TAIL, DH), F32),
            pltpu.VMEM((3, EXT, DH), F32),
            pltpu.VMEM((3, SLAB + TAIL, DH), F32),
            pltpu.VMEM((TILE, SLAB + TAIL + MRLEN - TILE, DH), F32),
            pltpu.VMEM((TILE, TAPS, TILE, DH), F32),
            dma((SLABS - 1,)),
            dma((SLABS - 1,)),
            dma((SLABS - 1,)),
            dma((SLABS - 1,)),
            dma((22,)),
            dma((22,)),
            dma((6,)),
        ],
        compiler_params=pltpu.CompilerParams(
            collective_id=2, has_side_effects=True, vmem_limit_bytes=60 << 20
        ),
    )(tokens, queries, keys, cot, weights, short, mr)


def finale_kernel(
    fg, sg, dk, short_part, mg, pr, part0, part1, part2, part3, weights,
    grad_input, grad_feat, dk_home, small_home,
    w, tq, tqt, fgall, fgm, wsend, zr1, zr2, tsend, xr1, xr2, yr, ysend, sgh, slots, small, total, shifts, lines,
    send, recv, loc,
):
    mail = Courier(send, recv, loc)
    z, a = place()
    row, col = lax.axis_index("row"), lax.axis_index("col")
    side, core = lax.div(a, 2), lax.rem(a, 2)
    mate, far, far_mate = side * 2 + 1 - core, (1 - side) * 2 + core, (1 - side) * 2 + 1 - core
    up, down = turn(z, 1, SLABS), turn(z, -1, SLABS)
    right, left = turn(col, 1, 4), turn(col, -1, 4)
    half = ROWS // 2
    pair = 2 * ROWS

    mail.keep(fg, fgall.at[a])
    for d, part in enumerate((part0, part1, part2, part3)):
        mail.keep(part, tq.at[rows(turn(a, -d, HEADS), ROWS)])
    greeted = greet(around(z, a) + [{"row": 1 - row}, {"col": right}, {"col": left}])
    loads = [pltpu.make_async_copy(weights.at[j], w.at[j], loc.at[8 + j]) for j in range(3)]
    for load in loads:
        load.start()
    greeted()

    near_rows, far_rows = rows(side, pair), rows(1 - side, pair)
    direct = [
        mail.push(fg.at[:, rows(to, ROWS)], fgall.at[a, :, rows(to, ROWS)], at_ctx(z, to)) for to in (far, far_mate)
    ]
    to_mate = mail.push(fg, fgall.at[a], at_ctx(z, mate))
    second = mail.push(fg.at[:, near_rows], fgall.at[a, :, near_rows], at_ctx(z, far))
    mail.settle()

    for b in range(SLABS):
        tqt[pl.ds(b * ROWS, ROWS)] = tq[:, pl.ds(b * ROWS, ROWS)].T

    def weight_block(n, head, dz):
        rhs = jnp.concatenate([fgall[head, j] for j in range(3)], axis=1)
        lhs = tqt[rows(turn(z, dz, SLABS), ROWS)]
        out = jnp.dot(lhs, rhs, preferred_element_type=F32)
        for j in range(3):
            wsend[n, dz, j] = out[:, j * DH : (j + 1) * DH].astype(BF)

    def weight_first(n, head):
        weight_block(n, head, 2)
        keys = (
            mail.push(wsend.at[n, 2, :, pl.ds(0, half)], zr1.at[n, 0], at_ctx(up, a)),
            mail.push(wsend.at[n, 2, :, pl.ds(half, half)], zr1.at[n, 1], at_ctx(down, a)),
        )
        for dz in (1, 3, 0):
            weight_block(n, head, dz)
        return keys

    def weight_second(n, keys):
        top, bottom = pl.ds(0, half), pl.ds(half, half)
        mail.arrive(keys[0])
        wsend[n, 1, :, top] = (wsend[n, 1, :, top].astype(F32) + zr1[n, 0].astype(F32)).astype(BF)
        one = mail.push(wsend.at[n, 1], zr2.at[n, 0], at_ctx(up, a))
        mail.arrive(keys[1])
        wsend[n, 3, :, bottom] = (wsend[n, 3, :, bottom].astype(F32) + zr1[n, 1].astype(F32)).astype(BF)
        return one, mail.push(wsend.at[n, 3], zr2.at[n, 1], at_ctx(down, a))

    def weight_third(n, head, keys):
        for k in keys:
            mail.arrive(k)
        for j in range(3):
            grad_feat[j, :, cols(head)] = (
                wsend[n, 0, j].astype(F32) + zr2[n, 0, j].astype(F32) + zr2[n, 1, j].astype(F32)
            )

    ring = [weight_first(0, a)]
    mail.arrive(to_mate)
    ring.append(weight_first(1, mate))
    spread_shifts(shifts, pr, HALO - MRLEN + TILE, -1)
    tap_grads(shifts, mg, lines)
    small[pl.ds(0, MRLEN)] = lines[...].reshape(MRLEN, DH).astype(BF)
    small[pl.ds(MRLEN, short_part.shape[0])] = short_part[...]
    small_in = [mail.push(small, slots.at[d - 1], at_ctx(turn(z, d, SLABS), a)) for d in range(1, SLABS)]
    for k in direct:
        mail.arrive(k)
    relays = [
        mail.push(fgall.at[h, :, rows(a, ROWS)], fgall.at[h, :, rows(a, ROWS)], at_ctx(z, mate))
        for h in (far, far_mate)
    ]

    for n in range(2):
        ring[n] = weight_second(n, ring[n])
    for j in range(3):
        for h in range(HEADS):
            fgm[j, :, pl.ds(h * DH, DH)] = fgall[h, j, rows(a, ROWS)]
    for load in loads:
        load.wait()

    top, bottom = pl.ds(0, half), pl.ds(half, half)
    shares = (1 - row, row)

    def term_block(dc, n):
        columns = rows(shares[n] * 4 + turn(col, dc, 4), WIDTH)
        out = jnp.zeros((ROWS, WIDTH), F32)
        for j in range(3):
            out += lax.dot_general(fgm[j], w[j, columns], (((1,), (1,)), ((), ())), preferred_element_type=F32)
        tsend[dc, n] = out.astype(BF)

    firsts, seconds = [], []
    for n in range(2):
        term_block(2, n)
        firsts.append(
            (
                mail.push(tsend.at[2, n, top], xr1.at[0, n], {"col": right}),
                mail.push(tsend.at[2, n, bottom], xr1.at[1, n], {"col": left}),
            )
        )
    for n in range(2):
        term_block(1, n)
        term_block(3, n)
        mail.arrive(firsts[n][0])
        tsend[1, n, top] = (tsend[1, n, top].astype(F32) + xr1[0, n].astype(F32)).astype(BF)
        from_left = mail.push(tsend.at[1, n], xr2.at[0, n], {"col": right})
        mail.arrive(firsts[n][1])
        tsend[3, n, bottom] = (tsend[3, n, bottom].astype(F32) + xr1[1, n].astype(F32)).astype(BF)
        seconds.append((from_left, mail.push(tsend.at[3, n], xr2.at[1, n], {"col": left})))
    home_sg = []
    for d in range(1, HEADS):
        to = turn(a, d, HEADS)
        home_sg.append(mail.push(sg.at[rows(to, ROWS)], sgh.at[:, cols(a)], at_ctx(z, to)))
        mail.push(dk.at[rows(to, ROWS)], dk_home.at[:, cols(a)], at_ctx(z, to))
    mail.keep(sg.at[rows(a, ROWS)], sgh.at[:, cols(a)])
    mail.keep(dk.at[rows(a, ROWS)], dk_home.at[:, cols(a)])
    term_block(0, 0)
    term_block(0, 1)
    mail.arrive(second)
    relays.append(mail.push(fgall.at[far, :, far_rows], fgall.at[far, :, far_rows], at_ctx(z, mate)))
    for k in relays[:2]:
        mail.arrive(k)
    ring.append(weight_first(2, far))
    mail.arrive(relays[2])
    ring.append(weight_first(3, far_mate))

    def term_sum(n):
        for k in seconds[n]:
            mail.arrive(k)
        return tsend[0, n].astype(F32) + xr2[0, n].astype(F32) + xr2[1, n].astype(F32)

    ysend[...] = term_sum(0).astype(BF)
    across = mail.push(ysend, yr, {"row": 1 - row})
    ring[2] = weight_second(2, ring[2])
    ring[3] = weight_second(3, ring[3])

    for k in small_in:
        mail.arrive(k)
    total[...] = (small_sum(small, slots)).astype(BF)
    for d in range(1, HEADS):
        mail.push(total, small_home.at[:, cols(a)], at_ctx(z, turn(a, d, HEADS)))
    mail.keep(total, small_home.at[:, cols(a)])

    weight_third(0, a, ring[0])
    weight_third(1, mate, ring[1])
    for k in home_sg:
        mail.arrive(k)
    mail.settle()
    mail.arrive(across)
    grad_input[...] = (sgh[...].astype(F32) + term_sum(1) + yr[...].astype(F32)).astype(BF)
    weight_third(2, far, ring[2])
    weight_third(3, far_mate, ring[3])
    mail.finish()


def small_sum(small, slots):
    return small[...].astype(F32) + sum(slots[d].astype(F32) for d in range(SLABS - 1))


def finale(fg, sg, dk, short_part, mg, pr, parts, weights):
    lines = MRLEN + short_part.shape[0]
    any_space, vmem = pl.BlockSpec(memory_space=pl.ANY), pl.BlockSpec(memory_space=pltpu.VMEM)
    remotes = 1 + 3 + 3 + 6 + 6 + 16 + 8 + 1
    return pl.pallas_call(
        finale_kernel,
        out_shape=[
            shape(ROWS, WIDTH),
            shape(3, ROWS, WIDTH, kind=F32),
            shape(ROWS, WIDTH),
            shape(lines, WIDTH),
        ],
        in_specs=[any_space] * 3 + [vmem] * 3 + [any_space] * 5,
        out_specs=[vmem, vmem, any_space, any_space],
        scratch_shapes=[
            pltpu.VMEM(weights.shape, BF),
            pltpu.VMEM((SLAB, SLABS * ROWS), BF),
            pltpu.VMEM((SLABS * ROWS, SLAB), BF),
            pltpu.VMEM((HEADS, 3, SLAB, DH), BF),
            pltpu.VMEM((3, ROWS, WIDTH), BF),
            pltpu.VMEM((HEADS, SLABS, 3, ROWS, DH), BF),
            pltpu.VMEM((HEADS, 2, 3, ROWS // 2, DH), BF),
            pltpu.VMEM((HEADS, 2, 3, ROWS, DH), BF),
            pltpu.VMEM((4, 2, ROWS, WIDTH), BF),
            pltpu.VMEM((2, 2, ROWS // 2, WIDTH), BF),
            pltpu.VMEM((2, 2, ROWS, WIDTH), BF),
            pltpu.VMEM((ROWS, WIDTH), BF),
            pltpu.VMEM((ROWS, WIDTH), BF),
            pltpu.VMEM((ROWS, WIDTH), BF),
            pltpu.VMEM((SLABS - 1, lines, DH), BF),
            pltpu.VMEM((lines, DH), BF),
            pltpu.VMEM((lines, DH), BF),
            pltpu.VMEM((TILE, SLAB + TAIL + MRLEN - TILE, DH), F32),
            pltpu.VMEM((TAPS, TILE, DH), F32),
            pltpu.SemaphoreType.DMA((remotes,)),
            pltpu.SemaphoreType.DMA((remotes,)),
            pltpu.SemaphoreType.DMA((11,)),
        ],
        compiler_params=pltpu.CompilerParams(
            collective_id=5, has_side_effects=True, vmem_limit_bytes=56 << 20
        ),
    )(fg, sg, dk, short_part, mg, pr, *parts, weights)


def deliver_kernel(block, grad_q, grad_k, grad_in, grad_feat, small, block_o, in_o, feat_o, short_o, mr_o, q_o, k_o):
    feat_o[...] = grad_feat[...]
    block_o[...] = block[...]
    in_o[...] = grad_in[...]
    q_o[...] = grad_q[...]
    k_o[...] = grad_k[...]

    @pl.when(pl.program_id(0) == 0)
    def _():
        mr_o[...] = small[pl.ds(0, MRLEN)].astype(F32)
        for j in range(3):
            short_o[j] = small[pl.ds(MRLEN + 16 * j, 16)].astype(F32)[:SHORT]


def deliver(*ins):
    steps = 4

    def fixed(*dims):
        return pl.BlockSpec(dims, lambda n: (0,) * len(dims))

    mine = pl.BlockSpec((ROWS // steps, WIDTH), lambda n: (n, 0))
    feat = pl.BlockSpec((3, ROWS // steps, WIDTH), lambda n: (0, n, 0))
    out = shape(ROWS, WIDTH)
    return pl.pallas_call(
        deliver_kernel,
        grid=(steps,),
        out_shape=[
            out,
            out,
            shape(3, ROWS, WIDTH, kind=F32),
            shape(3, SHORT, WIDTH, kind=F32),
            shape(MRLEN, WIDTH, kind=F32),
            out,
            out,
        ],
        in_specs=[mine] * 4 + [feat, fixed(*ins[-1].shape)],
        out_specs=[mine, mine, feat, fixed(3, SHORT, WIDTH), fixed(MRLEN, WIDTH), mine, mine],
        compiler_params=pltpu.CompilerParams(vmem_limit_bytes=60 << 20),
    )(*ins)


def local(tokens, w_feat, short_filter, mr_filter, queries, key_rows, cotangent):
    weights = w_feat.transpose(1, 0, 2)
    short_taps = short_filter.transpose(1, 0, 2)
    block, grad_queries, *token_parts, sg, fg, dk, short_part, mg, pr = opening(
        tokens, queries, key_rows, cotangent, weights, short_taps, mr_filter
    )
    grad_input, grad_feat, grad_keys, small = finale(fg, sg, dk, short_part, mg, pr, token_parts, weights)
    block_out, grad_input, grad_feat, grad_short, grad_mr, grad_queries, grad_keys = deliver(
        block, grad_queries, grad_keys, grad_input, grad_feat, small
    )
    grad_feat, grad_short = grad_feat.transpose(1, 0, 2), grad_short.transpose(1, 0, 2)
    return (block_out, grad_input, grad_feat, grad_short, grad_mr, grad_queries, grad_keys)


def solution(mesh):
    placed = (
        P("ctx", ("row", "col")),
        P(None, None, ("row", "col")),
        P(None, None, ("row", "col")),
        P(None, ("row", "col")),
        P("ctx", ("row", "col")),
        P("ctx", ("row", "col")),
        P("ctx", ("row", "col")),
    )
    return jax.shard_map(
        local,
        mesh=mesh,
        in_specs=placed,
        out_specs=(
            P("ctx", ("row", "col")),
            P("ctx", ("row", "col")),
            P("ctx", None, ("row", "col")),
            P(None, None, ("row", "col")),
            P(None, ("row", "col")),
            P("ctx", ("row", "col")),
            P("ctx", ("row", "col")),
        ),
        check_vma=False,
    )
```

```python
import functools

import jax
import jax.numpy as jnp
from jax import lax
from jax.experimental import pallas as pl
from jax.experimental.pallas import tpu as pltpu
from jax.sharding import PartitionSpec as P

DH = 128
SHORT = 7
MRLEN = 128
HALO = 144
TAIL = 16
ROWS = 256
HEADS = 4
SLABS = 4
SLAB = ROWS * HEADS
EXT = HALO + SLAB + HALO
WIDTH = HEADS * DH
MESH = pl.DeviceIdType.MESH
BF = jnp.bfloat16
F32 = jnp.float32


def place():
    ctx = lax.axis_index("ctx")
    return lax.div(ctx, HEADS), lax.rem(ctx, HEADS)


def turn(index, step, size):
    return lax.rem(index + (step + size), size)


def at_ctx(z, a):
    return {"ctx": z * HEADS + a}


def cols(index, width=DH):
    return pl.ds(pl.multiple_of(index * width, width), width)


def rows(index, height, offset=0):
    return pl.ds(pl.multiple_of(index * height + offset, 16), height)


def greet(devices):
    barrier = pltpu.get_barrier_semaphore()
    for device in devices:
        pl.semaphore_signal(barrier, inc=1, device_id=device, device_id_type=MESH)
    return functools.partial(pl.semaphore_wait, barrier, len(devices))


class Courier:
    def __init__(self, send, recv, local):
        self.send, self.recv, self.local = send, recv, local
        self.remote, self.here = [], []
        self.arrived = set()
        self.settled = 0

    def push(self, src, dst, device):
        k = len(self.remote)
        copy = pltpu.make_async_remote_copy(
            src_ref=src,
            dst_ref=dst,
            send_sem=self.send.at[k],
            recv_sem=self.recv.at[k],
            device_id=device,
            device_id_type=MESH,
        )
        copy.start()
        self.remote.append(copy)
        return k

    def keep(self, src, dst):
        copy = pltpu.make_async_copy(src, dst, self.local.at[len(self.here)])
        copy.start()
        self.here.append(copy)

    def arrive(self, k):
        if k not in self.arrived:
            self.arrived.add(k)
            self.remote[k].wait_recv()

    def finish(self):
        for k in range(len(self.remote)):
            self.arrive(k)
        for copy in self.remote:
            copy.wait_send()
        self.settle()

    def settle(self):
        for copy in self.here[self.settled :]:
            copy.wait()
        self.settled = len(self.here)


def shape(*dims, kind=BF):
    return jax.ShapeDtypeStruct(dims, kind)


def slab_gather(mail, part, whole, z, a):
    up, down = turn(z, 1, SLABS), turn(z, -1, SLABS)
    mine = whole.at[rows(z, SLAB)]
    mail.keep(part, mine)
    return mail.push(part, mine, at_ctx(up, a)), mail.push(part, mine, at_ctx(down, a))


def slab_relay(mail, whole, z, a, from_down, from_up):
    up, down = turn(z, 1, SLABS), turn(z, -1, SLABS)
    half = SLAB // 2
    mail.arrive(from_down)
    lower = whole.at[pl.ds(pl.multiple_of(down * SLAB, 16), half)]
    mail.push(lower, lower, at_ctx(up, a))
    mail.arrive(from_up)
    upper = whole.at[pl.ds(pl.multiple_of(up * SLAB + half, 16), half)]
    mail.push(upper, upper, at_ctx(down, a))


def front_phase(
    greeted, w, tokens, queries, keys, cot, weights, th, qh, ch, chalo, fx, kfull, full, acc, feats, kh, send, recv, loc,
):
    mail = Courier(send, recv, loc)
    z, a = place()
    row, col = lax.axis_index("row"), lax.axis_index("col")
    other = 1 - row
    right, left, across = turn(col, 1, 4), turn(col, -1, 4), turn(col, 2, 4)
    up, down = turn(z, 1, SLABS), turn(z, -1, SLABS)
    for j in range(3):
        mail.keep(weights.at[j], w.at[j])
    full[:, cols(row * 4 + col, WIDTH)] = tokens[...]
    kh[rows(a, ROWS)] = keys[:, cols(a)]
    acc[...] = jnp.zeros_like(acc)
    greeted()

    half, quarter = ROWS // 2, ROWS // 4

    def piece(r, c, h):
        return full.at[pl.ds(h * half, half), cols(r * 4 + c, WIDTH)]

    def part(r, c, h, n):
        return full.at[pl.ds(h * half + n * quarter, quarter), cols(r * 4 + c, WIDTH)]

    def project(r, c, h):
        here = pl.ds(h * half, half)
        lhs = full[here, cols(r * 4 + c, WIDTH)]
        for j in range(3):
            acc[j, here] += jnp.dot(lhs, w[j, rows(r * 4 + c, WIDTH)], preferred_element_type=F32)

    def launch(h):
        src, dst = tokens.at[pl.ds(h * half, half)], piece(row, col, h)
        return [mail.push(src, dst, device) for device in ({"row": other}, {"col": right}, {"col": left})]

    def sideways(h, arrival):
        mail.arrive(arrival)
        dst = piece(other, col, h)
        return [mail.push(dst, dst, device) for device in ({"col": right}, {"col": left})]

    def relay(r, h, from_left, from_right):
        mail.arrive(from_left)
        one = mail.push(part(r, left, h, 0), part(r, left, h, 0), {"col": right})
        mail.arrive(from_right)
        return one, mail.push(part(r, right, h, 1), part(r, right, h, 1), {"col": left})

    def finish_half(h, relays):
        for r, keys_in in zip((row, other), relays):
            for k in keys_in:
                mail.arrive(k)
            project(r, across, h)
        here = pl.ds(h * half, half)
        for j in range(3):
            feats[j, here] = acc[j, here].astype(BF)
        there = pl.ds(pl.multiple_of(a * ROWS + (HALO + h * half), 16), half)
        for d in range(1, HEADS):
            to = turn(a, d, HEADS)
            mail.push(feats.at[:, here, cols(to)], fx.at[:, there], at_ctx(z, to))
        mail.keep(feats.at[:, here, cols(a)], fx.at[:, there])

    first = launch(0)
    mail.settle()
    project(row, col, 0)
    first_side = sideways(0, first[0])
    second = launch(1)
    key_parts = []
    for src, dst in ((keys, kh), (tokens, th), (queries, qh), (cot, ch)):
        for d in range(1, HEADS):
            to = turn(a, d, HEADS)
            k = mail.push(src.at[:, cols(to)], dst.at[rows(a, ROWS)], at_ctx(z, to))
            if dst is kh:
                key_parts.append(k)
        if dst is not kh:
            mail.keep(src.at[:, cols(a)], dst.at[rows(a, ROWS)])
    project(other, col, 0)
    relays = [[relay(row, 0, *first[1:])], []]
    second_side = sideways(1, second[0])
    relays[0].append(relay(other, 0, *first_side))
    for r in (row, other):
        project(r, left, 0)
        project(r, right, 0)
    relays[1].append(relay(row, 1, *second[1:]))
    finish_half(0, relays[0])
    relays[1].append(relay(other, 1, *second_side))
    for k in key_parts:
        mail.arrive(k)
    gathered = slab_gather(mail, kh, kfull, z, a)
    for r in (row, other):
        project(r, col, 1)
        project(r, left, 1)
        project(r, right, 1)
    finish_half(1, relays[1])

    n = len(mail.remote) + 2

    def edge(src, dst, k, b, device):
        return pltpu.make_async_remote_copy(
            src_ref=src,
            dst_ref=dst,
            send_sem=mail.send.at[k + 3 * b],
            recv_sem=mail.recv.at[k],
            device_id=device,
            device_id_type=MESH,
        )

    def first_rows(b):
        lanes = pl.ds(b * DH, DH)
        return (
            edge(feats.at[:, pl.ds(0, HALO), lanes], fx.at[:, pl.ds(HALO + SLAB, HALO)], n, b, at_ctx(down, b)),
            edge(cot.at[pl.ds(0, HALO), lanes], chalo, n + 1, b, at_ctx(down, b)),
        )

    def last_rows(b):
        lanes = pl.ds(b * DH, DH)
        return (edge(feats.at[:, pl.ds(ROWS - HALO, HALO), lanes], fx.at[:, pl.ds(0, HALO)], n + 2, b, at_ctx(up, b)),)

    @pl.when(a == 0)
    def _():
        for b in range(HEADS):
            for copy in first_rows(b):
                copy.start()

    @pl.when(a == HEADS - 1)
    def _():
        for b in range(HEADS):
            for copy in last_rows(b):
                copy.start()

    slab_relay(mail, kfull, z, a, *gathered)
    mail.finish()
    for copy in first_rows(0) + last_rows(0):
        copy.wait_recv()

    @pl.when(a == 0)
    def _():
        for b in range(HEADS):
            for copy in first_rows(b):
                copy.wait_send()

    @pl.when(a == HEADS - 1)
    def _():
        for b in range(HEADS):
            for copy in last_rows(b):
                copy.wait_send()


def around(z, a):
    return [at_ctx(turn(z, d, SLABS), a) for d in range(1, SLABS)] + [
        at_ctx(z, turn(a, d, HEADS)) for d in range(1, HEADS)
    ]


def home(mail, src, dst, z, a):
    for d in range(1, HEADS):
        to = turn(a, d, HEADS)
        mail.push(src.at[rows(to, ROWS)], dst.at[:, cols(a)], at_ctx(z, to))
    mail.keep(src.at[rows(a, ROWS)], dst.at[:, cols(a)])


CHUNK = 512


def dot(x, y):
    return jnp.dot(x, y, preferred_element_type=F32)


def dot_t(x, y):
    return lax.dot_general(x, y, (((1,), (1,)), ((), ())), preferred_element_type=F32)


GROUP = 40
TILE = 8
TAPS = MRLEN // TILE
SPAN = 13


def spread_taps(spread, taps, a):
    for i in range(MRLEN):
        spread[i % TILE, i // TILE] = jnp.broadcast_to(taps[pl.ds(i, 1), cols(a)], (TILE, DH))


def spread_shifts(shifts, rows_of, first, sign):
    count = shifts.shape[1]
    for r in range(TILE):
        shifts[r] = rows_of[pl.ds(first + sign * r, count)]


def long_filter(shifts, spread, backward, store):
    def step(g, carry):
        base = pl.multiple_of(g * (SPAN * TILE), TILE)

        def shift(r, totals):
            totals = list(totals)
            taps = [spread[r, m] for m in range(TAPS)]
            for t in range(SPAN + TAPS - 1):
                tile = shifts[r, pl.ds(base + t * TILE, TILE)]
                for n in range(SPAN):
                    m = t - n if backward else n + TAPS - 1 - t
                    if 0 <= m < TAPS:
                        totals[n] += taps[m] * tile
            return tuple(totals)

        totals = lax.fori_loop(0, TILE, shift, tuple(jnp.zeros((TILE, DH), F32) for _ in range(SPAN)))
        for n in range(SPAN):
            store(pl.ds(base + n * TILE, TILE), totals[n])
        return carry

    lax.fori_loop(0, (SLAB + TAIL) // (SPAN * TILE), step, 0)


def tap_grads(shifts, grads, lines):
    count = 16

    def shift(r, carry):
        def step(g, sums):
            sums = list(sums)
            base = pl.multiple_of(g * (count * TILE), TILE)
            own = [grads[pl.ds(base + n * TILE, TILE)] for n in range(count)]
            for t in range(count + TAPS - 1):
                tile = shifts[r, pl.ds(base + t * TILE, TILE)]
                for n in range(count):
                    m = n + TAPS - 1 - t
                    if 0 <= m < TAPS:
                        sums[m] += own[n] * tile
            return tuple(sums)

        zero = tuple(jnp.zeros((TILE, DH), F32) for _ in range(TAPS))
        sums = lax.fori_loop(0, SLAB // (count * TILE), step, zero)
        for m in range(TAPS):
            lines[m, pl.ds(r, 1)] = jnp.sum(sums[m], axis=0, keepdims=True)
        return carry

    lax.fori_loop(0, TILE, shift, 0)


def hyena(z, a, fx, short, tok, stream, qm, km, vm, lm, pr, feat, shifts, spread):
    keep_head = (z > 0).astype(F32)
    keep_tail = (z < SLABS - 1).astype(F32)
    for j in range(3):
        feat[j, pl.ds(0, HALO)] = fx[j, pl.ds(0, HALO)].astype(F32) * keep_head
        feat[j, pl.ds(HALO, SLAB)] = fx[j, pl.ds(HALO, SLAB)].astype(F32)
        feat[j, pl.ds(HALO + SLAB, HALO)] = fx[j, pl.ds(HALO + SLAB, HALO)].astype(F32) * keep_tail

    taps = [[short[j, pl.ds(s, 1), cols(a)] for s in range(SHORT)] for j in range(3)]

    def mixed(j, base, count):
        total = taps[j][0] * feat[j, pl.ds(base, count)]
        for s in range(1, SHORT):
            total += taps[j][s] * feat[j, pl.ds(base - s, count)]
        return total

    pr[pl.ds(0, 16)] = jnp.zeros((16, DH), F32)

    def head_step(g, carry):
        base = pl.multiple_of(16 + g * 16, 16)
        pr[pl.ds(base, 16)] = (mixed(1, base, 16) * mixed(2, base, 16)).astype(BF).astype(F32)
        return carry

    lax.fori_loop(0, (HALO - 16) // 16, head_step, 0)

    def mix_step(g, carry):
        base = pl.multiple_of(HALO + g * GROUP, 8)
        here = pl.ds(pl.multiple_of(g * GROUP, 8), GROUP)
        key, value = mixed(1, base, GROUP), mixed(2, base, GROUP)
        km[here] = key
        vm[here] = value
        qm[here] = mixed(0, base, GROUP)
        pr[pl.ds(base, GROUP)] = (key * value).astype(BF).astype(F32)
        return carry

    lax.fori_loop(0, (SLAB + TAIL) // GROUP, mix_step, 0)

    def tail_step(g, carry):
        here = pl.multiple_of(SLAB + TAIL + g * 16, 16)
        qm[pl.ds(here, 16)] = mixed(0, here + HALO, 16)
        return carry

    lax.fori_loop(0, (HALO - TAIL) // 16, tail_step, 0)
    spread_shifts(shifts, pr, HALO - MRLEN + TILE, -1)

    def store(here, total):
        lm[here] = total

    long_filter(shifts, spread, False, store)
    own = pl.ds(0, SLAB)
    stream[...] = (tok[...].astype(F32) + qm[own] * lm[own]).astype(BF)


def back(z, a, dv, ch, chalo, short, qm, km, vm, lm, feat, sg, fg, short_part, mg, stack, shifts, spread):
    keep_tail = (z < SLABS - 1).astype(F32)
    own, halo = pl.ds(0, SLAB), pl.ds(SLAB, HALO)
    grad = (ch[...].astype(F32) + dv[own]).astype(BF)
    sg[...] = grad
    mg[own] = (grad.astype(F32) * qm[own]).astype(BF).astype(F32)
    grad_halo = (chalo[...].astype(F32) + dv[halo]).astype(BF).astype(F32) * keep_tail
    mg[halo] = (grad_halo * qm[halo]).astype(BF).astype(F32)
    stack[0, own] = grad.astype(F32) * lm[own]
    stack[0, pl.ds(SLAB, TAIL)] = grad_halo[:TAIL] * lm[pl.ds(SLAB, TAIL)]
    spread_shifts(shifts, mg, 0, 1)

    def store(here, total):
        stack[1, here] = total * vm[here]
        stack[2, here] = total * km[here]

    long_filter(shifts, spread, True, store)
    for j in range(3):
        taps = [short[j, pl.ds(s, 1), cols(a)] for s in range(SHORT)]

        def short_step(g, sums):
            base = pl.multiple_of(g * 32, 32)
            line = stack[j, pl.ds(base, 32)]
            total = taps[0] * line
            for s in range(1, SHORT):
                total += taps[s] * stack[j, pl.ds(base + s, 32)]
            fg[j, pl.ds(base, 32)] = total.astype(BF)
            out = []
            for s in range(SHORT):
                term = line * feat[j, pl.ds(base + HALO - s, 32)]
                out.append(sums[s] + (term[0:8] + term[8:16] + term[16:24] + term[24:32]))
            return tuple(out)

        sums = lax.fori_loop(0, SLAB // 32, short_step, tuple(jnp.zeros((8, DH), F32) for _ in range(SHORT)))
        lines = [jnp.sum(t, axis=0, keepdims=True) for t in sums]
        short_part[pl.ds(16 * j, 16)] = jnp.concatenate(lines + [jnp.zeros((16 - SHORT, DH), F32)], axis=0).astype(BF)


def middle_phase(
    st, full, fx, tok, q, k, ct, chalo, short, mr,
    block_home, dq_home, part0, part1, part2, part3, sg, fg, dk, short_part, mg, pr,
    stream, v, kt, vt, pt, tops, outs, ctt, cs, delta, block, dq, dqt, dv, dka, edge, dv_out, dk_out, dv_in, dk_in,
    qm, km, vm, lm, feat, stack, shifts, spread,
    dv_send, dv_recv, dk_send, dk_recv, send, recv, loc,
):
    mail = Courier(send, recv, loc)
    z, a = place()
    scale = DH ** -0.5
    gain = scale * 1.4426950408889634
    mine = rows(z, SLAB)
    up, down = at_ctx(turn(z, 1, SLABS), a), at_ctx(turn(z, -1, SLABS), a)
    spread_taps(spread, mr, a)

    def turn_keys(s, carry):
        kt[:, cols(s, SLAB)] = k[rows(s, SLAB)].T
        return carry

    hyena(z, a, fx, short, tok, stream, qm, km, vm, lm, pr, feat, shifts, spread)
    from_down = mail.push(stream, v.at[mine], up)
    from_up = mail.push(stream, v.at[mine], down)
    v[mine] = stream[...]
    for d, part in enumerate((part0, part1, part2, part3)):
        to = turn(a, d, HEADS)
        for n in range(SLABS):
            piece, slot = full.at[:, cols(n * HEADS + to, ROWS)], part.at[:, pl.ds(n * ROWS, ROWS)]
            if d:
                mail.push(piece, slot, at_ctx(z, to))
            else:
                mail.keep(piece, slot)

    def lanes_of(i):
        return pl.ds(i * ROWS, ROWS)

    def slots(c):
        return pl.ds(pl.multiple_of(SLAB + c * CHUNK, CHUNK), CHUNK)

    def keys_of(c):
        return pl.ds(pl.multiple_of(c * CHUNK, CHUNK), CHUNK)

    after = lax.broadcasted_iota(jnp.int32, (ROWS, ROWS), 0) > lax.broadcasted_iota(jnp.int32, (ROWS, ROWS), 1)
    for i in range(HEADS):
        span = ROWS * (i + 1)
        scores = dot_t(k[pl.ds(pl.multiple_of(z * SLAB, SLAB), span)], q[lanes_of(i)])
        corner = jnp.where(after, -1e30, scores[span - ROWS :])
        top = jnp.max(corner, axis=0, keepdims=True)
        if i:
            top = jnp.maximum(top, jnp.max(scores[: span - ROWS], axis=0, keepdims=True))
            st[pl.ds(0, span - ROWS), lanes_of(i)] = scores[: span - ROWS]
        st[pl.ds(span - ROWS, ROWS), lanes_of(i)] = corner
        tops[:, lanes_of(i)] = top

    def score_step(c, top):
        past = dot_t(k[keys_of(c)], q[...])
        st[slots(c)] = past
        return jnp.maximum(top, jnp.max(past, axis=0, keepdims=True))

    top = lax.fori_loop(0, z * (SLAB // CHUNK), score_step, tops[...]) * gain

    half = SLAB // 2
    mail.arrive(from_down)
    lower = v.at[pl.ds(pl.multiple_of(turn(z, -1, SLABS) * SLAB, SLAB), half)]
    low = mail.push(lower, lower, up)
    mail.arrive(from_up)
    upper = v.at[pl.ds(pl.multiple_of(turn(z, 1, SLABS) * SLAB + half, half), half)]
    high = mail.push(upper, upper, down)

    for i in range(HEADS):
        span = ROWS * (i + 1)
        p = jnp.exp2(st[pl.ds(0, span), lanes_of(i)] * gain - top[:, i * ROWS : (i + 1) * ROWS])
        tops[:, lanes_of(i)] = jnp.sum(p, axis=0, keepdims=True)
        pt[pl.ds(0, span), lanes_of(i)] = p.astype(BF)

    def weigh_step(c, total):
        p = jnp.exp2(st[slots(c)] * gain - top)
        pt[slots(c)] = p.astype(BF)
        return total + jnp.sum(p, axis=0, keepdims=True)

    inverse = 1.0 / lax.fori_loop(0, z * (SLAB // CHUNK), weigh_step, tops[...])
    lax.fori_loop(0, z + 1, turn_keys, 0)
    mail.arrive(low)
    mail.arrive(high)

    def turn_values(s, carry):
        vt[:, cols(s, SLAB)] = v[rows(s, SLAB)].T
        return carry

    lax.fori_loop(0, z + 1, turn_values, 0)
    for i in range(HEADS):
        span = ROWS * (i + 1)
        outs[:, lanes_of(i)] = dot(vt[:, pl.ds(pl.multiple_of(z * SLAB, SLAB), span)], pt[pl.ds(0, span), lanes_of(i)])

    def attend_step(c, carry):
        outs[...] += dot(vt[:, keys_of(c)], pt[slots(c)])
        return carry

    lax.fori_loop(0, z * (SLAB // CHUNK), attend_step, 0)
    out = outs[...] * inverse
    ctt[...] = (ct[...].astype(F32).T * inverse).astype(BF)
    cs[...] = ctt[...].T
    delta[...] = jnp.sum(ctt[...].astype(F32) * out, axis=0, keepdims=True)

    for i in reversed(range(HEADS)):
        span = ROWS * (i + 1)
        part = dot(pt[pl.ds(0, span), lanes_of(i)], cs[lanes_of(i)])
        if i == HEADS - 1:
            dv[pl.ds(0, SLAB)] = part
        else:
            dv[pl.ds(0, span)] += part
    dv[pl.ds(SLAB, HALO)] = jnp.zeros((HALO, DH), F32)
    edge[...] = dv[pl.ds(0, HALO)].astype(BF)

    def parcel(d, to, kind):
        src, dst, sent, got = ((dv_out, dv_in, dv_send, dv_recv), (dk_out, dk_in, dk_send, dk_recv))[kind]
        return pltpu.make_async_remote_copy(
            src_ref=src.at[d - 1],
            dst_ref=dst.at[d - 1],
            send_sem=sent.at[d - 1],
            recv_sem=got.at[d - 1],
            device_id=at_ctx(to, a),
            device_id_type=MESH,
        )

    def value_step(d, carry):
        s = z - d
        dv_out[d - 1, pl.ds(SLAB, HALO)] = edge[...]
        for n in range(SLAB // CHUNK):
            part = dot(pt[slots(s * (SLAB // CHUNK) + n)], cs[...]).astype(BF)
            dv_out[d - 1, pl.ds(n * CHUNK, CHUNK)] = part
            if n == 0:
                edge[...] = part[:HALO]
        parcel(d, s, 0).start()
        return carry

    lax.fori_loop(1, z + 1, value_step, 0)
    block[...] = (stream[...].astype(F32) + out.T).astype(BF)
    home(mail, block, block_home, z, a)

    for i in reversed(range(HEADS)):
        span = ROWS * (i + 1)
        here = pl.ds(pl.multiple_of(z * SLAB, SLAB), span)
        p = pt[pl.ds(0, span), lanes_of(i)]
        dp = dot(v[here], ctt[:, lanes_of(i)])
        ds = (p.astype(F32) * (dp - delta[:, lanes_of(i)])).astype(BF)
        part = dot(ds, q[lanes_of(i)])
        dqt[:, lanes_of(i)] = dot(kt[:, here], ds)
        if i == HEADS - 1:
            dka[...] = part
        else:
            dka[pl.ds(0, span)] += part

    def key_step(d, carry):
        s = z - d
        for n in range(SLAB // CHUNK):
            c = s * (SLAB // CHUNK) + n
            dp = dot(v[keys_of(c)], ctt[...])
            ds = (pt[slots(c)].astype(F32) * (dp - delta[...])).astype(BF)
            dk_out[d - 1, pl.ds(n * CHUNK, CHUNK)] = (dot(ds, q[...]) * scale).astype(BF)
            dqt[...] += dot(kt[:, keys_of(c)], ds)
        parcel(d, s, 1).start()
        return carry

    lax.fori_loop(1, z + 1, key_step, 0)
    dq[...] = (dqt[...].T * scale).astype(BF)
    home(mail, dq, dq_home, z, a)

    def add_values(d, carry):
        parcel(d, turn(z, d, SLABS), 0).wait_recv()
        dv[...] += dv_in[d - 1].astype(F32)
        return carry

    lax.fori_loop(1, SLABS - z, add_values, 0)
    back(z, a, dv, ct, chalo, short, qm, km, vm, lm, feat, sg, fg, short_part, mg, stack, shifts, spread)
    dka[...] = dka[...] * scale

    def add_keys(d, carry):
        parcel(d, turn(z, d, SLABS), 1).wait_recv()
        dka[...] += dk_in[d - 1].astype(F32)
        return carry

    lax.fori_loop(1, SLABS - z, add_keys, 0)
    dk[...] = dka[...].astype(BF)
    mail.finish()

    def sent_step(d, carry):
        for kind in range(2):
            parcel(d, turn(z, -d, SLABS), kind).wait_send()
        return carry

    lax.fori_loop(1, z + 1, sent_step, 0)


FRONT_REFS = 13
OUT_REFS = 12


def opening_kernel(tokens, queries, keys, cot, weights, short, mr, *refs):
    outs, held, rest = refs[:OUT_REFS], refs[OUT_REFS : OUT_REFS + FRONT_REFS], refs[OUT_REFS + FRONT_REFS :]
    th, qh, ch, chalo, fx, kfull, full = held[:7]
    z, a = place()
    row, col = lax.axis_index("row"), lax.axis_index("col")
    greeted = greet(
        [{"row": 1 - row}, {"col": turn(col, 1, 4)}, {"col": turn(col, -1, 4)}]
        + [at_ctx(z, turn(a, d, HEADS)) for d in range(1, HEADS)]
        + [at_ctx(turn(z, d, SLABS), b) for d in (1, -1) for b in range(HEADS)]
        + [at_ctx(turn(z, 2, SLABS), a)]
    )
    pl.run_scoped(
        lambda w: front_phase(greeted, w, tokens, queries, keys, cot, weights, *held), pltpu.VMEM(weights.shape, BF)
    )
    pl.run_scoped(
        lambda st: middle_phase(st, full, fx, th, qh, kfull, ch, chalo, short, mr, *outs, *rest),
        pltpu.VMEM((SLABS * SLAB, SLAB), F32),
    )


def opening(tokens, queries, keys, cot, weights, short, mr):
    any_space, vmem = pl.BlockSpec(memory_space=pl.ANY), pl.BlockSpec(memory_space=pltpu.VMEM)
    whole = SLABS * SLAB
    mine, head = shape(ROWS, WIDTH), shape(SLAB, DH)
    dma = pltpu.SemaphoreType.DMA
    remotes = 6 + 4 + 8 + 12 + 2 + 2 + 6 + 12
    return pl.pallas_call(
        opening_kernel,
        out_shape=[
            mine,
            mine,
            *[shape(ROWS, SLABS * ROWS)] * HEADS,
            head,
            shape(3, SLAB, DH),
            head,
            shape(3 * 16, DH),
            shape(SLAB + HALO, DH, kind=F32),
            shape(HALO + SLAB + TAIL, DH, kind=F32),
        ],
        in_specs=[vmem] * 4 + [any_space] + [vmem] * 2,
        out_specs=[any_space] * 6 + [vmem] * 6,
        scratch_shapes=[
            pltpu.VMEM((SLAB, DH), BF),
            pltpu.VMEM((SLAB, DH), BF),
            pltpu.VMEM((SLAB, DH), BF),
            pltpu.VMEM((HALO, DH), BF),
            pltpu.VMEM((3, EXT, DH), BF),
            pltpu.VMEM((whole, DH), BF),
            pltpu.VMEM((ROWS, 8 * WIDTH), BF),
            pltpu.VMEM((3, ROWS, WIDTH), F32),
            pltpu.VMEM((3, ROWS, WIDTH), BF),
            pltpu.VMEM((SLAB, DH), BF),
            dma((remotes,)),
            dma((remotes,)),
            dma((3 + 3 + 2 + 1,)),
            pltpu.VMEM((SLAB, DH), BF),
            pltpu.VMEM((whole, DH), BF),
            pltpu.VMEM((DH, whole), BF),
            pltpu.VMEM((DH, whole), BF),
            pltpu.VMEM((whole, SLAB), BF),
            pltpu.VMEM((1, SLAB), F32),
            pltpu.VMEM((DH, SLAB), F32),
            pltpu.VMEM((DH, SLAB), BF),
            pltpu.VMEM((SLAB, DH), BF),
            pltpu.VMEM((1, SLAB), F32),
            pltpu.VMEM((SLAB, DH), BF),
            pltpu.VMEM((SLAB, DH), BF),
            pltpu.VMEM((DH, SLAB), F32),
            pltpu.VMEM((SLAB + HALO, DH), F32),
            pltpu.VMEM((SLAB, DH), F32),
            pltpu.VMEM((HALO, DH), BF),
            pltpu.VMEM((SLABS - 1, SLAB + HALO, DH), BF),
            pltpu.VMEM((SLABS - 1, SLAB, DH), BF),
            pltpu.VMEM((SLABS - 1, SLAB + HALO, DH), BF),
            pltpu.VMEM((SLABS - 1, SLAB, DH), BF),
            pltpu.VMEM((SLAB + HALO, DH), F32),
            pltpu.VMEM((SLAB + TAIL, DH), F32),
            pltpu.VMEM((SLAB + TAIL, DH), F32),
            pltpu.VMEM((SLAB + TAIL, DH), F32),
            pltpu.VMEM((3, EXT, DH), F32),
            pltpu.VMEM((3, SLAB + TAIL, DH), F32),
            pltpu.VMEM((TILE, SLAB + TAIL + MRLEN - TILE, DH), F32),
            pltpu.VMEM((TILE, TAPS, TILE, DH), F32),
            dma((SLABS - 1,)),
            dma((SLABS - 1,)),
            dma((SLABS - 1,)),
            dma((SLABS - 1,)),
            dma((22,)),
            dma((22,)),
            dma((6,)),
        ],
        compiler_params=pltpu.CompilerParams(
            collective_id=2, has_side_effects=True, vmem_limit_bytes=60 << 20
        ),
    )(tokens, queries, keys, cot, weights, short, mr)


def finale_kernel(
    fg, sg, dk, short_part, mg, pr, part0, part1, part2, part3, weights,
    grad_input, grad_feat, dk_home, small_home,
    w, tq, tqt, fgall, fgm, wsend, zr1, zr2, tsend, xr1, xr2, yr, ysend, sgh, slots, small, total, shifts, lines,
    send, recv, loc,
):
    mail = Courier(send, recv, loc)
    z, a = place()
    row, col = lax.axis_index("row"), lax.axis_index("col")
    side, core = lax.div(a, 2), lax.rem(a, 2)
    mate, far, far_mate = side * 2 + 1 - core, (1 - side) * 2 + core, (1 - side) * 2 + 1 - core
    up, down = turn(z, 1, SLABS), turn(z, -1, SLABS)
    right, left = turn(col, 1, 4), turn(col, -1, 4)
    half = ROWS // 2
    pair = 2 * ROWS

    mail.keep(fg, fgall.at[a])
    for d, part in enumerate((part0, part1, part2, part3)):
        mail.keep(part, tq.at[rows(turn(a, -d, HEADS), ROWS)])
    greeted = greet(around(z, a) + [{"row": 1 - row}, {"col": right}, {"col": left}])
    loads = [pltpu.make_async_copy(weights.at[j], w.at[j], loc.at[8 + j]) for j in range(3)]
    for load in loads:
        load.start()
    greeted()

    near_rows, far_rows = rows(side, pair), rows(1 - side, pair)
    direct = [
        mail.push(fg.at[:, rows(to, ROWS)], fgall.at[a, :, rows(to, ROWS)], at_ctx(z, to)) for to in (far, far_mate)
    ]
    to_mate = mail.push(fg, fgall.at[a], at_ctx(z, mate))
    second = mail.push(fg.at[:, near_rows], fgall.at[a, :, near_rows], at_ctx(z, far))
    mail.settle()

    for b in range(SLABS):
        tqt[pl.ds(b * ROWS, ROWS)] = tq[:, pl.ds(b * ROWS, ROWS)].T

    def weight_block(n, head, dz):
        rhs = jnp.concatenate([fgall[head, j] for j in range(3)], axis=1)
        lhs = tqt[rows(turn(z, dz, SLABS), ROWS)]
        out = jnp.dot(lhs, rhs, preferred_element_type=F32)
        for j in range(3):
            wsend[n, dz, j] = out[:, j * DH : (j + 1) * DH].astype(BF)

    def weight_first(n, head):
        weight_block(n, head, 2)
        keys = (
            mail.push(wsend.at[n, 2, :, pl.ds(0, half)], zr1.at[n, 0], at_ctx(up, a)),
            mail.push(wsend.at[n, 2, :, pl.ds(half, half)], zr1.at[n, 1], at_ctx(down, a)),
        )
        for dz in (1, 3, 0):
            weight_block(n, head, dz)
        return keys

    def weight_second(n, keys):
        top, bottom = pl.ds(0, half), pl.ds(half, half)
        mail.arrive(keys[0])
        wsend[n, 1, :, top] = (wsend[n, 1, :, top].astype(F32) + zr1[n, 0].astype(F32)).astype(BF)
        one = mail.push(wsend.at[n, 1], zr2.at[n, 0], at_ctx(up, a))
        mail.arrive(keys[1])
        wsend[n, 3, :, bottom] = (wsend[n, 3, :, bottom].astype(F32) + zr1[n, 1].astype(F32)).astype(BF)
        return one, mail.push(wsend.at[n, 3], zr2.at[n, 1], at_ctx(down, a))

    def weight_third(n, head, keys):
        for k in keys:
            mail.arrive(k)
        for j in range(3):
            grad_feat[j, :, cols(head)] = (
                wsend[n, 0, j].astype(F32) + zr2[n, 0, j].astype(F32) + zr2[n, 1, j].astype(F32)
            )

    ring = [weight_first(0, a)]
    mail.arrive(to_mate)
    ring.append(weight_first(1, mate))
    spread_shifts(shifts, pr, HALO - MRLEN + TILE, -1)
    tap_grads(shifts, mg, lines)
    small[pl.ds(0, MRLEN)] = lines[...].reshape(MRLEN, DH).astype(BF)
    small[pl.ds(MRLEN, short_part.shape[0])] = short_part[...]
    small_in = [mail.push(small, slots.at[d - 1], at_ctx(turn(z, d, SLABS), a)) for d in range(1, SLABS)]
    for k in direct:
        mail.arrive(k)
    relays = [
        mail.push(fgall.at[h, :, rows(a, ROWS)], fgall.at[h, :, rows(a, ROWS)], at_ctx(z, mate))
        for h in (far, far_mate)
    ]

    for n in range(2):
        ring[n] = weight_second(n, ring[n])
    for j in range(3):
        for h in range(HEADS):
            fgm[j, :, pl.ds(h * DH, DH)] = fgall[h, j, rows(a, ROWS)]
    for load in loads:
        load.wait()

    top, bottom = pl.ds(0, half), pl.ds(half, half)
    shares = (1 - row, row)

    def term_block(dc, n):
        columns = rows(shares[n] * 4 + turn(col, dc, 4), WIDTH)
        out = jnp.zeros((ROWS, WIDTH), F32)
        for j in range(3):
            out += lax.dot_general(fgm[j], w[j, columns], (((1,), (1,)), ((), ())), preferred_element_type=F32)
        tsend[dc, n] = out.astype(BF)

    firsts, seconds = [], []
    for n in range(2):
        term_block(2, n)
        firsts.append(
            (
                mail.push(tsend.at[2, n, top], xr1.at[0, n], {"col": right}),
                mail.push(tsend.at[2, n, bottom], xr1.at[1, n], {"col": left}),
            )
        )
    for n in range(2):
        term_block(1, n)
        term_block(3, n)
        mail.arrive(firsts[n][0])
        tsend[1, n, top] = (tsend[1, n, top].astype(F32) + xr1[0, n].astype(F32)).astype(BF)
        from_left = mail.push(tsend.at[1, n], xr2.at[0, n], {"col": right})
        mail.arrive(firsts[n][1])
        tsend[3, n, bottom] = (tsend[3, n, bottom].astype(F32) + xr1[1, n].astype(F32)).astype(BF)
        seconds.append((from_left, mail.push(tsend.at[3, n], xr2.at[1, n], {"col": left})))
    home_sg = []
    for d in range(1, HEADS):
        to = turn(a, d, HEADS)
        home_sg.append(mail.push(sg.at[rows(to, ROWS)], sgh.at[:, cols(a)], at_ctx(z, to)))
        mail.push(dk.at[rows(to, ROWS)], dk_home.at[:, cols(a)], at_ctx(z, to))
    mail.keep(sg.at[rows(a, ROWS)], sgh.at[:, cols(a)])
    mail.keep(dk.at[rows(a, ROWS)], dk_home.at[:, cols(a)])
    term_block(0, 0)
    term_block(0, 1)
    mail.arrive(second)
    relays.append(mail.push(fgall.at[far, :, far_rows], fgall.at[far, :, far_rows], at_ctx(z, mate)))
    for k in relays[:2]:
        mail.arrive(k)
    ring.append(weight_first(2, far))
    mail.arrive(relays[2])
    ring.append(weight_first(3, far_mate))

    def term_sum(n):
        for k in seconds[n]:
            mail.arrive(k)
        return tsend[0, n].astype(F32) + xr2[0, n].astype(F32) + xr2[1, n].astype(F32)

    ysend[...] = term_sum(0).astype(BF)
    across = mail.push(ysend, yr, {"row": 1 - row})
    ring[2] = weight_second(2, ring[2])
    ring[3] = weight_second(3, ring[3])

    for k in small_in:
        mail.arrive(k)
    total[...] = (small_sum(small, slots)).astype(BF)
    for d in range(1, HEADS):
        mail.push(total, small_home.at[:, cols(a)], at_ctx(z, turn(a, d, HEADS)))
    mail.keep(total, small_home.at[:, cols(a)])

    weight_third(0, a, ring[0])
    weight_third(1, mate, ring[1])
    for k in home_sg:
        mail.arrive(k)
    mail.settle()
    mail.arrive(across)
    grad_input[...] = (sgh[...].astype(F32) + term_sum(1) + yr[...].astype(F32)).astype(BF)
    weight_third(2, far, ring[2])
    weight_third(3, far_mate, ring[3])
    mail.finish()


def small_sum(small, slots):
    return small[...].astype(F32) + sum(slots[d].astype(F32) for d in range(SLABS - 1))


def finale(fg, sg, dk, short_part, mg, pr, parts, weights):
    lines = MRLEN + short_part.shape[0]
    any_space, vmem = pl.BlockSpec(memory_space=pl.ANY), pl.BlockSpec(memory_space=pltpu.VMEM)
    remotes = 1 + 3 + 3 + 6 + 6 + 16 + 8 + 1
    return pl.pallas_call(
        finale_kernel,
        out_shape=[
            shape(ROWS, WIDTH),
            shape(3, ROWS, WIDTH, kind=F32),
            shape(ROWS, WIDTH),
            shape(lines, WIDTH),
        ],
        in_specs=[any_space] * 3 + [vmem] * 3 + [any_space] * 5,
        out_specs=[vmem, vmem, any_space, any_space],
        scratch_shapes=[
            pltpu.VMEM(weights.shape, BF),
            pltpu.VMEM((SLAB, SLABS * ROWS), BF),
            pltpu.VMEM((SLABS * ROWS, SLAB), BF),
            pltpu.VMEM((HEADS, 3, SLAB, DH), BF),
            pltpu.VMEM((3, ROWS, WIDTH), BF),
            pltpu.VMEM((HEADS, SLABS, 3, ROWS, DH), BF),
            pltpu.VMEM((HEADS, 2, 3, ROWS // 2, DH), BF),
            pltpu.VMEM((HEADS, 2, 3, ROWS, DH), BF),
            pltpu.VMEM((4, 2, ROWS, WIDTH), BF),
            pltpu.VMEM((2, 2, ROWS // 2, WIDTH), BF),
            pltpu.VMEM((2, 2, ROWS, WIDTH), BF),
            pltpu.VMEM((ROWS, WIDTH), BF),
            pltpu.VMEM((ROWS, WIDTH), BF),
            pltpu.VMEM((ROWS, WIDTH), BF),
            pltpu.VMEM((SLABS - 1, lines, DH), BF),
            pltpu.VMEM((lines, DH), BF),
            pltpu.VMEM((lines, DH), BF),
            pltpu.VMEM((TILE, SLAB + TAIL + MRLEN - TILE, DH), F32),
            pltpu.VMEM((TAPS, TILE, DH), F32),
            pltpu.SemaphoreType.DMA((remotes,)),
            pltpu.SemaphoreType.DMA((remotes,)),
            pltpu.SemaphoreType.DMA((11,)),
        ],
        compiler_params=pltpu.CompilerParams(
            collective_id=5, has_side_effects=True, vmem_limit_bytes=56 << 20
        ),
    )(fg, sg, dk, short_part, mg, pr, *parts, weights)


def deliver_kernel(block, grad_q, grad_k, grad_in, grad_feat, small, block_o, in_o, feat_o, short_o, mr_o, q_o, k_o):
    feat_o[...] = grad_feat[...]
    block_o[...] = block[...]
    in_o[...] = grad_in[...]
    q_o[...] = grad_q[...]
    k_o[...] = grad_k[...]

    @pl.when(pl.program_id(0) == 0)
    def _():
        mr_o[...] = small[pl.ds(0, MRLEN)].astype(F32)
        for j in range(3):
            short_o[j] = small[pl.ds(MRLEN + 16 * j, 16)].astype(F32)[:SHORT]


def deliver(*ins):
    steps = 4

    def fixed(*dims):
        return pl.BlockSpec(dims, lambda n: (0,) * len(dims))

    mine = pl.BlockSpec((ROWS // steps, WIDTH), lambda n: (n, 0))
    feat = pl.BlockSpec((3, ROWS // steps, WIDTH), lambda n: (0, n, 0))
    out = shape(ROWS, WIDTH)
    return pl.pallas_call(
        deliver_kernel,
        grid=(steps,),
        out_shape=[
            out,
            out,
            shape(3, ROWS, WIDTH, kind=F32),
            shape(3, SHORT, WIDTH, kind=F32),
            shape(MRLEN, WIDTH, kind=F32),
            out,
            out,
        ],
        in_specs=[mine] * 4 + [feat, fixed(*ins[-1].shape)],
        out_specs=[mine, mine, feat, fixed(3, SHORT, WIDTH), fixed(MRLEN, WIDTH), mine, mine],
        compiler_params=pltpu.CompilerParams(vmem_limit_bytes=60 << 20),
    )(*ins)


def local(tokens, w_feat, short_filter, mr_filter, queries, key_rows, cotangent):
    weights = w_feat.transpose(1, 0, 2)
    short_taps = short_filter.transpose(1, 0, 2)
    block, grad_queries, *token_parts, sg, fg, dk, short_part, mg, pr = opening(
        tokens, queries, key_rows, cotangent, weights, short_taps, mr_filter
    )
    grad_input, grad_feat, grad_keys, small = finale(fg, sg, dk, short_part, mg, pr, token_parts, weights)
    block_out, grad_input, grad_feat, grad_short, grad_mr, grad_queries, grad_keys = deliver(
        block, grad_queries, grad_keys, grad_input, grad_feat, small
    )
    grad_feat, grad_short = grad_feat.transpose(1, 0, 2), grad_short.transpose(1, 0, 2)
    return (block_out, grad_input, grad_feat, grad_short, grad_mr, grad_queries, grad_keys)


def solution(mesh):
    placed = (
        P("ctx", ("row", "col")),
        P(None, None, ("row", "col")),
        P(None, None, ("row", "col")),
        P(None, ("row", "col")),
        P("ctx", ("row", "col")),
        P("ctx", ("row", "col")),
        P("ctx", ("row", "col")),
    )
    return jax.shard_map(
        local,
        mesh=mesh,
        in_specs=placed,
        out_specs=(
            P("ctx", ("row", "col")),
            P("ctx", ("row", "col")),
            P("ctx", None, ("row", "col")),
            P(None, None, ("row", "col")),
            P(None, ("row", "col")),
            P("ctx", ("row", "col")),
            P("ctx", ("row", "col")),
        ),
        check_vma=False,
    )
```

```python
import functools

import jax
import jax.numpy as jnp
from jax import lax
from jax.experimental import pallas as pl
from jax.experimental.pallas import tpu as pltpu
from jax.sharding import PartitionSpec as P

DH = 128
SHORT = 7
MRLEN = 128
HALO = 144
TAIL = 16
ROWS = 256
HEADS = 4
SLABS = 4
SLAB = ROWS * HEADS
EXT = HALO + SLAB + HALO
WIDTH = HEADS * DH
MESH = pl.DeviceIdType.MESH
BF = jnp.bfloat16
F32 = jnp.float32


def place():
    ctx = lax.axis_index("ctx")
    return lax.div(ctx, HEADS), lax.rem(ctx, HEADS)


def turn(index, step, size):
    return lax.rem(index + (step + size), size)


def at_ctx(z, a):
    return {"ctx": z * HEADS + a}


def cols(index, width=DH):
    return pl.ds(pl.multiple_of(index * width, width), width)


def rows(index, height, offset=0):
    return pl.ds(pl.multiple_of(index * height + offset, 16), height)


def greet(devices):
    barrier = pltpu.get_barrier_semaphore()
    for device in devices:
        pl.semaphore_signal(barrier, inc=1, device_id=device, device_id_type=MESH)
    return functools.partial(pl.semaphore_wait, barrier, len(devices))


class Courier:
    def __init__(self, send, recv, local):
        self.send, self.recv, self.local = send, recv, local
        self.remote, self.here = [], []
        self.arrived = set()
        self.settled = 0

    def push(self, src, dst, device):
        k = len(self.remote)
        copy = pltpu.make_async_remote_copy(
            src_ref=src,
            dst_ref=dst,
            send_sem=self.send.at[k],
            recv_sem=self.recv.at[k],
            device_id=device,
            device_id_type=MESH,
        )
        copy.start()
        self.remote.append(copy)
        return k

    def keep(self, src, dst):
        copy = pltpu.make_async_copy(src, dst, self.local.at[len(self.here)])
        copy.start()
        self.here.append(copy)

    def arrive(self, k):
        if k not in self.arrived:
            self.arrived.add(k)
            self.remote[k].wait_recv()

    def finish(self):
        for k in range(len(self.remote)):
            self.arrive(k)
        for copy in self.remote:
            copy.wait_send()
        self.settle()

    def settle(self):
        for copy in self.here[self.settled :]:
            copy.wait()
        self.settled = len(self.here)


def shape(*dims, kind=BF):
    return jax.ShapeDtypeStruct(dims, kind)


def slab_gather(mail, part, whole, z, a):
    up, down = turn(z, 1, SLABS), turn(z, -1, SLABS)
    mine = whole.at[rows(z, SLAB)]
    mail.keep(part, mine)
    return mail.push(part, mine, at_ctx(up, a)), mail.push(part, mine, at_ctx(down, a))


def slab_relay(mail, whole, z, a, from_down, from_up):
    up, down = turn(z, 1, SLABS), turn(z, -1, SLABS)
    half = SLAB // 2
    mail.arrive(from_down)
    lower = whole.at[pl.ds(pl.multiple_of(down * SLAB, 16), half)]
    mail.push(lower, lower, at_ctx(up, a))
    mail.arrive(from_up)
    upper = whole.at[pl.ds(pl.multiple_of(up * SLAB + half, 16), half)]
    mail.push(upper, upper, at_ctx(down, a))


def front_phase(
    greeted, mix, w, tokens, queries, keys, cot, weights, th, qh, ch, chalo, fx, kfull, full, acc, feats, kh, send, recv, loc,
):
    mail = Courier(send, recv, loc)
    z, a = place()
    row, col = lax.axis_index("row"), lax.axis_index("col")
    other = 1 - row
    right, left, across = turn(col, 1, 4), turn(col, -1, 4), turn(col, 2, 4)
    up, down = turn(z, 1, SLABS), turn(z, -1, SLABS)
    for j in range(3):
        mail.keep(weights.at[j], w.at[j])
    full[:, cols(row * 4 + col, WIDTH)] = tokens[...]
    kh[rows(a, ROWS)] = keys[:, cols(a)]
    acc[...] = jnp.zeros_like(acc)
    greeted()

    half, quarter = ROWS // 2, ROWS // 4

    def piece(r, c, h):
        return full.at[pl.ds(h * half, half), cols(r * 4 + c, WIDTH)]

    def part(r, c, h, n):
        return full.at[pl.ds(h * half + n * quarter, quarter), cols(r * 4 + c, WIDTH)]

    def project(r, c, h):
        here = pl.ds(h * half, half)
        lhs = full[here, cols(r * 4 + c, WIDTH)]
        for j in range(3):
            acc[j, here] += jnp.dot(lhs, w[j, rows(r * 4 + c, WIDTH)], preferred_element_type=F32)

    def launch(h):
        src, dst = tokens.at[pl.ds(h * half, half)], piece(row, col, h)
        return [mail.push(src, dst, device) for device in ({"row": other}, {"col": right}, {"col": left})]

    def sideways(h, arrival):
        mail.arrive(arrival)
        dst = piece(other, col, h)
        return [mail.push(dst, dst, device) for device in ({"col": right}, {"col": left})]

    def relay(r, h, from_left, from_right):
        mail.arrive(from_left)
        one = mail.push(part(r, left, h, 0), part(r, left, h, 0), {"col": right})
        mail.arrive(from_right)
        return one, mail.push(part(r, right, h, 1), part(r, right, h, 1), {"col": left})

    def finish_half(h, relays):
        for r, keys_in in zip((row, other), relays):
            for k in keys_in:
                mail.arrive(k)
            project(r, across, h)
        here = pl.ds(h * half, half)
        for j in range(3):
            feats[j, here] = acc[j, here].astype(BF)
        there = pl.ds(pl.multiple_of(a * ROWS + (HALO + h * half), 16), half)
        for d in range(1, HEADS):
            to = turn(a, d, HEADS)
            needed.append(mail.push(feats.at[:, here, cols(to)], fx.at[:, there], at_ctx(z, to)))
        mail.keep(feats.at[:, here, cols(a)], fx.at[:, there])

    first = launch(0)
    mail.settle()
    project(row, col, 0)
    first_side = sideways(0, first[0])
    second = launch(1)
    key_parts, needed = [], []
    for src, dst in ((keys, kh), (tokens, th), (queries, qh), (cot, ch)):
        for d in range(1, HEADS):
            to = turn(a, d, HEADS)
            k = mail.push(src.at[:, cols(to)], dst.at[rows(a, ROWS)], at_ctx(z, to))
            if dst is kh:
                key_parts.append(k)
            elif dst is th:
                needed.append(k)
        if dst is not kh:
            mail.keep(src.at[:, cols(a)], dst.at[rows(a, ROWS)])
    project(other, col, 0)
    relays = [[relay(row, 0, *first[1:])], []]
    second_side = sideways(1, second[0])
    relays[0].append(relay(other, 0, *first_side))
    for r in (row, other):
        project(r, left, 0)
        project(r, right, 0)
    relays[1].append(relay(row, 1, *second[1:]))
    finish_half(0, relays[0])
    relays[1].append(relay(other, 1, *second_side))
    for k in key_parts:
        mail.arrive(k)
    gathered = slab_gather(mail, kh, kfull, z, a)
    for r in (row, other):
        project(r, col, 1)
        project(r, left, 1)
        project(r, right, 1)
    finish_half(1, relays[1])

    n = len(mail.remote) + 2

    def edge(src, dst, k, b, device):
        return pltpu.make_async_remote_copy(
            src_ref=src,
            dst_ref=dst,
            send_sem=mail.send.at[k + 3 * b],
            recv_sem=mail.recv.at[k],
            device_id=device,
            device_id_type=MESH,
        )

    def first_rows(b):
        lanes = pl.ds(b * DH, DH)
        return (
            edge(feats.at[:, pl.ds(0, HALO), lanes], fx.at[:, pl.ds(HALO + SLAB, HALO)], n, b, at_ctx(down, b)),
            edge(cot.at[pl.ds(0, HALO), lanes], chalo, n + 1, b, at_ctx(down, b)),
        )

    def last_rows(b):
        lanes = pl.ds(b * DH, DH)
        return (edge(feats.at[:, pl.ds(ROWS - HALO, HALO), lanes], fx.at[:, pl.ds(0, HALO)], n + 2, b, at_ctx(up, b)),)

    @pl.when(a == 0)
    def _():
        for b in range(HEADS):
            for copy in first_rows(b):
                copy.start()

    @pl.when(a == HEADS - 1)
    def _():
        for b in range(HEADS):
            for copy in last_rows(b):
                copy.start()

    slab_relay(mail, kfull, z, a, *gathered)
    mail.settle()
    for k in needed:
        mail.arrive(k)
    for copy in first_rows(0) + last_rows(0):
        copy.wait_recv()
    mix()
    mail.finish()

    @pl.when(a == 0)
    def _():
        for b in range(HEADS):
            for copy in first_rows(b):
                copy.wait_send()

    @pl.when(a == HEADS - 1)
    def _():
        for b in range(HEADS):
            for copy in last_rows(b):
                copy.wait_send()


def around(z, a):
    return [at_ctx(turn(z, d, SLABS), a) for d in range(1, SLABS)] + [
        at_ctx(z, turn(a, d, HEADS)) for d in range(1, HEADS)
    ]


def home(mail, src, dst, z, a):
    for d in range(1, HEADS):
        to = turn(a, d, HEADS)
        mail.push(src.at[rows(to, ROWS)], dst.at[:, cols(a)], at_ctx(z, to))
    mail.keep(src.at[rows(a, ROWS)], dst.at[:, cols(a)])


CHUNK = 512


def dot(x, y):
    return jnp.dot(x, y, preferred_element_type=F32)


def dot_t(x, y):
    return lax.dot_general(x, y, (((1,), (1,)), ((), ())), preferred_element_type=F32)


GROUP = 40
TILE = 8
TAPS = MRLEN // TILE
SPAN = 13


def spread_taps(spread, taps, a):
    for i in range(MRLEN):
        spread[i % TILE, i // TILE] = jnp.broadcast_to(taps[pl.ds(i, 1), cols(a)], (TILE, DH))


def spread_shifts(shifts, rows_of, first, sign):
    count = shifts.shape[1]
    for r in range(TILE):
        shifts[r] = rows_of[pl.ds(first + sign * r, count)]


def long_filter(shifts, spread, backward, store):
    def step(g, carry):
        base = pl.multiple_of(g * (SPAN * TILE), TILE)

        def shift(r, totals):
            totals = list(totals)
            taps = [spread[r, m] for m in range(TAPS)]
            for t in range(SPAN + TAPS - 1):
                tile = shifts[r, pl.ds(base + t * TILE, TILE)]
                for n in range(SPAN):
                    m = t - n if backward else n + TAPS - 1 - t
                    if 0 <= m < TAPS:
                        totals[n] += taps[m] * tile
            return tuple(totals)

        totals = lax.fori_loop(0, TILE, shift, tuple(jnp.zeros((TILE, DH), F32) for _ in range(SPAN)))
        for n in range(SPAN):
            store(pl.ds(base + n * TILE, TILE), totals[n])
        return carry

    lax.fori_loop(0, (SLAB + TAIL) // (SPAN * TILE), step, 0)


def tap_grads(shifts, grads, lines):
    count = 16

    def shift(r, carry):
        def step(g, sums):
            sums = list(sums)
            base = pl.multiple_of(g * (count * TILE), TILE)
            own = [grads[pl.ds(base + n * TILE, TILE)] for n in range(count)]
            for t in range(count + TAPS - 1):
                tile = shifts[r, pl.ds(base + t * TILE, TILE)]
                for n in range(count):
                    m = n + TAPS - 1 - t
                    if 0 <= m < TAPS:
                        sums[m] += own[n] * tile
            return tuple(sums)

        zero = tuple(jnp.zeros((TILE, DH), F32) for _ in range(TAPS))
        sums = lax.fori_loop(0, SLAB // (count * TILE), step, zero)
        for m in range(TAPS):
            lines[m, pl.ds(r, 1)] = jnp.sum(sums[m], axis=0, keepdims=True)
        return carry

    lax.fori_loop(0, TILE, shift, 0)


def hyena(z, a, fx, short, tok, stream, qm, km, vm, lm, pr, feat, shifts, spread):
    keep_head = (z > 0).astype(F32)
    keep_tail = (z < SLABS - 1).astype(F32)
    for j in range(3):
        feat[j, pl.ds(0, HALO)] = fx[j, pl.ds(0, HALO)].astype(F32) * keep_head
        feat[j, pl.ds(HALO, SLAB)] = fx[j, pl.ds(HALO, SLAB)].astype(F32)
        feat[j, pl.ds(HALO + SLAB, HALO)] = fx[j, pl.ds(HALO + SLAB, HALO)].astype(F32) * keep_tail

    taps = [[short[j, pl.ds(s, 1), cols(a)] for s in range(SHORT)] for j in range(3)]

    def mixed(j, base, count):
        total = taps[j][0] * feat[j, pl.ds(base, count)]
        for s in range(1, SHORT):
            total += taps[j][s] * feat[j, pl.ds(base - s, count)]
        return total

    pr[pl.ds(0, 16)] = jnp.zeros((16, DH), F32)

    def head_step(g, carry):
        base = pl.multiple_of(16 + g * 16, 16)
        pr[pl.ds(base, 16)] = (mixed(1, base, 16) * mixed(2, base, 16)).astype(BF).astype(F32)
        return carry

    lax.fori_loop(0, (HALO - 16) // 16, head_step, 0)

    def mix_step(g, carry):
        base = pl.multiple_of(HALO + g * GROUP, 8)
        here = pl.ds(pl.multiple_of(g * GROUP, 8), GROUP)
        key, value = mixed(1, base, GROUP), mixed(2, base, GROUP)
        km[here] = key
        vm[here] = value
        qm[here] = mixed(0, base, GROUP)
        pr[pl.ds(base, GROUP)] = (key * value).astype(BF).astype(F32)
        return carry

    lax.fori_loop(0, (SLAB + TAIL) // GROUP, mix_step, 0)

    def tail_step(g, carry):
        here = pl.multiple_of(SLAB + TAIL + g * 16, 16)
        qm[pl.ds(here, 16)] = mixed(0, here + HALO, 16)
        return carry

    lax.fori_loop(0, (HALO - TAIL) // 16, tail_step, 0)
    spread_shifts(shifts, pr, HALO - MRLEN + TILE, -1)

    def store(here, total):
        lm[here] = total

    long_filter(shifts, spread, False, store)
    own = pl.ds(0, SLAB)
    stream[...] = (tok[...].astype(F32) + qm[own] * lm[own]).astype(BF)


def back(z, a, dv, ch, chalo, short, qm, km, vm, lm, feat, sg, fg, short_part, mg, stack, shifts, spread):
    keep_tail = (z < SLABS - 1).astype(F32)
    own, halo = pl.ds(0, SLAB), pl.ds(SLAB, HALO)
    grad = (ch[...].astype(F32) + dv[own]).astype(BF)
    sg[...] = grad
    mg[own] = (grad.astype(F32) * qm[own]).astype(BF).astype(F32)
    grad_halo = (chalo[...].astype(F32) + dv[halo]).astype(BF).astype(F32) * keep_tail
    mg[halo] = (grad_halo * qm[halo]).astype(BF).astype(F32)
    stack[0, own] = grad.astype(F32) * lm[own]
    stack[0, pl.ds(SLAB, TAIL)] = grad_halo[:TAIL] * lm[pl.ds(SLAB, TAIL)]
    spread_shifts(shifts, mg, 0, 1)

    def store(here, total):
        stack[1, here] = total * vm[here]
        stack[2, here] = total * km[here]

    long_filter(shifts, spread, True, store)
    for j in range(3):
        taps = [short[j, pl.ds(s, 1), cols(a)] for s in range(SHORT)]

        def short_step(g, sums):
            base = pl.multiple_of(g * 32, 32)
            line = stack[j, pl.ds(base, 32)]
            total = taps[0] * line
            for s in range(1, SHORT):
                total += taps[s] * stack[j, pl.ds(base + s, 32)]
            fg[j, pl.ds(base, 32)] = total.astype(BF)
            out = []
            for s in range(SHORT):
                term = line * feat[j, pl.ds(base + HALO - s, 32)]
                out.append(sums[s] + (term[0:8] + term[8:16] + term[16:24] + term[24:32]))
            return tuple(out)

        sums = lax.fori_loop(0, SLAB // 32, short_step, tuple(jnp.zeros((8, DH), F32) for _ in range(SHORT)))
        lines = [jnp.sum(t, axis=0, keepdims=True) for t in sums]
        short_part[pl.ds(16 * j, 16)] = jnp.concatenate(lines + [jnp.zeros((16 - SHORT, DH), F32)], axis=0).astype(BF)


def middle_phase(
    st, full, fx, tok, q, k, ct, chalo, short, mr,
    block_home, dq_home, part0, part1, part2, part3, sg, fg, dk, short_part, mg, pr,
    stream, v, kt, vt, pt, tops, outs, ctt, cs, delta, block, dq, dqt, dv, dka, edge, dv_out, dk_out, dv_in, dk_in,
    qm, km, vm, lm, feat, stack, shifts, spread,
    dv_send, dv_recv, dk_send, dk_recv, send, recv, loc,
):
    mail = Courier(send, recv, loc)
    z, a = place()
    scale = DH ** -0.5
    gain = scale * 1.4426950408889634
    mine = rows(z, SLAB)
    up, down = at_ctx(turn(z, 1, SLABS), a), at_ctx(turn(z, -1, SLABS), a)
    def turn_keys(s, carry):
        kt[:, cols(s, SLAB)] = k[rows(s, SLAB)].T
        return carry

    from_down = mail.push(stream, v.at[mine], up)
    from_up = mail.push(stream, v.at[mine], down)
    v[mine] = stream[...]
    for d, part in enumerate((part0, part1, part2, part3)):
        to = turn(a, d, HEADS)
        for n in range(SLABS):
            piece, slot = full.at[:, cols(n * HEADS + to, ROWS)], part.at[:, pl.ds(n * ROWS, ROWS)]
            if d:
                mail.push(piece, slot, at_ctx(z, to))
            else:
                mail.keep(piece, slot)

    def lanes_of(i):
        return pl.ds(i * ROWS, ROWS)

    def slots(c):
        return pl.ds(pl.multiple_of(SLAB + c * CHUNK, CHUNK), CHUNK)

    def keys_of(c):
        return pl.ds(pl.multiple_of(c * CHUNK, CHUNK), CHUNK)

    after = lax.broadcasted_iota(jnp.int32, (ROWS, ROWS), 0) > lax.broadcasted_iota(jnp.int32, (ROWS, ROWS), 1)
    for i in range(HEADS):
        span = ROWS * (i + 1)
        scores = dot_t(k[pl.ds(pl.multiple_of(z * SLAB, SLAB), span)], q[lanes_of(i)])
        corner = jnp.where(after, -1e30, scores[span - ROWS :])
        top = jnp.max(corner, axis=0, keepdims=True)
        if i:
            top = jnp.maximum(top, jnp.max(scores[: span - ROWS], axis=0, keepdims=True))
            st[pl.ds(0, span - ROWS), lanes_of(i)] = scores[: span - ROWS]
        st[pl.ds(span - ROWS, ROWS), lanes_of(i)] = corner
        tops[:, lanes_of(i)] = top

    def score_step(c, top):
        past = dot_t(k[keys_of(c)], q[...])
        st[slots(c)] = past
        return jnp.maximum(top, jnp.max(past, axis=0, keepdims=True))

    top = lax.fori_loop(0, z * (SLAB // CHUNK), score_step, tops[...]) * gain

    half = SLAB // 2
    mail.arrive(from_down)
    lower = v.at[pl.ds(pl.multiple_of(turn(z, -1, SLABS) * SLAB, SLAB), half)]
    low = mail.push(lower, lower, up)
    mail.arrive(from_up)
    upper = v.at[pl.ds(pl.multiple_of(turn(z, 1, SLABS) * SLAB + half, half), half)]
    high = mail.push(upper, upper, down)

    for i in range(HEADS):
        span = ROWS * (i + 1)
        p = jnp.exp2(st[pl.ds(0, span), lanes_of(i)] * gain - top[:, i * ROWS : (i + 1) * ROWS])
        tops[:, lanes_of(i)] = jnp.sum(p, axis=0, keepdims=True)
        pt[pl.ds(0, span), lanes_of(i)] = p.astype(BF)

    def weigh_step(c, total):
        p = jnp.exp2(st[slots(c)] * gain - top)
        pt[slots(c)] = p.astype(BF)
        return total + jnp.sum(p, axis=0, keepdims=True)

    inverse = 1.0 / lax.fori_loop(0, z * (SLAB // CHUNK), weigh_step, tops[...])
    lax.fori_loop(0, z + 1, turn_keys, 0)
    mail.arrive(low)
    mail.arrive(high)

    def turn_values(s, carry):
        vt[:, cols(s, SLAB)] = v[rows(s, SLAB)].T
        return carry

    lax.fori_loop(0, z + 1, turn_values, 0)
    for i in range(HEADS):
        span = ROWS * (i + 1)
        outs[:, lanes_of(i)] = dot(vt[:, pl.ds(pl.multiple_of(z * SLAB, SLAB), span)], pt[pl.ds(0, span), lanes_of(i)])

    def attend_step(c, carry):
        outs[...] += dot(vt[:, keys_of(c)], pt[slots(c)])
        return carry

    lax.fori_loop(0, z * (SLAB // CHUNK), attend_step, 0)
    out = outs[...] * inverse
    ctt[...] = (ct[...].astype(F32).T * inverse).astype(BF)
    cs[...] = ctt[...].T
    delta[...] = jnp.sum(ctt[...].astype(F32) * out, axis=0, keepdims=True)

    for i in reversed(range(HEADS)):
        span = ROWS * (i + 1)
        part = dot(pt[pl.ds(0, span), lanes_of(i)], cs[lanes_of(i)])
        if i == HEADS - 1:
            dv[pl.ds(0, SLAB)] = part
        else:
            dv[pl.ds(0, span)] += part
    dv[pl.ds(SLAB, HALO)] = jnp.zeros((HALO, DH), F32)
    edge[...] = dv[pl.ds(0, HALO)].astype(BF)

    def parcel(d, to, kind):
        src, dst, sent, got = ((dv_out, dv_in, dv_send, dv_recv), (dk_out, dk_in, dk_send, dk_recv))[kind]
        return pltpu.make_async_remote_copy(
            src_ref=src.at[d - 1],
            dst_ref=dst.at[d - 1],
            send_sem=sent.at[d - 1],
            recv_sem=got.at[d - 1],
            device_id=at_ctx(to, a),
            device_id_type=MESH,
        )

    def value_step(d, carry):
        s = z - d
        dv_out[d - 1, pl.ds(SLAB, HALO)] = edge[...]
        for n in range(SLAB // CHUNK):
            part = dot(pt[slots(s * (SLAB // CHUNK) + n)], cs[...]).astype(BF)
            dv_out[d - 1, pl.ds(n * CHUNK, CHUNK)] = part
            if n == 0:
                edge[...] = part[:HALO]
        parcel(d, s, 0).start()
        return carry

    lax.fori_loop(1, z + 1, value_step, 0)
    block[...] = (stream[...].astype(F32) + out.T).astype(BF)
    home(mail, block, block_home, z, a)

    for i in reversed(range(HEADS)):
        span = ROWS * (i + 1)
        here = pl.ds(pl.multiple_of(z * SLAB, SLAB), span)
        p = pt[pl.ds(0, span), lanes_of(i)]
        dp = dot(v[here], ctt[:, lanes_of(i)])
        ds = (p.astype(F32) * (dp - delta[:, lanes_of(i)])).astype(BF)
        part = dot(ds, q[lanes_of(i)])
        dqt[:, lanes_of(i)] = dot(kt[:, here], ds)
        if i == HEADS - 1:
            dka[...] = part
        else:
            dka[pl.ds(0, span)] += part

    def key_step(d, carry):
        s = z - d
        for n in range(SLAB // CHUNK):
            c = s * (SLAB // CHUNK) + n
            dp = dot(v[keys_of(c)], ctt[...])
            ds = (pt[slots(c)].astype(F32) * (dp - delta[...])).astype(BF)
            dk_out[d - 1, pl.ds(n * CHUNK, CHUNK)] = (dot(ds, q[...]) * scale).astype(BF)
            dqt[...] += dot(kt[:, keys_of(c)], ds)
        parcel(d, s, 1).start()
        return carry

    lax.fori_loop(1, z + 1, key_step, 0)
    dq[...] = (dqt[...].T * scale).astype(BF)
    home(mail, dq, dq_home, z, a)

    def add_values(d, carry):
        parcel(d, turn(z, d, SLABS), 0).wait_recv()
        dv[...] += dv_in[d - 1].astype(F32)
        return carry

    lax.fori_loop(1, SLABS - z, add_values, 0)
    back(z, a, dv, ct, chalo, short, qm, km, vm, lm, feat, sg, fg, short_part, mg, stack, shifts, spread)
    dka[...] = dka[...] * scale

    def add_keys(d, carry):
        parcel(d, turn(z, d, SLABS), 1).wait_recv()
        dka[...] += dk_in[d - 1].astype(F32)
        return carry

    lax.fori_loop(1, SLABS - z, add_keys, 0)
    dk[...] = dka[...].astype(BF)
    mail.finish()

    def sent_step(d, carry):
        for kind in range(2):
            parcel(d, turn(z, -d, SLABS), kind).wait_send()
        return carry

    lax.fori_loop(1, z + 1, sent_step, 0)


FRONT_REFS = 13
OUT_REFS = 12


def opening_kernel(tokens, queries, keys, cot, weights, short, mr, *refs):
    outs, held, rest = refs[:OUT_REFS], refs[OUT_REFS : OUT_REFS + FRONT_REFS], refs[OUT_REFS + FRONT_REFS :]
    th, qh, ch, chalo, fx, kfull, full = held[:7]
    z, a = place()
    row, col = lax.axis_index("row"), lax.axis_index("col")
    greeted = greet(
        [{"row": 1 - row}, {"col": turn(col, 1, 4)}, {"col": turn(col, -1, 4)}]
        + [at_ctx(z, turn(a, d, HEADS)) for d in range(1, HEADS)]
        + [at_ctx(turn(z, d, SLABS), b) for d in (1, -1) for b in range(HEADS)]
        + [at_ctx(turn(z, 2, SLABS), a)]
    )
    stream, (qm, km, vm, lm, feat, _, shifts, spread), pr = rest[0], rest[20:28], outs[-1]

    def mix():
        spread_taps(spread, mr, a)
        hyena(z, a, fx, short, th, stream, qm, km, vm, lm, pr, feat, shifts, spread)

    pl.run_scoped(
        lambda w: front_phase(greeted, mix, w, tokens, queries, keys, cot, weights, *held), pltpu.VMEM(weights.shape, BF)
    )
    pl.run_scoped(
        lambda st: middle_phase(st, full, fx, th, qh, kfull, ch, chalo, short, mr, *outs, *rest),
        pltpu.VMEM((SLABS * SLAB, SLAB), F32),
    )


def opening(tokens, queries, keys, cot, weights, short, mr):
    any_space, vmem = pl.BlockSpec(memory_space=pl.ANY), pl.BlockSpec(memory_space=pltpu.VMEM)
    whole = SLABS * SLAB
    mine, head = shape(ROWS, WIDTH), shape(SLAB, DH)
    dma = pltpu.SemaphoreType.DMA
    remotes = 6 + 4 + 8 + 12 + 2 + 2 + 6 + 12
    return pl.pallas_call(
        opening_kernel,
        out_shape=[
            mine,
            mine,
            *[shape(ROWS, SLABS * ROWS)] * HEADS,
            head,
            shape(3, SLAB, DH),
            head,
            shape(3 * 16, DH),
            shape(SLAB + HALO, DH, kind=F32),
            shape(HALO + SLAB + TAIL, DH, kind=F32),
        ],
        in_specs=[vmem] * 4 + [any_space] + [vmem] * 2,
        out_specs=[any_space] * 6 + [vmem] * 6,
        scratch_shapes=[
            pltpu.VMEM((SLAB, DH), BF),
            pltpu.VMEM((SLAB, DH), BF),
            pltpu.VMEM((SLAB, DH), BF),
            pltpu.VMEM((HALO, DH), BF),
            pltpu.VMEM((3, EXT, DH), BF),
            pltpu.VMEM((whole, DH), BF),
            pltpu.VMEM((ROWS, 8 * WIDTH), BF),
            pltpu.VMEM((3, ROWS, WIDTH), F32),
            pltpu.VMEM((3, ROWS, WIDTH), BF),
            pltpu.VMEM((SLAB, DH), BF),
            dma((remotes,)),
            dma((remotes,)),
            dma((3 + 3 + 2 + 1,)),
            pltpu.VMEM((SLAB, DH), BF),
            pltpu.VMEM((whole, DH), BF),
            pltpu.VMEM((DH, whole), BF),
            pltpu.VMEM((DH, whole), BF),
            pltpu.VMEM((whole, SLAB), BF),
            pltpu.VMEM((1, SLAB), F32),
            pltpu.VMEM((DH, SLAB), F32),
            pltpu.VMEM((DH, SLAB), BF),
            pltpu.VMEM((SLAB, DH), BF),
            pltpu.VMEM((1, SLAB), F32),
            pltpu.VMEM((SLAB, DH), BF),
            pltpu.VMEM((SLAB, DH), BF),
            pltpu.VMEM((DH, SLAB), F32),
            pltpu.VMEM((SLAB + HALO, DH), F32),
            pltpu.VMEM((SLAB, DH), F32),
            pltpu.VMEM((HALO, DH), BF),
            pltpu.VMEM((SLABS - 1, SLAB + HALO, DH), BF),
            pltpu.VMEM((SLABS - 1, SLAB, DH), BF),
            pltpu.VMEM((SLABS - 1, SLAB + HALO, DH), BF),
            pltpu.VMEM((SLABS - 1, SLAB, DH), BF),
            pltpu.VMEM((SLAB + HALO, DH), F32),
            pltpu.VMEM((SLAB + TAIL, DH), F32),
            pltpu.VMEM((SLAB + TAIL, DH), F32),
            pltpu.VMEM((SLAB + TAIL, DH), F32),
            pltpu.VMEM((3, EXT, DH), F32),
            pltpu.VMEM((3, SLAB + TAIL, DH), F32),
            pltpu.VMEM((TILE, SLAB + TAIL + MRLEN - TILE, DH), F32),
            pltpu.VMEM((TILE, TAPS, TILE, DH), F32),
            dma((SLABS - 1,)),
            dma((SLABS - 1,)),
            dma((SLABS - 1,)),
            dma((SLABS - 1,)),
            dma((22,)),
            dma((22,)),
            dma((6,)),
        ],
        compiler_params=pltpu.CompilerParams(
            collective_id=2, has_side_effects=True, vmem_limit_bytes=60 << 20
        ),
    )(tokens, queries, keys, cot, weights, short, mr)


def finale_kernel(
    fg, sg, dk, short_part, mg, pr, part0, part1, part2, part3, weights,
    grad_input, grad_feat, dk_home, small_home,
    w, tq, tqt, fgall, fgm, wsend, zr1, zr2, tsend, xr1, xr2, yr, ysend, sgh, slots, small, total, shifts, lines,
    send, recv, loc,
):
    mail = Courier(send, recv, loc)
    z, a = place()
    row, col = lax.axis_index("row"), lax.axis_index("col")
    side, core = lax.div(a, 2), lax.rem(a, 2)
    mate, far, far_mate = side * 2 + 1 - core, (1 - side) * 2 + core, (1 - side) * 2 + 1 - core
    up, down = turn(z, 1, SLABS), turn(z, -1, SLABS)
    right, left = turn(col, 1, 4), turn(col, -1, 4)
    half = ROWS // 2
    pair = 2 * ROWS

    mail.keep(fg, fgall.at[a])
    for d, part in enumerate((part0, part1, part2, part3)):
        mail.keep(part, tq.at[rows(turn(a, -d, HEADS), ROWS)])
    greeted = greet(around(z, a) + [{"row": 1 - row}, {"col": right}, {"col": left}])
    loads = [pltpu.make_async_copy(weights.at[j], w.at[j], loc.at[8 + j]) for j in range(3)]
    for load in loads:
        load.start()
    greeted()

    near_rows, far_rows = rows(side, pair), rows(1 - side, pair)
    direct = [
        mail.push(fg.at[:, rows(to, ROWS)], fgall.at[a, :, rows(to, ROWS)], at_ctx(z, to)) for to in (far, far_mate)
    ]
    to_mate = mail.push(fg, fgall.at[a], at_ctx(z, mate))
    second = mail.push(fg.at[:, near_rows], fgall.at[a, :, near_rows], at_ctx(z, far))
    mail.settle()

    for b in range(SLABS):
        tqt[pl.ds(b * ROWS, ROWS)] = tq[:, pl.ds(b * ROWS, ROWS)].T

    def weight_block(n, head, dz):
        rhs = jnp.concatenate([fgall[head, j] for j in range(3)], axis=1)
        lhs = tqt[rows(turn(z, dz, SLABS), ROWS)]
        out = jnp.dot(lhs, rhs, preferred_element_type=F32)
        for j in range(3):
            wsend[n, dz, j] = out[:, j * DH : (j + 1) * DH].astype(BF)

    def weight_first(n, head):
        weight_block(n, head, 2)
        keys = (
            mail.push(wsend.at[n, 2, :, pl.ds(0, half)], zr1.at[n, 0], at_ctx(up, a)),
            mail.push(wsend.at[n, 2, :, pl.ds(half, half)], zr1.at[n, 1], at_ctx(down, a)),
        )
        for dz in (1, 3, 0):
            weight_block(n, head, dz)
        return keys

    def weight_second(n, keys):
        top, bottom = pl.ds(0, half), pl.ds(half, half)
        mail.arrive(keys[0])
        wsend[n, 1, :, top] = (wsend[n, 1, :, top].astype(F32) + zr1[n, 0].astype(F32)).astype(BF)
        one = mail.push(wsend.at[n, 1], zr2.at[n, 0], at_ctx(up, a))
        mail.arrive(keys[1])
        wsend[n, 3, :, bottom] = (wsend[n, 3, :, bottom].astype(F32) + zr1[n, 1].astype(F32)).astype(BF)
        return one, mail.push(wsend.at[n, 3], zr2.at[n, 1], at_ctx(down, a))

    def weight_third(n, head, keys):
        for k in keys:
            mail.arrive(k)
        for j in range(3):
            grad_feat[j, :, cols(head)] = (
                wsend[n, 0, j].astype(F32) + zr2[n, 0, j].astype(F32) + zr2[n, 1, j].astype(F32)
            )

    ring = [weight_first(0, a)]
    mail.arrive(to_mate)
    ring.append(weight_first(1, mate))
    spread_shifts(shifts, pr, HALO - MRLEN + TILE, -1)
    tap_grads(shifts, mg, lines)
    small[pl.ds(0, MRLEN)] = lines[...].reshape(MRLEN, DH).astype(BF)
    small[pl.ds(MRLEN, short_part.shape[0])] = short_part[...]
    small_in = [mail.push(small, slots.at[d - 1], at_ctx(turn(z, d, SLABS), a)) for d in range(1, SLABS)]
    for k in direct:
        mail.arrive(k)
    relays = [
        mail.push(fgall.at[h, :, rows(a, ROWS)], fgall.at[h, :, rows(a, ROWS)], at_ctx(z, mate))
        for h in (far, far_mate)
    ]

    for n in range(2):
        ring[n] = weight_second(n, ring[n])
    for j in range(3):
        for h in range(HEADS):
            fgm[j, :, pl.ds(h * DH, DH)] = fgall[h, j, rows(a, ROWS)]
    for load in loads:
        load.wait()

    top, bottom = pl.ds(0, half), pl.ds(half, half)
    shares = (1 - row, row)

    def term_block(dc, n):
        columns = rows(shares[n] * 4 + turn(col, dc, 4), WIDTH)
        out = jnp.zeros((ROWS, WIDTH), F32)
        for j in range(3):
            out += lax.dot_general(fgm[j], w[j, columns], (((1,), (1,)), ((), ())), preferred_element_type=F32)
        tsend[dc, n] = out.astype(BF)

    firsts, seconds = [], []
    for n in range(2):
        term_block(2, n)
        firsts.append(
            (
                mail.push(tsend.at[2, n, top], xr1.at[0, n], {"col": right}),
                mail.push(tsend.at[2, n, bottom], xr1.at[1, n], {"col": left}),
            )
        )
    for n in range(2):
        term_block(1, n)
        term_block(3, n)
        mail.arrive(firsts[n][0])
        tsend[1, n, top] = (tsend[1, n, top].astype(F32) + xr1[0, n].astype(F32)).astype(BF)
        from_left = mail.push(tsend.at[1, n], xr2.at[0, n], {"col": right})
        mail.arrive(firsts[n][1])
        tsend[3, n, bottom] = (tsend[3, n, bottom].astype(F32) + xr1[1, n].astype(F32)).astype(BF)
        seconds.append((from_left, mail.push(tsend.at[3, n], xr2.at[1, n], {"col": left})))
    home_sg = []
    for d in range(1, HEADS):
        to = turn(a, d, HEADS)
        home_sg.append(mail.push(sg.at[rows(to, ROWS)], sgh.at[:, cols(a)], at_ctx(z, to)))
        mail.push(dk.at[rows(to, ROWS)], dk_home.at[:, cols(a)], at_ctx(z, to))
    mail.keep(sg.at[rows(a, ROWS)], sgh.at[:, cols(a)])
    mail.keep(dk.at[rows(a, ROWS)], dk_home.at[:, cols(a)])
    term_block(0, 0)
    term_block(0, 1)
    mail.arrive(second)
    relays.append(mail.push(fgall.at[far, :, far_rows], fgall.at[far, :, far_rows], at_ctx(z, mate)))
    for k in relays[:2]:
        mail.arrive(k)
    ring.append(weight_first(2, far))
    mail.arrive(relays[2])
    ring.append(weight_first(3, far_mate))

    def term_sum(n):
        for k in seconds[n]:
            mail.arrive(k)
        return tsend[0, n].astype(F32) + xr2[0, n].astype(F32) + xr2[1, n].astype(F32)

    ysend[...] = term_sum(0).astype(BF)
    across = mail.push(ysend, yr, {"row": 1 - row})
    ring[2] = weight_second(2, ring[2])
    ring[3] = weight_second(3, ring[3])

    for k in small_in:
        mail.arrive(k)
    total[...] = (small_sum(small, slots)).astype(BF)
    for d in range(1, HEADS):
        mail.push(total, small_home.at[:, cols(a)], at_ctx(z, turn(a, d, HEADS)))
    mail.keep(total, small_home.at[:, cols(a)])

    weight_third(0, a, ring[0])
    weight_third(1, mate, ring[1])
    for k in home_sg:
        mail.arrive(k)
    mail.settle()
    mail.arrive(across)
    grad_input[...] = (sgh[...].astype(F32) + term_sum(1) + yr[...].astype(F32)).astype(BF)
    weight_third(2, far, ring[2])
    weight_third(3, far_mate, ring[3])
    mail.finish()


def small_sum(small, slots):
    return small[...].astype(F32) + sum(slots[d].astype(F32) for d in range(SLABS - 1))


def finale(fg, sg, dk, short_part, mg, pr, parts, weights):
    lines = MRLEN + short_part.shape[0]
    any_space, vmem = pl.BlockSpec(memory_space=pl.ANY), pl.BlockSpec(memory_space=pltpu.VMEM)
    remotes = 1 + 3 + 3 + 6 + 6 + 16 + 8 + 1
    return pl.pallas_call(
        finale_kernel,
        out_shape=[
            shape(ROWS, WIDTH),
            shape(3, ROWS, WIDTH, kind=F32),
            shape(ROWS, WIDTH),
            shape(lines, WIDTH),
        ],
        in_specs=[any_space] * 3 + [vmem] * 3 + [any_space] * 5,
        out_specs=[vmem, vmem, any_space, any_space],
        scratch_shapes=[
            pltpu.VMEM(weights.shape, BF),
            pltpu.VMEM((SLAB, SLABS * ROWS), BF),
            pltpu.VMEM((SLABS * ROWS, SLAB), BF),
            pltpu.VMEM((HEADS, 3, SLAB, DH), BF),
            pltpu.VMEM((3, ROWS, WIDTH), BF),
            pltpu.VMEM((HEADS, SLABS, 3, ROWS, DH), BF),
            pltpu.VMEM((HEADS, 2, 3, ROWS // 2, DH), BF),
            pltpu.VMEM((HEADS, 2, 3, ROWS, DH), BF),
            pltpu.VMEM((4, 2, ROWS, WIDTH), BF),
            pltpu.VMEM((2, 2, ROWS // 2, WIDTH), BF),
            pltpu.VMEM((2, 2, ROWS, WIDTH), BF),
            pltpu.VMEM((ROWS, WIDTH), BF),
            pltpu.VMEM((ROWS, WIDTH), BF),
            pltpu.VMEM((ROWS, WIDTH), BF),
            pltpu.VMEM((SLABS - 1, lines, DH), BF),
            pltpu.VMEM((lines, DH), BF),
            pltpu.VMEM((lines, DH), BF),
            pltpu.VMEM((TILE, SLAB + TAIL + MRLEN - TILE, DH), F32),
            pltpu.VMEM((TAPS, TILE, DH), F32),
            pltpu.SemaphoreType.DMA((remotes,)),
            pltpu.SemaphoreType.DMA((remotes,)),
            pltpu.SemaphoreType.DMA((11,)),
        ],
        compiler_params=pltpu.CompilerParams(
            collective_id=5, has_side_effects=True, vmem_limit_bytes=56 << 20
        ),
    )(fg, sg, dk, short_part, mg, pr, *parts, weights)


def deliver_kernel(block, grad_q, grad_k, grad_in, grad_feat, small, block_o, in_o, feat_o, short_o, mr_o, q_o, k_o):
    feat_o[...] = grad_feat[...]
    block_o[...] = block[...]
    in_o[...] = grad_in[...]
    q_o[...] = grad_q[...]
    k_o[...] = grad_k[...]

    @pl.when(pl.program_id(0) == 0)
    def _():
        mr_o[...] = small[pl.ds(0, MRLEN)].astype(F32)
        for j in range(3):
            short_o[j] = small[pl.ds(MRLEN + 16 * j, 16)].astype(F32)[:SHORT]


def deliver(*ins):
    steps = 4

    def fixed(*dims):
        return pl.BlockSpec(dims, lambda n: (0,) * len(dims))

    mine = pl.BlockSpec((ROWS // steps, WIDTH), lambda n: (n, 0))
    feat = pl.BlockSpec((3, ROWS // steps, WIDTH), lambda n: (0, n, 0))
    out = shape(ROWS, WIDTH)
    return pl.pallas_call(
        deliver_kernel,
        grid=(steps,),
        out_shape=[
            out,
            out,
            shape(3, ROWS, WIDTH, kind=F32),
            shape(3, SHORT, WIDTH, kind=F32),
            shape(MRLEN, WIDTH, kind=F32),
            out,
            out,
        ],
        in_specs=[mine] * 4 + [feat, fixed(*ins[-1].shape)],
        out_specs=[mine, mine, feat, fixed(3, SHORT, WIDTH), fixed(MRLEN, WIDTH), mine, mine],
        compiler_params=pltpu.CompilerParams(vmem_limit_bytes=60 << 20),
    )(*ins)


def local(tokens, w_feat, short_filter, mr_filter, queries, key_rows, cotangent):
    weights = w_feat.transpose(1, 0, 2)
    short_taps = short_filter.transpose(1, 0, 2)
    block, grad_queries, *token_parts, sg, fg, dk, short_part, mg, pr = opening(
        tokens, queries, key_rows, cotangent, weights, short_taps, mr_filter
    )
    grad_input, grad_feat, grad_keys, small = finale(fg, sg, dk, short_part, mg, pr, token_parts, weights)
    block_out, grad_input, grad_feat, grad_short, grad_mr, grad_queries, grad_keys = deliver(
        block, grad_queries, grad_keys, grad_input, grad_feat, small
    )
    grad_feat, grad_short = grad_feat.transpose(1, 0, 2), grad_short.transpose(1, 0, 2)
    return (block_out, grad_input, grad_feat, grad_short, grad_mr, grad_queries, grad_keys)


def solution(mesh):
    placed = (
        P("ctx", ("row", "col")),
        P(None, None, ("row", "col")),
        P(None, None, ("row", "col")),
        P(None, ("row", "col")),
        P("ctx", ("row", "col")),
        P("ctx", ("row", "col")),
        P("ctx", ("row", "col")),
    )
    return jax.shard_map(
        local,
        mesh=mesh,
        in_specs=placed,
        out_specs=(
            P("ctx", ("row", "col")),
            P("ctx", ("row", "col")),
            P("ctx", None, ("row", "col")),
            P(None, None, ("row", "col")),
            P(None, ("row", "col")),
            P("ctx", ("row", "col")),
            P("ctx", ("row", "col")),
        ),
        check_vma=False,
    )
```

```python
import functools

import jax
import jax.numpy as jnp
from jax import lax
from jax.experimental import pallas as pl
from jax.experimental.pallas import tpu as pltpu
from jax.sharding import PartitionSpec as P

DH = 128
SHORT = 7
MRLEN = 128
HALO = 144
TAIL = 16
ROWS = 256
HEADS = 4
SLABS = 4
SLAB = ROWS * HEADS
EXT = HALO + SLAB + HALO
WIDTH = HEADS * DH
MESH = pl.DeviceIdType.MESH
BF = jnp.bfloat16
F32 = jnp.float32


def place():
    ctx = lax.axis_index("ctx")
    return lax.div(ctx, HEADS), lax.rem(ctx, HEADS)


def turn(index, step, size):
    return lax.rem(index + (step + size), size)


def at_ctx(z, a):
    return {"ctx": z * HEADS + a}


def cols(index, width=DH):
    return pl.ds(pl.multiple_of(index * width, width), width)


def rows(index, height, offset=0):
    return pl.ds(pl.multiple_of(index * height + offset, 16), height)


def greet(devices):
    barrier = pltpu.get_barrier_semaphore()
    for device in devices:
        pl.semaphore_signal(barrier, inc=1, device_id=device, device_id_type=MESH)
    return functools.partial(pl.semaphore_wait, barrier, len(devices))


class Courier:
    def __init__(self, send, recv, local):
        self.send, self.recv, self.local = send, recv, local
        self.remote, self.here = [], []
        self.arrived = set()
        self.settled = 0

    def push(self, src, dst, device):
        k = len(self.remote)
        copy = pltpu.make_async_remote_copy(
            src_ref=src,
            dst_ref=dst,
            send_sem=self.send.at[k],
            recv_sem=self.recv.at[k],
            device_id=device,
            device_id_type=MESH,
        )
        copy.start()
        self.remote.append(copy)
        return k

    def keep(self, src, dst):
        copy = pltpu.make_async_copy(src, dst, self.local.at[len(self.here)])
        copy.start()
        self.here.append(copy)

    def arrive(self, k):
        if k not in self.arrived:
            self.arrived.add(k)
            self.remote[k].wait_recv()

    def finish(self):
        for k in range(len(self.remote)):
            self.arrive(k)
        for copy in self.remote:
            copy.wait_send()
        self.settle()

    def settle(self):
        for copy in self.here[self.settled :]:
            copy.wait()
        self.settled = len(self.here)


def shape(*dims, kind=BF):
    return jax.ShapeDtypeStruct(dims, kind)


def slab_gather(mail, part, whole, z, a):
    up, down = turn(z, 1, SLABS), turn(z, -1, SLABS)
    mine = whole.at[rows(z, SLAB)]
    mail.keep(part, mine)
    return mail.push(part, mine, at_ctx(up, a)), mail.push(part, mine, at_ctx(down, a))


def slab_relay(mail, whole, z, a, from_down, from_up):
    up, down = turn(z, 1, SLABS), turn(z, -1, SLABS)
    half = SLAB // 2
    mail.arrive(from_down)
    lower = whole.at[pl.ds(pl.multiple_of(down * SLAB, 16), half)]
    mail.push(lower, lower, at_ctx(up, a))
    mail.arrive(from_up)
    upper = whole.at[pl.ds(pl.multiple_of(up * SLAB + half, 16), half)]
    mail.push(upper, upper, at_ctx(down, a))


def front_phase(
    greeted, w, tokens, queries, keys, cot, weights, th, qh, ch, chalo, fx, kfull, full, acc, feats, kh, send, recv, loc,
):
    mail = Courier(send, recv, loc)
    z, a = place()
    row, col = lax.axis_index("row"), lax.axis_index("col")
    other = 1 - row
    right, left, across = turn(col, 1, 4), turn(col, -1, 4), turn(col, 2, 4)
    up, down = turn(z, 1, SLABS), turn(z, -1, SLABS)
    for j in range(3):
        mail.keep(weights.at[j], w.at[j])
    full[:, cols(row * 4 + col, WIDTH)] = tokens[...]
    kh[rows(a, ROWS)] = keys[:, cols(a)]
    acc[...] = jnp.zeros_like(acc)
    greeted()

    half, quarter = ROWS // 2, ROWS // 4

    def piece(r, c, h):
        return full.at[pl.ds(h * half, half), cols(r * 4 + c, WIDTH)]

    def part(r, c, h, n):
        return full.at[pl.ds(h * half + n * quarter, quarter), cols(r * 4 + c, WIDTH)]

    def project(r, c, h):
        here = pl.ds(h * half, half)
        lhs = full[here, cols(r * 4 + c, WIDTH)]
        for j in range(3):
            acc[j, here] += jnp.dot(lhs, w[j, rows(r * 4 + c, WIDTH)], preferred_element_type=F32)

    def launch(h):
        src, dst = tokens.at[pl.ds(h * half, half)], piece(row, col, h)
        return [mail.push(src, dst, device) for device in ({"row": other}, {"col": right}, {"col": left})]

    def sideways(h, arrival):
        mail.arrive(arrival)
        dst = piece(other, col, h)
        return [mail.push(dst, dst, device) for device in ({"col": right}, {"col": left})]

    def relay(r, h, from_left, from_right):
        mail.arrive(from_left)
        one = mail.push(part(r, left, h, 0), part(r, left, h, 0), {"col": right})
        mail.arrive(from_right)
        return one, mail.push(part(r, right, h, 1), part(r, right, h, 1), {"col": left})

    def finish_half(h, relays):
        for r, keys_in in zip((row, other), relays):
            for k in keys_in:
                mail.arrive(k)
            project(r, across, h)
        here = pl.ds(h * half, half)
        for j in range(3):
            feats[j, here] = acc[j, here].astype(BF)
        there = pl.ds(pl.multiple_of(a * ROWS + (HALO + h * half), 16), half)
        for d in range(1, HEADS):
            to = turn(a, d, HEADS)
            mail.push(feats.at[:, here, cols(to)], fx.at[:, there], at_ctx(z, to))
        mail.keep(feats.at[:, here, cols(a)], fx.at[:, there])

    first = launch(0)
    mail.settle()
    project(row, col, 0)
    first_side = sideways(0, first[0])
    second = launch(1)
    key_parts = []
    for src, dst in ((keys, kh), (tokens, th), (queries, qh), (cot, ch)):
        for d in range(1, HEADS):
            to = turn(a, d, HEADS)
            k = mail.push(src.at[:, cols(to)], dst.at[rows(a, ROWS)], at_ctx(z, to))
            if dst is kh:
                key_parts.append(k)
        if dst is not kh:
            mail.keep(src.at[:, cols(a)], dst.at[rows(a, ROWS)])
    project(other, col, 0)
    relays = [[relay(row, 0, *first[1:])], []]
    second_side = sideways(1, second[0])
    relays[0].append(relay(other, 0, *first_side))
    for r in (row, other):
        project(r, left, 0)
        project(r, right, 0)
    relays[1].append(relay(row, 1, *second[1:]))
    finish_half(0, relays[0])
    relays[1].append(relay(other, 1, *second_side))
    for k in key_parts:
        mail.arrive(k)
    gathered = slab_gather(mail, kh, kfull, z, a)
    for r in (row, other):
        project(r, col, 1)
        project(r, left, 1)
        project(r, right, 1)
    finish_half(1, relays[1])

    n = len(mail.remote) + 2

    def edge(src, dst, k, b, device):
        return pltpu.make_async_remote_copy(
            src_ref=src,
            dst_ref=dst,
            send_sem=mail.send.at[k + 3 * b],
            recv_sem=mail.recv.at[k],
            device_id=device,
            device_id_type=MESH,
        )

    def first_rows(b):
        lanes = pl.ds(b * DH, DH)
        return (
            edge(feats.at[:, pl.ds(0, HALO), lanes], fx.at[:, pl.ds(HALO + SLAB, HALO)], n, b, at_ctx(down, b)),
            edge(cot.at[pl.ds(0, HALO), lanes], chalo, n + 1, b, at_ctx(down, b)),
        )

    def last_rows(b):
        lanes = pl.ds(b * DH, DH)
        return (edge(feats.at[:, pl.ds(ROWS - HALO, HALO), lanes], fx.at[:, pl.ds(0, HALO)], n + 2, b, at_ctx(up, b)),)

    @pl.when(a == 0)
    def _():
        for b in range(HEADS):
            for copy in first_rows(b):
                copy.start()

    @pl.when(a == HEADS - 1)
    def _():
        for b in range(HEADS):
            for copy in last_rows(b):
                copy.start()

    slab_relay(mail, kfull, z, a, *gathered)
    mail.finish()
    for copy in first_rows(0) + last_rows(0):
        copy.wait_recv()

    @pl.when(a == 0)
    def _():
        for b in range(HEADS):
            for copy in first_rows(b):
                copy.wait_send()

    @pl.when(a == HEADS - 1)
    def _():
        for b in range(HEADS):
            for copy in last_rows(b):
                copy.wait_send()


def around(z, a):
    return [at_ctx(turn(z, d, SLABS), a) for d in range(1, SLABS)] + [
        at_ctx(z, turn(a, d, HEADS)) for d in range(1, HEADS)
    ]


def home(mail, src, dst, z, a):
    for d in range(1, HEADS):
        to = turn(a, d, HEADS)
        mail.push(src.at[rows(to, ROWS)], dst.at[:, cols(a)], at_ctx(z, to))
    mail.keep(src.at[rows(a, ROWS)], dst.at[:, cols(a)])


CHUNK = 512


def dot(x, y):
    return jnp.dot(x, y, preferred_element_type=F32)


def dot_t(x, y):
    return lax.dot_general(x, y, (((1,), (1,)), ((), ())), preferred_element_type=F32)


GROUP = 40
TILE = 8
TAPS = MRLEN // TILE
SPAN = 13


def spread_taps(spread, taps, a):
    for i in range(MRLEN):
        spread[i % TILE, i // TILE] = jnp.broadcast_to(taps[pl.ds(i, 1), cols(a)], (TILE, DH))


def spread_shifts(shifts, rows_of, first, sign):
    count = shifts.shape[1]
    for r in range(TILE):
        shifts[r] = rows_of[pl.ds(first + sign * r, count)]


def long_filter(shifts, spread, backward, store):
    def step(g, carry):
        base = pl.multiple_of(g * (SPAN * TILE), TILE)

        def shift(r, totals):
            totals = list(totals)
            taps = [spread[r, m] for m in range(TAPS)]
            for t in range(SPAN + TAPS - 1):
                tile = shifts[r, pl.ds(base + t * TILE, TILE)]
                for n in range(SPAN):
                    m = t - n if backward else n + TAPS - 1 - t
                    if 0 <= m < TAPS:
                        totals[n] += taps[m] * tile
            return tuple(totals)

        totals = lax.fori_loop(0, TILE, shift, tuple(jnp.zeros((TILE, DH), F32) for _ in range(SPAN)))
        for n in range(SPAN):
            store(pl.ds(base + n * TILE, TILE), totals[n])
        return carry

    lax.fori_loop(0, (SLAB + TAIL) // (SPAN * TILE), step, 0)


def tap_grads(shifts, grads, lines):
    count = 16

    def shift(r, carry):
        def step(g, sums):
            sums = list(sums)
            base = pl.multiple_of(g * (count * TILE), TILE)
            own = [grads[pl.ds(base + n * TILE, TILE)] for n in range(count)]
            for t in range(count + TAPS - 1):
                tile = shifts[r, pl.ds(base + t * TILE, TILE)]
                for n in range(count):
                    m = n + TAPS - 1 - t
                    if 0 <= m < TAPS:
                        sums[m] += own[n] * tile
            return tuple(sums)

        zero = tuple(jnp.zeros((TILE, DH), F32) for _ in range(TAPS))
        sums = lax.fori_loop(0, SLAB // (count * TILE), step, zero)
        for m in range(TAPS):
            lines[m, pl.ds(r, 1)] = jnp.sum(sums[m], axis=0, keepdims=True)
        return carry

    lax.fori_loop(0, TILE, shift, 0)


def hyena(z, a, fx, short, tok, stream, qm, km, vm, lm, pr, feat, shifts, spread):
    keep_head = (z > 0).astype(F32)
    keep_tail = (z < SLABS - 1).astype(F32)
    for j in range(3):
        feat[j, pl.ds(0, HALO)] = fx[j, pl.ds(0, HALO)].astype(F32) * keep_head
        feat[j, pl.ds(HALO, SLAB)] = fx[j, pl.ds(HALO, SLAB)].astype(F32)
        feat[j, pl.ds(HALO + SLAB, HALO)] = fx[j, pl.ds(HALO + SLAB, HALO)].astype(F32) * keep_tail

    taps = [[short[j, pl.ds(s, 1), cols(a)] for s in range(SHORT)] for j in range(3)]

    def mixed(j, base, count):
        total = taps[j][0] * feat[j, pl.ds(base, count)]
        for s in range(1, SHORT):
            total += taps[j][s] * feat[j, pl.ds(base - s, count)]
        return total

    pr[pl.ds(0, 16)] = jnp.zeros((16, DH), F32)

    def head_step(g, carry):
        base = pl.multiple_of(16 + g * 16, 16)
        pr[pl.ds(base, 16)] = (mixed(1, base, 16) * mixed(2, base, 16)).astype(BF).astype(F32)
        return carry

    lax.fori_loop(0, (HALO - 16) // 16, head_step, 0)

    def mix_step(g, carry):
        base = pl.multiple_of(HALO + g * GROUP, 8)
        here = pl.ds(pl.multiple_of(g * GROUP, 8), GROUP)
        key, value = mixed(1, base, GROUP), mixed(2, base, GROUP)
        km[here] = key
        vm[here] = value
        qm[here] = mixed(0, base, GROUP)
        pr[pl.ds(base, GROUP)] = (key * value).astype(BF).astype(F32)
        return carry

    lax.fori_loop(0, (SLAB + TAIL) // GROUP, mix_step, 0)

    def tail_step(g, carry):
        here = pl.multiple_of(SLAB + TAIL + g * 16, 16)
        qm[pl.ds(here, 16)] = mixed(0, here + HALO, 16)
        return carry

    lax.fori_loop(0, (HALO - TAIL) // 16, tail_step, 0)
    spread_shifts(shifts, pr, HALO - MRLEN + TILE, -1)

    def store(here, total):
        lm[here] = total

    long_filter(shifts, spread, False, store)
    own = pl.ds(0, SLAB)
    stream[...] = (tok[...].astype(F32) + qm[own] * lm[own]).astype(BF)


def back(z, a, dv, ch, chalo, short, qm, km, vm, lm, feat, sg, fg, short_part, mg, stack, shifts, spread):
    keep_tail = (z < SLABS - 1).astype(F32)
    own, halo = pl.ds(0, SLAB), pl.ds(SLAB, HALO)
    grad = (ch[...].astype(F32) + dv[own]).astype(BF)
    sg[...] = grad
    mg[own] = (grad.astype(F32) * qm[own]).astype(BF).astype(F32)
    grad_halo = (chalo[...].astype(F32) + dv[halo]).astype(BF).astype(F32) * keep_tail
    mg[halo] = (grad_halo * qm[halo]).astype(BF).astype(F32)
    stack[0, own] = grad.astype(F32) * lm[own]
    stack[0, pl.ds(SLAB, TAIL)] = grad_halo[:TAIL] * lm[pl.ds(SLAB, TAIL)]
    spread_shifts(shifts, mg, 0, 1)

    def store(here, total):
        stack[1, here] = total * vm[here]
        stack[2, here] = total * km[here]

    long_filter(shifts, spread, True, store)
    for j in range(3):
        taps = [short[j, pl.ds(s, 1), cols(a)] for s in range(SHORT)]

        def short_step(g, sums):
            base = pl.multiple_of(g * 32, 32)
            line = stack[j, pl.ds(base, 32)]
            total = taps[0] * line
            for s in range(1, SHORT):
                total += taps[s] * stack[j, pl.ds(base + s, 32)]
            fg[j, pl.ds(base, 32)] = total.astype(BF)
            out = []
            for s in range(SHORT):
                term = line * feat[j, pl.ds(base + HALO - s, 32)]
                out.append(sums[s] + (term[0:8] + term[8:16] + term[16:24] + term[24:32]))
            return tuple(out)

        sums = lax.fori_loop(0, SLAB // 32, short_step, tuple(jnp.zeros((8, DH), F32) for _ in range(SHORT)))
        lines = [jnp.sum(t, axis=0, keepdims=True) for t in sums]
        short_part[pl.ds(16 * j, 16)] = jnp.concatenate(lines + [jnp.zeros((16 - SHORT, DH), F32)], axis=0).astype(BF)


def middle_phase(
    st, full, fx, tok, q, k, ct, chalo, short, mr,
    block_home, dq_home, part0, part1, part2, part3, sg, fg, dk, short_part, mg, pr,
    stream, v, kt, vt, pt, tops, outs, ctt, cs, delta, block, dq, dqt, dv, dka, edge, dv_out, dk_out, dv_in, dk_in,
    qm, km, vm, lm, feat, stack, shifts, spread,
    dv_send, dv_recv, dk_send, dk_recv, send, recv, loc,
):
    mail = Courier(send, recv, loc)
    z, a = place()
    scale = DH ** -0.5
    gain = scale * 1.4426950408889634
    mine = rows(z, SLAB)
    up, down = at_ctx(turn(z, 1, SLABS), a), at_ctx(turn(z, -1, SLABS), a)
    spread_taps(spread, mr, a)

    def turn_keys(s, carry):
        kt[:, cols(s, SLAB)] = k[rows(s, SLAB)].T
        return carry

    hyena(z, a, fx, short, tok, stream, qm, km, vm, lm, pr, feat, shifts, spread)
    from_down = mail.push(stream, v.at[mine], up)
    from_up = mail.push(stream, v.at[mine], down)
    v[mine] = stream[...]
    for d, part in enumerate((part0, part1, part2, part3)):
        to = turn(a, d, HEADS)
        for n in range(SLABS):
            piece, slot = full.at[:, cols(n * HEADS + to, ROWS)], part.at[:, pl.ds(n * ROWS, ROWS)]
            if d:
                mail.push(piece, slot, at_ctx(z, to))
            else:
                mail.keep(piece, slot)

    def lanes_of(i):
        return pl.ds(i * ROWS, ROWS)

    def slots(c):
        return pl.ds(pl.multiple_of(SLAB + c * CHUNK, CHUNK), CHUNK)

    def keys_of(c):
        return pl.ds(pl.multiple_of(c * CHUNK, CHUNK), CHUNK)

    after = lax.broadcasted_iota(jnp.int32, (ROWS, ROWS), 0) > lax.broadcasted_iota(jnp.int32, (ROWS, ROWS), 1)
    for i in range(HEADS):
        span = ROWS * (i + 1)
        scores = dot_t(k[pl.ds(pl.multiple_of(z * SLAB, SLAB), span)], q[lanes_of(i)])
        corner = jnp.where(after, -1e30, scores[span - ROWS :])
        top = jnp.max(corner, axis=0, keepdims=True)
        if i:
            top = jnp.maximum(top, jnp.max(scores[: span - ROWS], axis=0, keepdims=True))
            st[pl.ds(0, span - ROWS), lanes_of(i)] = scores[: span - ROWS]
        st[pl.ds(span - ROWS, ROWS), lanes_of(i)] = corner
        tops[:, lanes_of(i)] = top

    def score_step(c, top):
        past = dot_t(k[keys_of(c)], q[...])
        st[slots(c)] = past
        return jnp.maximum(top, jnp.max(past, axis=0, keepdims=True))

    top = lax.fori_loop(0, z * (SLAB // CHUNK), score_step, tops[...]) * gain

    half = SLAB // 2
    mail.arrive(from_down)
    lower = v.at[pl.ds(pl.multiple_of(turn(z, -1, SLABS) * SLAB, SLAB), half)]
    low = mail.push(lower, lower, up)
    mail.arrive(from_up)
    upper = v.at[pl.ds(pl.multiple_of(turn(z, 1, SLABS) * SLAB + half, half), half)]
    high = mail.push(upper, upper, down)

    for i in range(HEADS):
        span = ROWS * (i + 1)
        p = jnp.exp2(st[pl.ds(0, span), lanes_of(i)] * gain - top[:, i * ROWS : (i + 1) * ROWS])
        tops[:, lanes_of(i)] = jnp.sum(p, axis=0, keepdims=True)
        pt[pl.ds(0, span), lanes_of(i)] = p.astype(BF)

    def weigh_step(c, total):
        p = jnp.exp2(st[slots(c)] * gain - top)
        pt[slots(c)] = p.astype(BF)
        return total + jnp.sum(p, axis=0, keepdims=True)

    inverse = 1.0 / lax.fori_loop(0, z * (SLAB // CHUNK), weigh_step, tops[...])
    lax.fori_loop(0, z + 1, turn_keys, 0)
    mail.arrive(low)
    mail.arrive(high)

    def turn_values(s, carry):
        vt[:, cols(s, SLAB)] = v[rows(s, SLAB)].T
        return carry

    lax.fori_loop(0, z + 1, turn_values, 0)
    for i in range(HEADS):
        span = ROWS * (i + 1)
        outs[:, lanes_of(i)] = dot(vt[:, pl.ds(pl.multiple_of(z * SLAB, SLAB), span)], pt[pl.ds(0, span), lanes_of(i)])

    def attend_step(c, carry):
        outs[...] += dot(vt[:, keys_of(c)], pt[slots(c)])
        return carry

    lax.fori_loop(0, z * (SLAB // CHUNK), attend_step, 0)
    out = outs[...] * inverse
    ctt[...] = (ct[...].astype(F32).T * inverse).astype(BF)
    cs[...] = ctt[...].T
    delta[...] = jnp.sum(ctt[...].astype(F32) * out, axis=0, keepdims=True)

    for i in reversed(range(HEADS)):
        span = ROWS * (i + 1)
        part = dot(pt[pl.ds(0, span), lanes_of(i)], cs[lanes_of(i)])
        if i == HEADS - 1:
            dv[pl.ds(0, SLAB)] = part
        else:
            dv[pl.ds(0, span)] += part
    dv[pl.ds(SLAB, HALO)] = jnp.zeros((HALO, DH), F32)
    edge[...] = dv[pl.ds(0, HALO)].astype(BF)

    def parcel(d, to, kind):
        src, dst, sent, got = ((dv_out, dv_in, dv_send, dv_recv), (dk_out, dk_in, dk_send, dk_recv))[kind]
        return pltpu.make_async_remote_copy(
            src_ref=src.at[d - 1],
            dst_ref=dst.at[d - 1],
            send_sem=sent.at[d - 1],
            recv_sem=got.at[d - 1],
            device_id=at_ctx(to, a),
            device_id_type=MESH,
        )

    def value_step(d, carry):
        s = z - d
        dv_out[d - 1, pl.ds(SLAB, HALO)] = edge[...]
        for n in range(SLAB // CHUNK):
            part = dot(pt[slots(s * (SLAB // CHUNK) + n)], cs[...]).astype(BF)
            dv_out[d - 1, pl.ds(n * CHUNK, CHUNK)] = part
            if n == 0:
                edge[...] = part[:HALO]
        parcel(d, s, 0).start()
        return carry

    lax.fori_loop(1, z + 1, value_step, 0)
    block[...] = (stream[...].astype(F32) + out.T).astype(BF)
    home(mail, block, block_home, z, a)

    for i in reversed(range(HEADS)):
        span = ROWS * (i + 1)
        here = pl.ds(pl.multiple_of(z * SLAB, SLAB), span)
        p = pt[pl.ds(0, span), lanes_of(i)]
        dp = dot(v[here], ctt[:, lanes_of(i)])
        ds = (p.astype(F32) * (dp - delta[:, lanes_of(i)])).astype(BF)
        part = dot(ds, q[lanes_of(i)])
        dqt[:, lanes_of(i)] = dot(kt[:, here], ds)
        if i == HEADS - 1:
            dka[...] = part
        else:
            dka[pl.ds(0, span)] += part

    def key_step(d, carry):
        s = z - d
        for n in range(SLAB // CHUNK):
            c = s * (SLAB // CHUNK) + n
            dp = dot(v[keys_of(c)], ctt[...])
            ds = (pt[slots(c)].astype(F32) * (dp - delta[...])).astype(BF)
            dk_out[d - 1, pl.ds(n * CHUNK, CHUNK)] = (dot(ds, q[...]) * scale).astype(BF)
            dqt[...] += dot(kt[:, keys_of(c)], ds)
        parcel(d, s, 1).start()
        return carry

    lax.fori_loop(1, z + 1, key_step, 0)
    dq[...] = (dqt[...].T * scale).astype(BF)
    home(mail, dq, dq_home, z, a)

    def add_values(d, carry):
        parcel(d, turn(z, d, SLABS), 0).wait_recv()
        dv[...] += dv_in[d - 1].astype(F32)
        return carry

    lax.fori_loop(1, SLABS - z, add_values, 0)
    back(z, a, dv, ct, chalo, short, qm, km, vm, lm, feat, sg, fg, short_part, mg, stack, shifts, spread)
    dka[...] = dka[...] * scale

    def add_keys(d, carry):
        parcel(d, turn(z, d, SLABS), 1).wait_recv()
        dka[...] += dk_in[d - 1].astype(F32)
        return carry

    lax.fori_loop(1, SLABS - z, add_keys, 0)
    dk[...] = dka[...].astype(BF)
    mail.finish()

    def sent_step(d, carry):
        for kind in range(2):
            parcel(d, turn(z, -d, SLABS), kind).wait_send()
        return carry

    lax.fori_loop(1, z + 1, sent_step, 0)


FRONT_REFS = 13
OUT_REFS = 12


def opening_kernel(tokens, queries, keys, cot, weights, short, mr, *refs):
    outs, held, rest = refs[:OUT_REFS], refs[OUT_REFS : OUT_REFS + FRONT_REFS], refs[OUT_REFS + FRONT_REFS :]
    th, qh, ch, chalo, fx, kfull, full = held[:7]
    z, a = place()
    row, col = lax.axis_index("row"), lax.axis_index("col")
    greeted = greet(
        [{"row": 1 - row}, {"col": turn(col, 1, 4)}, {"col": turn(col, -1, 4)}]
        + [at_ctx(z, turn(a, d, HEADS)) for d in range(1, HEADS)]
        + [at_ctx(turn(z, d, SLABS), b) for d in (1, -1) for b in range(HEADS)]
        + [at_ctx(turn(z, 2, SLABS), a)]
    )
    pl.run_scoped(
        lambda w: front_phase(greeted, w, tokens, queries, keys, cot, weights, *held), pltpu.VMEM(weights.shape, BF)
    )
    pl.run_scoped(
        lambda st: middle_phase(st, full, fx, th, qh, kfull, ch, chalo, short, mr, *outs, *rest),
        pltpu.VMEM((SLABS * SLAB, SLAB), F32),
    )


def opening(tokens, queries, keys, cot, weights, short, mr):
    any_space, vmem = pl.BlockSpec(memory_space=pl.ANY), pl.BlockSpec(memory_space=pltpu.VMEM)
    whole = SLABS * SLAB
    mine, head = shape(ROWS, WIDTH), shape(SLAB, DH)
    dma = pltpu.SemaphoreType.DMA
    remotes = 6 + 4 + 8 + 12 + 2 + 2 + 6 + 12
    return pl.pallas_call(
        opening_kernel,
        out_shape=[
            mine,
            mine,
            *[shape(ROWS, SLABS * ROWS)] * HEADS,
            head,
            shape(3, SLAB, DH),
            head,
            shape(3 * 16, DH),
            shape(SLAB + HALO, DH, kind=F32),
            shape(HALO + SLAB + TAIL, DH, kind=F32),
        ],
        in_specs=[vmem] * 4 + [any_space] + [vmem] * 2,
        out_specs=[any_space] * 6 + [vmem] * 6,
        scratch_shapes=[
            pltpu.VMEM((SLAB, DH), BF),
            pltpu.VMEM((SLAB, DH), BF),
            pltpu.VMEM((SLAB, DH), BF),
            pltpu.VMEM((HALO, DH), BF),
            pltpu.VMEM((3, EXT, DH), BF),
            pltpu.VMEM((whole, DH), BF),
            pltpu.VMEM((ROWS, 8 * WIDTH), BF),
            pltpu.VMEM((3, ROWS, WIDTH), F32),
            pltpu.VMEM((3, ROWS, WIDTH), BF),
            pltpu.VMEM((SLAB, DH), BF),
            dma((remotes,)),
            dma((remotes,)),
            dma((3 + 3 + 2 + 1,)),
            pltpu.VMEM((SLAB, DH), BF),
            pltpu.VMEM((whole, DH), BF),
            pltpu.VMEM((DH, whole), BF),
            pltpu.VMEM((DH, whole), BF),
            pltpu.VMEM((whole, SLAB), BF),
            pltpu.VMEM((1, SLAB), F32),
            pltpu.VMEM((DH, SLAB), F32),
            pltpu.VMEM((DH, SLAB), BF),
            pltpu.VMEM((SLAB, DH), BF),
            pltpu.VMEM((1, SLAB), F32),
            pltpu.VMEM((SLAB, DH), BF),
            pltpu.VMEM((SLAB, DH), BF),
            pltpu.VMEM((DH, SLAB), F32),
            pltpu.VMEM((SLAB + HALO, DH), F32),
            pltpu.VMEM((SLAB, DH), F32),
            pltpu.VMEM((HALO, DH), BF),
            pltpu.VMEM((SLABS - 1, SLAB + HALO, DH), BF),
            pltpu.VMEM((SLABS - 1, SLAB, DH), BF),
            pltpu.VMEM((SLABS - 1, SLAB + HALO, DH), BF),
            pltpu.VMEM((SLABS - 1, SLAB, DH), BF),
            pltpu.VMEM((SLAB + HALO, DH), F32),
            pltpu.VMEM((SLAB + TAIL, DH), F32),
            pltpu.VMEM((SLAB + TAIL, DH), F32),
            pltpu.VMEM((SLAB + TAIL, DH), F32),
            pltpu.VMEM((3, EXT, DH), F32),
            pltpu.VMEM((3, SLAB + TAIL, DH), F32),
            pltpu.VMEM((TILE, SLAB + TAIL + MRLEN - TILE, DH), F32),
            pltpu.VMEM((TILE, TAPS, TILE, DH), F32),
            dma((SLABS - 1,)),
            dma((SLABS - 1,)),
            dma((SLABS - 1,)),
            dma((SLABS - 1,)),
            dma((22,)),
            dma((22,)),
            dma((6,)),
        ],
        compiler_params=pltpu.CompilerParams(
            collective_id=2, has_side_effects=True, vmem_limit_bytes=60 << 20
        ),
    )(tokens, queries, keys, cot, weights, short, mr)


def finale_kernel(
    fg, sg, dk, short_part, mg, pr, part0, part1, part2, part3, weights,
    grad_input, grad_feat, dk_home, small_home,
    w, tq, tqt, fgall, fgm, wsend, zr1, zr2, tsend, xr1, xr2, yr, ysend, sgh, slots, small, total, shifts, lines,
    send, recv, loc,
):
    mail = Courier(send, recv, loc)
    z, a = place()
    row, col = lax.axis_index("row"), lax.axis_index("col")
    side, core = lax.div(a, 2), lax.rem(a, 2)
    mate, far, far_mate = side * 2 + 1 - core, (1 - side) * 2 + core, (1 - side) * 2 + 1 - core
    up, down = turn(z, 1, SLABS), turn(z, -1, SLABS)
    right, left = turn(col, 1, 4), turn(col, -1, 4)
    half = ROWS // 2
    pair = 2 * ROWS

    mail.keep(fg, fgall.at[a])
    for d, part in enumerate((part0, part1, part2, part3)):
        mail.keep(part, tq.at[rows(turn(a, -d, HEADS), ROWS)])
    greeted = greet(around(z, a) + [{"row": 1 - row}, {"col": right}, {"col": left}])
    loads = [pltpu.make_async_copy(weights.at[j], w.at[j], loc.at[8 + j]) for j in range(3)]
    for load in loads:
        load.start()
    greeted()

    near_rows, far_rows = rows(side, pair), rows(1 - side, pair)
    direct = [
        mail.push(fg.at[:, rows(to, ROWS)], fgall.at[a, :, rows(to, ROWS)], at_ctx(z, to)) for to in (far, far_mate)
    ]
    to_mate = mail.push(fg, fgall.at[a], at_ctx(z, mate))
    second = mail.push(fg.at[:, near_rows], fgall.at[a, :, near_rows], at_ctx(z, far))
    mail.settle()

    for b in range(SLABS):
        tqt[pl.ds(b * ROWS, ROWS)] = tq[:, pl.ds(b * ROWS, ROWS)].T

    def weight_block(n, head, dz):
        rhs = jnp.concatenate([fgall[head, j] for j in range(3)], axis=1)
        lhs = tqt[rows(turn(z, dz, SLABS), ROWS)]
        out = jnp.dot(lhs, rhs, preferred_element_type=F32)
        for j in range(3):
            wsend[n, dz, j] = out[:, j * DH : (j + 1) * DH].astype(BF)

    def weight_first(n, head):
        weight_block(n, head, 2)
        keys = (
            mail.push(wsend.at[n, 2, :, pl.ds(0, half)], zr1.at[n, 0], at_ctx(up, a)),
            mail.push(wsend.at[n, 2, :, pl.ds(half, half)], zr1.at[n, 1], at_ctx(down, a)),
        )
        for dz in (1, 3, 0):
            weight_block(n, head, dz)
        return keys

    def weight_second(n, keys):
        top, bottom = pl.ds(0, half), pl.ds(half, half)
        mail.arrive(keys[0])
        wsend[n, 1, :, top] = (wsend[n, 1, :, top].astype(F32) + zr1[n, 0].astype(F32)).astype(BF)
        one = mail.push(wsend.at[n, 1], zr2.at[n, 0], at_ctx(up, a))
        mail.arrive(keys[1])
        wsend[n, 3, :, bottom] = (wsend[n, 3, :, bottom].astype(F32) + zr1[n, 1].astype(F32)).astype(BF)
        return one, mail.push(wsend.at[n, 3], zr2.at[n, 1], at_ctx(down, a))

    def weight_third(n, head, keys):
        for k in keys:
            mail.arrive(k)
        for j in range(3):
            grad_feat[j, :, cols(head)] = (
                wsend[n, 0, j].astype(F32) + zr2[n, 0, j].astype(F32) + zr2[n, 1, j].astype(F32)
            )

    ring = [weight_first(0, a)]
    mail.arrive(to_mate)
    ring.append(weight_first(1, mate))
    spread_shifts(shifts, pr, HALO - MRLEN + TILE, -1)
    for k in direct:
        mail.arrive(k)
    relays = [
        mail.push(fgall.at[h, :, rows(a, ROWS)], fgall.at[h, :, rows(a, ROWS)], at_ctx(z, mate))
        for h in (far, far_mate)
    ]

    for n in range(2):
        ring[n] = weight_second(n, ring[n])
    for j in range(3):
        for h in range(HEADS):
            fgm[j, :, pl.ds(h * DH, DH)] = fgall[h, j, rows(a, ROWS)]
    for load in loads:
        load.wait()

    top, bottom = pl.ds(0, half), pl.ds(half, half)
    shares = (1 - row, row)

    def term_block(dc, n):
        columns = rows(shares[n] * 4 + turn(col, dc, 4), WIDTH)
        out = jnp.zeros((ROWS, WIDTH), F32)
        for j in range(3):
            out += lax.dot_general(fgm[j], w[j, columns], (((1,), (1,)), ((), ())), preferred_element_type=F32)
        tsend[dc, n] = out.astype(BF)

    firsts, seconds = [], []
    for n in range(2):
        term_block(2, n)
        firsts.append(
            (
                mail.push(tsend.at[2, n, top], xr1.at[0, n], {"col": right}),
                mail.push(tsend.at[2, n, bottom], xr1.at[1, n], {"col": left}),
            )
        )
    for n in range(2):
        term_block(1, n)
        term_block(3, n)
        if n == 0:
            tap_grads(shifts, mg, lines)
            small[pl.ds(0, MRLEN)] = lines[...].reshape(MRLEN, DH).astype(BF)
            small[pl.ds(MRLEN, short_part.shape[0])] = short_part[...]
            small_in = [mail.push(small, slots.at[d - 1], at_ctx(turn(z, d, SLABS), a)) for d in range(1, SLABS)]
        mail.arrive(firsts[n][0])
        tsend[1, n, top] = (tsend[1, n, top].astype(F32) + xr1[0, n].astype(F32)).astype(BF)
        from_left = mail.push(tsend.at[1, n], xr2.at[0, n], {"col": right})
        mail.arrive(firsts[n][1])
        tsend[3, n, bottom] = (tsend[3, n, bottom].astype(F32) + xr1[1, n].astype(F32)).astype(BF)
        seconds.append((from_left, mail.push(tsend.at[3, n], xr2.at[1, n], {"col": left})))
    home_sg = []
    for d in range(1, HEADS):
        to = turn(a, d, HEADS)
        home_sg.append(mail.push(sg.at[rows(to, ROWS)], sgh.at[:, cols(a)], at_ctx(z, to)))
        mail.push(dk.at[rows(to, ROWS)], dk_home.at[:, cols(a)], at_ctx(z, to))
    mail.keep(sg.at[rows(a, ROWS)], sgh.at[:, cols(a)])
    mail.keep(dk.at[rows(a, ROWS)], dk_home.at[:, cols(a)])
    term_block(0, 0)
    term_block(0, 1)
    mail.arrive(second)
    relays.append(mail.push(fgall.at[far, :, far_rows], fgall.at[far, :, far_rows], at_ctx(z, mate)))
    for k in relays[:2]:
        mail.arrive(k)
    ring.append(weight_first(2, far))
    mail.arrive(relays[2])
    ring.append(weight_first(3, far_mate))

    def term_sum(n):
        for k in seconds[n]:
            mail.arrive(k)
        return tsend[0, n].astype(F32) + xr2[0, n].astype(F32) + xr2[1, n].astype(F32)

    ysend[...] = term_sum(0).astype(BF)
    across = mail.push(ysend, yr, {"row": 1 - row})
    ring[2] = weight_second(2, ring[2])
    ring[3] = weight_second(3, ring[3])

    for k in small_in:
        mail.arrive(k)
    total[...] = (small_sum(small, slots)).astype(BF)
    for d in range(1, HEADS):
        mail.push(total, small_home.at[:, cols(a)], at_ctx(z, turn(a, d, HEADS)))
    mail.keep(total, small_home.at[:, cols(a)])

    weight_third(0, a, ring[0])
    weight_third(1, mate, ring[1])
    for k in home_sg:
        mail.arrive(k)
    mail.settle()
    mail.arrive(across)
    grad_input[...] = (sgh[...].astype(F32) + term_sum(1) + yr[...].astype(F32)).astype(BF)
    weight_third(2, far, ring[2])
    weight_third(3, far_mate, ring[3])
    mail.finish()


def small_sum(small, slots):
    return small[...].astype(F32) + sum(slots[d].astype(F32) for d in range(SLABS - 1))


def finale(fg, sg, dk, short_part, mg, pr, parts, weights):
    lines = MRLEN + short_part.shape[0]
    any_space, vmem = pl.BlockSpec(memory_space=pl.ANY), pl.BlockSpec(memory_space=pltpu.VMEM)
    remotes = 1 + 3 + 3 + 6 + 6 + 16 + 8 + 1
    return pl.pallas_call(
        finale_kernel,
        out_shape=[
            shape(ROWS, WIDTH),
            shape(3, ROWS, WIDTH, kind=F32),
            shape(ROWS, WIDTH),
            shape(lines, WIDTH),
        ],
        in_specs=[any_space] * 3 + [vmem] * 3 + [any_space] * 5,
        out_specs=[vmem, vmem, any_space, any_space],
        scratch_shapes=[
            pltpu.VMEM(weights.shape, BF),
            pltpu.VMEM((SLAB, SLABS * ROWS), BF),
            pltpu.VMEM((SLABS * ROWS, SLAB), BF),
            pltpu.VMEM((HEADS, 3, SLAB, DH), BF),
            pltpu.VMEM((3, ROWS, WIDTH), BF),
            pltpu.VMEM((HEADS, SLABS, 3, ROWS, DH), BF),
            pltpu.VMEM((HEADS, 2, 3, ROWS // 2, DH), BF),
            pltpu.VMEM((HEADS, 2, 3, ROWS, DH), BF),
            pltpu.VMEM((4, 2, ROWS, WIDTH), BF),
            pltpu.VMEM((2, 2, ROWS // 2, WIDTH), BF),
            pltpu.VMEM((2, 2, ROWS, WIDTH), BF),
            pltpu.VMEM((ROWS, WIDTH), BF),
            pltpu.VMEM((ROWS, WIDTH), BF),
            pltpu.VMEM((ROWS, WIDTH), BF),
            pltpu.VMEM((SLABS - 1, lines, DH), BF),
            pltpu.VMEM((lines, DH), BF),
            pltpu.VMEM((lines, DH), BF),
            pltpu.VMEM((TILE, SLAB + TAIL + MRLEN - TILE, DH), F32),
            pltpu.VMEM((TAPS, TILE, DH), F32),
            pltpu.SemaphoreType.DMA((remotes,)),
            pltpu.SemaphoreType.DMA((remotes,)),
            pltpu.SemaphoreType.DMA((11,)),
        ],
        compiler_params=pltpu.CompilerParams(
            collective_id=5, has_side_effects=True, vmem_limit_bytes=56 << 20
        ),
    )(fg, sg, dk, short_part, mg, pr, *parts, weights)


def deliver_kernel(block, grad_q, grad_k, grad_in, grad_feat, small, block_o, in_o, feat_o, short_o, mr_o, q_o, k_o):
    feat_o[...] = grad_feat[...]
    block_o[...] = block[...]
    in_o[...] = grad_in[...]
    q_o[...] = grad_q[...]
    k_o[...] = grad_k[...]

    @pl.when(pl.program_id(0) == 0)
    def _():
        mr_o[...] = small[pl.ds(0, MRLEN)].astype(F32)
        for j in range(3):
            short_o[j] = small[pl.ds(MRLEN + 16 * j, 16)].astype(F32)[:SHORT]


def deliver(*ins):
    steps = 4

    def fixed(*dims):
        return pl.BlockSpec(dims, lambda n: (0,) * len(dims))

    mine = pl.BlockSpec((ROWS // steps, WIDTH), lambda n: (n, 0))
    feat = pl.BlockSpec((3, ROWS // steps, WIDTH), lambda n: (0, n, 0))
    out = shape(ROWS, WIDTH)
    return pl.pallas_call(
        deliver_kernel,
        grid=(steps,),
        out_shape=[
            out,
            out,
            shape(3, ROWS, WIDTH, kind=F32),
            shape(3, SHORT, WIDTH, kind=F32),
            shape(MRLEN, WIDTH, kind=F32),
            out,
            out,
        ],
        in_specs=[mine] * 4 + [feat, fixed(*ins[-1].shape)],
        out_specs=[mine, mine, feat, fixed(3, SHORT, WIDTH), fixed(MRLEN, WIDTH), mine, mine],
        compiler_params=pltpu.CompilerParams(vmem_limit_bytes=60 << 20),
    )(*ins)


def local(tokens, w_feat, short_filter, mr_filter, queries, key_rows, cotangent):
    weights = w_feat.transpose(1, 0, 2)
    short_taps = short_filter.transpose(1, 0, 2)
    block, grad_queries, *token_parts, sg, fg, dk, short_part, mg, pr = opening(
        tokens, queries, key_rows, cotangent, weights, short_taps, mr_filter
    )
    grad_input, grad_feat, grad_keys, small = finale(fg, sg, dk, short_part, mg, pr, token_parts, weights)
    block_out, grad_input, grad_feat, grad_short, grad_mr, grad_queries, grad_keys = deliver(
        block, grad_queries, grad_keys, grad_input, grad_feat, small
    )
    grad_feat, grad_short = grad_feat.transpose(1, 0, 2), grad_short.transpose(1, 0, 2)
    return (block_out, grad_input, grad_feat, grad_short, grad_mr, grad_queries, grad_keys)


def solution(mesh):
    placed = (
        P("ctx", ("row", "col")),
        P(None, None, ("row", "col")),
        P(None, None, ("row", "col")),
        P(None, ("row", "col")),
        P("ctx", ("row", "col")),
        P("ctx", ("row", "col")),
        P("ctx", ("row", "col")),
    )
    return jax.shard_map(
        local,
        mesh=mesh,
        in_specs=placed,
        out_specs=(
            P("ctx", ("row", "col")),
            P("ctx", ("row", "col")),
            P("ctx", None, ("row", "col")),
            P(None, None, ("row", "col")),
            P(None, ("row", "col")),
            P("ctx", ("row", "col")),
            P("ctx", ("row", "col")),
        ),
        check_vma=False,
    )
```
